32 devices in a mesh: aux: 8 (over y, x, core), mu: 4 (over z).
Axes of the slice: x: 2, y: 2, z: 4, core: 2. Of those that a mesh axis runs over, the one named last changes fastest.
Arguments:
- three_center: float32 [4, 3, 512, 4096], P('mu', None, 'aux'), may hold values from -0.4375 to 0.4375
- nu_slots: int32 [4, 3, 8], P('mu', None, 'aux'), may hold values from 0 to 3
- nu_count: int32 [4, 8], P('mu', 'aux'), may hold values from 1 to 3, 16 in all within a row
- density: float32 [256, 64], P('mu'), may hold values from -6 to 6
- metric_tensor: float32 [4, 3, 512, 1024], P('mu', None, 'aux'), may hold values from -0.046875 to 0.046875
- sig_slots: int32 [4, 3, 8], P('mu', None, 'aux'), may hold values from 0 to 3
- sig_count: int32 [4, 8], P('mu', 'aux'), may hold values from 1 to 3, 16 in all within a row
Outputs:
- exchange_k: float32 [256, 256], P('aux', 'mu')
The draws below stay inside these ranges and needn't reach their ends.
Inputs may be any that keep to these rules, and one draw needn't show every extreme that they name: `nu_slots`: an orbital block index. `nu_count`: slots at or past the count are ignored; each row sums to 8 * (3 + 1) // 2. `sig_slots`: an orbital block index; slots may repeat. `sig_count`: slots at or past the count are ignored; each row sums to 8 * (3 + 1) // 2.
All inputs are finite; a program needn't handle non-finite values. No bound on the sum of `nu_count` or of `sig_count` on one device may be relied on, other than what follows from the above.
Results may differ from the reference program's by a relative error of at most 0.0029.
Values may be sent and summed in bfloat16 or wider, within the bound.
No kernel may reach another device: no remote copies, remote signals or barrier semaphores. Data moves between devices by JAX's collectives and lax.ppermute only.
A program may use at most 64 MiB of HBM per device.

```python
import math
import jax
import jax.numpy as jnp
import numpy as np
from jax import lax

B = 64
AUX_DEV = 64
KNU = 3
KS = 3
LAM_DEV = 16
NO = 256
NL = 64
NAUX = 512
N_AUX = 8
N_MU = 4


def set_ends(drawn, key, low, largest):
    place = [jax.random.randint(jax.random.fold_in(key, axis), (), 0, length) for axis, length in enumerate(drawn.shape)]
    longest = drawn.shape.index(max(drawn.shape))
    neighbour = place[:longest] + [(place[longest] + 1) % drawn.shape[longest]] + place[longest + 1:]
    return drawn.at[tuple(place)].set(low).at[tuple(neighbour)].set(largest)


def levels(rng, extent, shards, smallest, top_value):
    level, own = 1.0, jax.random.fold_in(rng, 6)
    for axis_at, parts in shards:
        steps = jnp.exp(jax.random.uniform(jax.random.fold_in(own, axis_at), (parts,), jnp.float32, smallest / len(shards), top_value / len(shards)))
        level = level * jnp.repeat(steps, extent[axis_at] // parts).reshape([-1 if axis == axis_at else 1 for axis in range(len(extent))])
    return level


def split_up(number_of, total, reach, skew):
    weights = [(1 << 20) // math.isqrt(grade ** skew) + 1 for grade in range(2, number_of + 1)]
    rest, given = total - reach - (number_of - 1), [1] * (number_of - 1)
    while rest > 0:
        candidates = [i for i in range(number_of - 1) if given[i] < reach]
        mass, remaining = sum([weights[i] for i in candidates]), rest
        for i in candidates:
            more = min(reach - given[i], max(1, remaining * weights[i] // mass), rest)
            given[i] = given[i] + more
            rest = rest - more
    return np.array([reach] + given)


def ragged_sizes(own_key, count, total, bound, skew):
    if count == 2:
        one = jax.random.randint(own_key, (), max(1, total - bound), min(bound, total - 1) + 1)
        return jnp.stack([one, total - one])
    lengths = jnp.asarray(split_up(count, total, bound, skew), jnp.int32)
    twos = (count - 1) // 2
    donor, receiver = lengths[1:1 + 2 * twos:2], lengths[2:2 + 2 * twos:2]
    room = jnp.minimum(donor - 1, bound - receiver)
    moved = jax.random.randint(jax.random.fold_in(own_key, 1), (twos,), 0, 1 << 20) % (room + 1)
    lengths = lengths.at[1:1 + 2 * twos:2].set(donor - moved).at[2:2 + 2 * twos:2].set(receiver + moved)
    return lengths[jax.random.permutation(jax.random.fold_in(own_key, 2), count)]


def bell_draw(stream_key, shape, deviation, most, split=(), dtype=jnp.bfloat16):
    drawn = deviation * jax.random.normal(stream_key, shape, jnp.float32)
    if split:
        drawn = drawn * levels(stream_key, shape, split, -0.22, 0.18)
    return jnp.clip(drawn, -most, most).astype(dtype)


def setup_inputs(seed: int = 0) -> dict:
    key_of = jax.random.split(jax.random.key(seed), 8)
    three_center = bell_draw(key_of[0], (N_MU, KNU, NAUX, B * B), (KNU * B) ** -0.5, 0.4375, ((0, 4), (2, 8)), jnp.float32)
    nu_slots = set_ends(jax.random.randint(key_of[1], (N_MU, KNU, N_AUX), 0, N_MU), jax.random.fold_in(key_of[1], 1), 0, N_MU - 1).astype(jnp.int32)
    nu_count = jax.vmap(lambda own: ragged_sizes(own, N_AUX, N_AUX * (KNU + 1) // 2, KNU, 1))(jax.random.split(key_of[2], N_MU)).reshape((N_MU, N_AUX)).astype(jnp.int32)
    density = bell_draw(key_of[3], (NO, NL), 1.0, 6.0, ((0, 4),), jnp.float32)
    metric_tensor = bell_draw(key_of[4], (N_MU, KS, NAUX, LAM_DEV * B), (N_AUX * (KS + 1) // 2 * AUX_DEV * LAM_DEV) ** -0.5, 0.046875, ((0, 4), (2, 8)), jnp.float32)
    sig_slots = set_ends(jax.random.randint(key_of[5], (N_MU, KS, N_AUX), 0, N_MU), jax.random.fold_in(key_of[5], 1), 0, N_MU - 1).astype(jnp.int32)
    sig_count = jax.vmap(lambda own: ragged_sizes(own, N_AUX, N_AUX * (KS + 1) // 2, KS, 1))(jax.random.split(key_of[6], N_MU)).reshape((N_MU, N_AUX)).astype(jnp.int32)
    return {"three_center": three_center, "nu_slots": nu_slots, "nu_count": nu_count, "density": density, "metric_tensor": metric_tensor, "sig_slots": sig_slots, "sig_count": sig_count}


def reference(three_center, nu_slots, nu_count, density, metric_tensor, sig_slots, sig_count):
    highest = lax.Precision.HIGHEST
    dens_blocks = density.reshape(N_MU, B, NL)
    slot_ids = jnp.arange(KNU)
    sig_ids = jnp.arange(KS)
    block_ids = jnp.arange(N_MU)

    def per_aux(running, aux_block):
        aux_block = aux_block.astype(jnp.int32)
        tensor_aux = lax.dynamic_slice_in_dim(three_center, aux_block * AUX_DEV, AUX_DEV, 2).reshape(N_MU, KNU, AUX_DEV, B, B)
        nu_picks = lax.dynamic_index_in_dim(nu_slots, aux_block, 2, keepdims=False)
        live_counts = lax.dynamic_index_in_dim(nu_count, aux_block, 1, keepdims=False)
        live_mask = (slot_ids[None, :] < live_counts[:, None]).astype(jnp.float32)
        chosen = jnp.take(dens_blocks, nu_picks, axis=0) * live_mask[:, :, None, None]
        contracted = jnp.einsum('bkpij,bkjl->pbil', tensor_aux, chosen, precision=highest)
        rounded = lax.optimization_barrier(contracted.reshape(AUX_DEV, NO, NL).astype(jnp.bfloat16)).astype(jnp.float32)
        grouped = rounded.reshape(AUX_DEV, NO, N_MU, LAM_DEV)
        weights = lax.dynamic_slice_in_dim(metric_tensor, aux_block * AUX_DEV, AUX_DEV, 2).reshape(N_MU, KS, AUX_DEV, LAM_DEV, B)
        pieces = jnp.einsum('pmgr,gqprc->gqmc', grouped, weights, precision=highest)
        sig_pick = lax.dynamic_index_in_dim(sig_slots, aux_block, 2, keepdims=False)
        sig_counts = lax.dynamic_index_in_dim(sig_count, aux_block, 1, keepdims=False)
        sig_live = (sig_ids[None, :] < sig_counts[:, None]).astype(jnp.float32)
        placing = (sig_pick[:, :, None] == block_ids[None, None, :]).astype(jnp.float32) * sig_live[:, :, None]
        addition = jnp.einsum('gqs,gqmc->msc', placing, pieces, precision=highest).reshape(NO, NO)
        return running + addition, None

    running, _ = lax.scan(per_aux, jnp.zeros((NO, NO), jnp.float32), jnp.arange(N_AUX).astype(jnp.int32))
    return running
```

```python
import functools

import jax
import jax.numpy as jnp
from jax import lax
from jax.experimental import pallas as pl
from jax.experimental.pallas import tpu as pltpu
from jax.sharding import PartitionSpec as P

F32 = jnp.float32
BF16 = jnp.bfloat16
VMEM = pl.BlockSpec(memory_space=pltpu.VMEM)
SMEM = pl.BlockSpec(memory_space=pltpu.SMEM)


def params(mib):
    return pltpu.CompilerParams(vmem_limit_bytes=mib * 1024 * 1024)


def split(x):
    hi = x.astype(BF16)
    return hi, (x - hi.astype(F32)).astype(BF16)


def iota(shape, dim):
    return lax.broadcasted_iota(jnp.int32, shape, dim)


def prepare_kernel(sig_slots, sig_count, tensor, metric, t_hi, t_lo, m_hi, m_lo):
    _, slots, aux_width, width = tensor.shape
    for k in range(slots):
        for chunk in range(width // 256):
            hi, lo = split(tensor[0, k, :, chunk * 256:(chunk + 1) * 256])
            rows = slice(chunk * aux_width, (chunk + 1) * aux_width)
            t_hi[rows, k * 256:(k + 1) * 256] = hi
            t_lo[rows, k * 256:(k + 1) * 256] = lo
    sig = metric.shape[1]
    half = iota((aux_width, 128), 1) >= 64
    pair_of = jnp.where(half, 1, 0)
    targets = [jnp.where(q < sig_count[0, 0], sig_slots[0, q, 0], -1) for q in range(sig)]
    for pair in range(metric.shape[3] // 128):
        sums = [[jnp.zeros((aux_width, 128), F32) for _ in range(2)] for _ in range(2)]
        for q in range(sig):
            block = metric[0, q, :, pair * 128:(pair + 1) * 128]
            turned = pltpu.roll(block, 64, 1)
            both = (jnp.where(half, turned, block), jnp.where(half, block, turned))
            for out_half in range(2):
                here = pair_of + 2 * out_half == targets[q]
                for parity in range(2):
                    sums[parity][out_half] += jnp.where(here, both[parity], 0.0)
        for parity in range(2):
            r = 2 * pair + parity
            at = ((r % 8) * 2 + r // 8) * aux_width
            for out_half in range(2):
                hi, lo = split(sums[parity][out_half])
                columns = slice(out_half * 128, (out_half + 1) * 128)
                m_hi[at:at + aux_width, columns] = hi
                m_lo[at:at + aux_width, columns] = lo


def half_kernel(n_mu, nu_slots, nu_count, *refs):
    dens = refs[:n_mu]
    t_hi, t_lo = refs[n_mu:n_mu + 2]
    outs = refs[n_mu + 2:2 * n_mu + 2]
    d_hi, d_lo, w_hi, w_lo, turned = refs[2 * n_mu + 2:]
    z = lax.axis_index("mu")
    orb, lam_all = dens[0].shape
    lam = lam_all // n_mu
    slots = nu_slots.shape[1]
    row, col = iota((lam_all, 256), 0), iota((lam_all, 256), 1)
    group = lax.rem(((col >> 3) & 3) + z, n_mu)
    wanted = group * lam + (col >> 7) * 8 + (col & 7)
    choose = jnp.where(row == wanted, 1.0, 0.0).astype(BF16)
    for s in range(n_mu):
        hi, lo = split(dens[s][...])
        d_hi[s] = jnp.dot(hi, choose, preferred_element_type=F32)
        d_lo[s] = jnp.dot(lo, choose, preferred_element_type=F32)
    orbital = (iota((orb, 256), 1) >> 5) & 3
    for k in range(slots):
        at = lax.rem(z - nu_slots[0, k, 0] + n_mu, n_mu)
        live = jnp.where(k < nu_count[0, 0], 1.0, 0.0)
        hi, lo = d_hi[at] * live, d_lo[at] * live
        for i in range(4):
            rows = slice(k * 256 + i * orb, k * 256 + (i + 1) * orb)
            w_hi[rows, :] = jnp.where(orbital == i, hi, 0.0).astype(BF16)
            w_lo[rows, :] = jnp.where(orbital == i, lo, 0.0).astype(BF16)
    total = jnp.dot(t_hi[...], w_hi[...], preferred_element_type=F32)
    total += jnp.dot(t_lo[...], w_hi[...], preferred_element_type=F32)
    total += jnp.dot(t_hi[...], w_lo[...], preferred_element_type=F32)
    aux_width = outs[0].shape[1] // lam
    for chunk in range(total.shape[0] // aux_width):
        piece = total[chunk * aux_width:(chunk + 1) * aux_width]
        stacked = jnp.concatenate([piece[:, :128], piece[:, 128:]], axis=0)
        turned[chunk * 128:(chunk + 1) * 128, :] = stacked.T
    for s in range(n_mu):
        for r in range(8):
            outs[s][:, r * 128:(r + 1) * 128] = turned[
                pl.ds(s * 8 + r, orb, stride=32), :
            ].astype(BF16)


def exchange_kernel(n_mu, n_aux, *refs):
    halves = refs[:n_mu]
    m_hi, m_lo = refs[n_mu:n_mu + 2]
    outs = refs[n_mu + 2:n_mu + 2 + n_aux]
    total = refs[-1]
    z, a = lax.axis_index("mu"), lax.axis_index("aux")
    left = jnp.concatenate([h[...] for h in halves], axis=0)
    product = jnp.dot(left, m_hi[...], preferred_element_type=F32)
    product += jnp.dot(left, m_lo[...], preferred_element_type=F32)
    orb = halves[0].shape[0]
    for s in range(n_mu):
        block = lax.rem(z - s + n_mu, n_mu)
        total[pl.ds(pl.multiple_of(block * orb, orb), orb), :] = product[s * orb:(s + 1) * orb]
    rows = outs[0].shape[0]
    for t in range(n_aux):
        outs[t][...] = total[pl.ds(pl.multiple_of((a ^ t) * rows, rows), rows), :]


def row_sum_kernel(n_mu, n_aux, *refs):
    parts, outs = refs[:n_aux], refs[n_aux:]
    z = lax.axis_index("mu")
    total = parts[0][...]
    for t in range(1, n_aux):
        total += parts[t][...]
    width = outs[0].shape[1]
    for s in range(n_mu):
        block = lax.rem(z + s, n_mu)
        picked = total[:, :width]
        for c in range(1, n_mu):
            picked = jnp.where(block == c, total[:, c * width:(c + 1) * width], picked)
        outs[s][...] = picked


def fast(n_mu, n_aux, three_center, nu_slots, nu_count, density, metric_tensor, sig_slots, sig_count):
    orb, lam_all = density.shape
    slots, aux_width = three_center.shape[1:3]
    lam = lam_all // n_mu
    turns = [[(z, (z + s) % n_mu) for z in range(n_mu)] for s in range(n_mu)]
    dens = [density] + [lax.ppermute(density, "mu", turns[s]) for s in range(1, n_mu)]
    chunks = three_center.shape[3] // 256
    t_shape = jax.ShapeDtypeStruct((chunks * aux_width, slots * 256), BF16)
    m_shape = jax.ShapeDtypeStruct((lam * aux_width, n_mu * orb), BF16)
    t_hi, t_lo, m_hi, m_lo = pl.pallas_call(
        prepare_kernel,
        out_shape=(t_shape, t_shape, m_shape, m_shape),
        in_specs=[SMEM, SMEM, VMEM, VMEM],
        out_specs=(VMEM,) * 4,
        compiler_params=params(16),
        cost_estimate=pl.CostEstimate(flops=10_000_000, bytes_accessed=8_000_000, transcendentals=0),
        name="prepare",
    )(sig_slots, sig_count, three_center, metric_tensor)
    half_shape = jax.ShapeDtypeStruct((orb, lam * aux_width), BF16)
    halves = pl.pallas_call(
        functools.partial(half_kernel, n_mu),
        out_shape=(half_shape,) * n_mu,
        in_specs=[SMEM, SMEM] + [VMEM] * (n_mu + 2),
        out_specs=(VMEM,) * n_mu,
        scratch_shapes=[
            pltpu.VMEM((n_mu, orb, 256), F32),
            pltpu.VMEM((n_mu, orb, 256), F32),
            pltpu.VMEM((slots * 256, 256), BF16),
            pltpu.VMEM((slots * 256, 256), BF16),
            pltpu.VMEM((chunks * 128, 128), F32),
        ],
        compiler_params=params(16),
        cost_estimate=pl.CostEstimate(flops=1_200_000_000, bytes_accessed=4_000_000, transcendentals=0),
        name="half",
    )(nu_slots, nu_count, *dens, t_hi, t_lo)
    halves = [halves[0]] + [lax.ppermute(halves[s], "mu", turns[s]) for s in range(1, n_mu)]
    rows = n_mu * orb // n_aux
    part_shape = jax.ShapeDtypeStruct((rows, n_mu * orb), F32)
    parts = pl.pallas_call(
        functools.partial(exchange_kernel, n_mu, n_aux),
        out_shape=(part_shape,) * n_aux,
        in_specs=[VMEM] * (n_mu + 2),
        out_specs=(VMEM,) * n_aux,
        scratch_shapes=[pltpu.VMEM((n_mu * orb, n_mu * orb), F32)],
        compiler_params=params(16),
        cost_estimate=pl.CostEstimate(flops=300_000_000, bytes_accessed=2_000_000, transcendentals=0),
        name="exchange",
    )(*halves, m_hi, m_lo)
    parts = [parts[0]] + [
        lax.ppermute(parts[t], "aux", [(a, a ^ t) for a in range(n_aux)]) for t in range(1, n_aux)
    ]
    share_shape = jax.ShapeDtypeStruct((rows, orb), F32)
    shares = pl.pallas_call(
        functools.partial(row_sum_kernel, n_mu, n_aux),
        out_shape=(share_shape,) * n_mu,
        in_specs=[VMEM] * n_aux,
        out_specs=(VMEM,) * n_mu,
        compiler_params=params(8),
        name="row_sum",
    )(*parts)
    result = shares[0]
    for s in range(1, n_mu):
        result = result + lax.ppermute(shares[s], "mu", turns[s])
    return result


def general(three_center, nu_slots, nu_count, density, metric_tensor, sig_slots, sig_count):
    highest = lax.Precision.HIGHEST
    orb_block = density.shape[0]
    lam_all = density.shape[1]
    aux_width = three_center.shape[2]
    dens_all = lax.all_gather(density, "mu", axis=0, tiled=True)

    def add_slot(k, running):
        nu_pick = nu_slots[0, k, 0]
        dens_rows = lax.dynamic_slice_in_dim(dens_all, nu_pick * orb_block, orb_block, 0)
        slab_piece = lax.dynamic_index_in_dim(three_center[0], k, 0, keepdims=False).reshape(
            aux_width, orb_block, orb_block
        )
        return running + jnp.einsum("pij,jl->lpi", slab_piece, dens_rows, precision=highest)

    halfway = lax.fori_loop(
        0, nu_count[0, 0], add_slot, jnp.zeros((lam_all, aux_width, orb_block), F32)
    )
    relayed = lax.all_to_all(halfway.astype(BF16), "mu", split_axis=0, concat_axis=2, tiled=True)
    widened = relayed.astype(F32)
    lam_rows = relayed.shape[0]
    orbitals = relayed.shape[2]

    def add_target(q, running):
        target = sig_slots[0, q, 0]
        weights = lax.dynamic_index_in_dim(metric_tensor[0], q, 0, keepdims=False).reshape(
            aux_width, lam_rows, orb_block
        )
        contrib = jnp.einsum("rpm,prc->mc", widened, weights, precision=highest)
        current = lax.dynamic_slice_in_dim(running, target * orb_block, orb_block, 1)
        return lax.dynamic_update_slice_in_dim(running, current + contrib, target * orb_block, 1)

    partial_k = lax.fori_loop(
        0, sig_count[0, 0], add_target, jnp.zeros((orbitals, orbitals), F32)
    )
    row_share = lax.psum_scatter(partial_k, "aux", scatter_dimension=0, tiled=True)
    return lax.psum_scatter(row_share, "mu", scatter_dimension=1, tiled=True)


def solution(mesh):
    n_aux, n_mu = mesh.shape["aux"], mesh.shape["mu"]

    def shards(three_center, nu_slots, nu_count, density, metric_tensor, sig_slots, sig_count):
        args = (three_center, nu_slots, nu_count, density, metric_tensor, sig_slots, sig_count)
        orb, lam_all = density.shape
        fits = (
            (n_aux, n_mu, orb, lam_all) == (8, 4, 64, 64)
            and three_center.shape[2:] == (64, orb * orb)
            and metric_tensor.shape[2:] == (64, lam_all // n_mu * orb)
        )
        return fast(n_mu, n_aux, *args) if fits else general(*args)

    placed = (
        P("mu", None, "aux", None),
        P("mu", None, "aux"),
        P("mu", "aux"),
        P("mu", None),
        P("mu", None, "aux", None),
        P("mu", None, "aux"),
        P("mu", "aux"),
    )
    return jax.shard_map(
        shards, mesh=mesh, in_specs=placed, out_specs=P("aux", "mu"), check_vma=False
    )
```

```python
import functools

import jax
import jax.numpy as jnp
from jax import lax
from jax.experimental import pallas as pl
from jax.experimental.pallas import tpu as pltpu
from jax.sharding import PartitionSpec as P

F32 = jnp.float32
BF16 = jnp.bfloat16
VMEM = pl.BlockSpec(memory_space=pltpu.VMEM)
SMEM = pl.BlockSpec(memory_space=pltpu.SMEM)
ANY = pl.BlockSpec(memory_space=pl.ANY)
HBM = pl.BlockSpec(memory_space=pltpu.HBM)


def params(mib):
    return pltpu.CompilerParams(vmem_limit_bytes=mib * 1024 * 1024)


def split(x):
    hi = x.astype(BF16)
    return hi, (x - hi.astype(F32)).astype(BF16)


def iota(shape, dim):
    return lax.broadcasted_iota(jnp.int32, shape, dim)


def tensor_kernel(tensor, t_hi, t_lo, buffer, arrived):
    _, slots, aux_width, width = tensor.shape
    parts = buffer.shape[0] // slots
    span = width // parts

    def fetch(k, part):
        return pltpu.make_async_copy(
            tensor.at[0, k, :, pl.ds(part * span, span)],
            buffer.at[k * parts + part],
            arrived.at[k * parts + part],
        )

    order = [(k, part) for k in range(slots) for part in range(parts)]
    for k, part in order:
        fetch(k, part).start()
    for k, part in order:
        fetch(k, part).wait()
        for chunk in range(span // 256):
            hi, lo = split(buffer[k * parts + part, :, chunk * 256:(chunk + 1) * 256])
            at = (part * (span // 256) + chunk) * aux_width
            t_hi[at:at + aux_width, k * 256:(k + 1) * 256] = hi
            t_lo[at:at + aux_width, k * 256:(k + 1) * 256] = lo


def metric_kernel(sig_slots, sig_count, after, metric, m_hi, m_lo):
    _, sig, aux_width, width = metric.shape
    half = iota((aux_width, 128), 1) >= 64
    pair_of = jnp.where(half, 1, 0)
    targets = [jnp.where(q < sig_count[0, 0], sig_slots[0, 0, q], -1) for q in range(sig)]
    for pair in range(width // 128):
        sums = [[jnp.zeros((aux_width, 128), F32) for _ in range(2)] for _ in range(2)]
        for q in range(sig):
            block = metric[0, q, :, pair * 128:(pair + 1) * 128]
            turned = pltpu.roll(block, 64, 1)
            both = (jnp.where(half, turned, block), jnp.where(half, block, turned))
            for out_half in range(2):
                here = pair_of + 2 * out_half == targets[q]
                for parity in range(2):
                    sums[parity][out_half] += jnp.where(here, both[parity], 0.0)
        for parity in range(2):
            r = 2 * pair + parity
            at = ((r % 8) * 2 + r // 8) * aux_width
            for out_half in range(2):
                hi, lo = split(sums[parity][out_half])
                columns = slice(out_half * 128, (out_half + 1) * 128)
                m_hi[at:at + aux_width, columns] = hi
                m_lo[at:at + aux_width, columns] = lo


def half_kernel(n_mu, nu_slots, nu_count, *refs):
    dens = refs[:n_mu]
    t_hi, t_lo = refs[n_mu:n_mu + 2]
    outs = refs[n_mu + 2:2 * n_mu + 2]
    d_hi, d_lo, w_hi, w_lo, turned = refs[2 * n_mu + 2:]
    z = lax.axis_index("mu")
    orb, lam_all = dens[0].shape
    lam = lam_all // n_mu
    slots = nu_slots.shape[2]
    row, col = iota((lam_all, 256), 0), iota((lam_all, 256), 1)
    group = lax.rem(((col >> 3) & 3) + z, n_mu)
    wanted = group * lam + (col >> 7) * 8 + (col & 7)
    choose = jnp.where(row == wanted, 1.0, 0.0).astype(BF16)
    for s in range(n_mu):
        hi, lo = split(dens[s][...])
        d_hi[s] = jnp.dot(hi, choose, preferred_element_type=F32)
        d_lo[s] = jnp.dot(lo, choose, preferred_element_type=F32)
    orbital = (iota((orb, 256), 1) >> 5) & 3
    for k in range(slots):
        at = lax.rem(z - nu_slots[0, 0, k] + n_mu, n_mu)
        live = jnp.where(k < nu_count[0, 0], 1.0, 0.0)
        hi, lo = d_hi[at] * live, d_lo[at] * live
        for i in range(4):
            rows = slice(k * 256 + i * orb, k * 256 + (i + 1) * orb)
            w_hi[rows, :] = jnp.where(orbital == i, hi, 0.0).astype(BF16)
            w_lo[rows, :] = jnp.where(orbital == i, lo, 0.0).astype(BF16)
    total = jnp.dot(t_hi[...], w_hi[...], preferred_element_type=F32)
    total += jnp.dot(t_lo[...], w_hi[...], preferred_element_type=F32)
    total += jnp.dot(t_hi[...], w_lo[...], preferred_element_type=F32)
    aux_width = outs[0].shape[1] // lam
    for chunk in range(total.shape[0] // aux_width):
        piece = total[chunk * aux_width:(chunk + 1) * aux_width]
        stacked = jnp.concatenate([piece[:, :128], piece[:, 128:]], axis=0)
        turned[chunk * 128:(chunk + 1) * 128, :] = stacked.T
    for s in range(n_mu):
        for r in range(8):
            outs[s][:, r * 128:(r + 1) * 128] = turned[
                pl.ds(s * 8 + r, orb, stride=32), :
            ].astype(BF16)


def exchange_kernel(n_mu, n_aux, *refs):
    halves = refs[:n_mu]
    m_hi, m_lo, out, total = refs[n_mu:]
    z = lax.axis_index("mu")
    left = jnp.concatenate([h[...] for h in halves], axis=0)
    product = jnp.dot(left, m_hi[...], preferred_element_type=F32)
    product += jnp.dot(left, m_lo[...], preferred_element_type=F32)
    orb = halves[0].shape[0]
    for s in range(n_mu):
        block = lax.rem(z - s + n_mu, n_mu)
        total[pl.ds(pl.multiple_of(block * orb, orb), orb), :] = product[s * orb:(s + 1) * orb]
    rows = out.shape[1]
    lower = iota((rows, 128), 1) < 64
    for a in range(n_aux):
        for pair in range(n_mu // 2):
            columns = slice(pair * 128, (pair + 1) * 128)
            top = total[a * 2 * rows:(a * 2 + 1) * rows, columns]
            bottom = total[(a * 2 + 1) * rows:(a * 2 + 2) * rows, columns]
            at = a * n_mu + pair * 2
            out[at] = jnp.where(lower, top, pltpu.roll(bottom, 64, 1))
            out[at + 1] = jnp.where(lower, pltpu.roll(top, 64, 1), bottom)


def sum_kernel(parts, out):
    total = parts[0]
    for d in range(1, parts.shape[0]):
        total += parts[d]
    rows = parts.shape[1]
    out[:rows, :] = total[:, :64]
    out[rows:, :] = total[:, 64:]


def fast(n_mu, n_aux, three_center, nu_slots, nu_count, density, metric_tensor, sig_slots, sig_count):
    orb, lam_all = density.shape
    slots, aux_width = three_center.shape[1:3]
    lam = lam_all // n_mu
    turns = [[(z, (z + s) % n_mu) for z in range(n_mu)] for s in range(n_mu)]
    dens = [density] + [lax.ppermute(density, "mu", turns[s]) for s in range(1, n_mu)]
    nu_slots, sig_slots = jnp.swapaxes(nu_slots, 1, 2), jnp.swapaxes(sig_slots, 1, 2)
    chunks = three_center.shape[3] // 256
    t_shape = jax.ShapeDtypeStruct((chunks * aux_width, slots * 256), BF16)
    m_shape = jax.ShapeDtypeStruct((lam * aux_width, n_mu * orb), BF16)
    t_hi, t_lo = pl.pallas_call(
        tensor_kernel,
        out_shape=(t_shape, t_shape),
        in_specs=[HBM],
        out_specs=(VMEM, VMEM),
        scratch_shapes=[
            pltpu.VMEM((slots * 4, aux_width, chunks * 64), F32),
            pltpu.SemaphoreType.DMA((slots * 4,)),
        ],
        compiler_params=params(16),
        cost_estimate=pl.CostEstimate(flops=10_000_000, bytes_accessed=6_000_000, transcendentals=0),
        name="tensor",
    )(three_center)
    half_shape = jax.ShapeDtypeStruct((orb, lam * aux_width), BF16)
    halves = pl.pallas_call(
        functools.partial(half_kernel, n_mu),
        out_shape=(half_shape,) * n_mu,
        in_specs=[SMEM, SMEM] + [VMEM] * (n_mu + 2),
        out_specs=(VMEM,) * n_mu,
        scratch_shapes=[
            pltpu.VMEM((n_mu, orb, 256), F32),
            pltpu.VMEM((n_mu, orb, 256), F32),
            pltpu.VMEM((slots * 256, 256), BF16),
            pltpu.VMEM((slots * 256, 256), BF16),
            pltpu.VMEM((chunks * 128, 128), F32),
        ],
        compiler_params=params(16),
        cost_estimate=pl.CostEstimate(flops=1_200_000_000, bytes_accessed=4_000_000, transcendentals=0),
        name="half",
    )(nu_slots, nu_count, *dens, t_hi, t_lo)
    m_hi, m_lo = pl.pallas_call(
        metric_kernel,
        out_shape=(m_shape, m_shape),
        in_specs=[SMEM, SMEM, ANY, VMEM],
        out_specs=(VMEM, VMEM),
        compiler_params=params(16),
        cost_estimate=pl.CostEstimate(flops=10_000_000, bytes_accessed=2_000_000, transcendentals=0),
        name="metric",
    )(sig_slots, sig_count, halves[0], metric_tensor)
    halves = [halves[0]] + [lax.ppermute(halves[s], "mu", turns[s]) for s in range(1, n_mu)]
    rows = n_mu * orb // n_aux
    parts = pl.pallas_call(
        functools.partial(exchange_kernel, n_mu, n_aux),
        out_shape=jax.ShapeDtypeStruct((n_aux * n_mu, rows // 2, 128), F32),
        in_specs=[VMEM] * (n_mu + 2),
        out_specs=VMEM,
        scratch_shapes=[pltpu.VMEM((n_mu * orb, n_mu * orb), F32)],
        compiler_params=params(16),
        cost_estimate=pl.CostEstimate(flops=300_000_000, bytes_accessed=2_000_000, transcendentals=0),
        name="exchange",
    )(*halves, m_hi, m_lo)
    parts = lax.all_to_all(parts, ("aux", "mu"), 0, 0)
    return pl.pallas_call(
        sum_kernel,
        out_shape=jax.ShapeDtypeStruct((rows, orb), F32),
        in_specs=[VMEM],
        out_specs=VMEM,
        compiler_params=params(8),
        name="sum",
    )(parts)


def general(three_center, nu_slots, nu_count, density, metric_tensor, sig_slots, sig_count):
    highest = lax.Precision.HIGHEST
    orb_block = density.shape[0]
    lam_all = density.shape[1]
    aux_width = three_center.shape[2]
    dens_all = lax.all_gather(density, "mu", axis=0, tiled=True)

    def add_slot(k, running):
        nu_pick = nu_slots[0, k, 0]
        dens_rows = lax.dynamic_slice_in_dim(dens_all, nu_pick * orb_block, orb_block, 0)
        slab_piece = lax.dynamic_index_in_dim(three_center[0], k, 0, keepdims=False).reshape(
            aux_width, orb_block, orb_block
        )
        return running + jnp.einsum("pij,jl->lpi", slab_piece, dens_rows, precision=highest)

    halfway = lax.fori_loop(
        0, nu_count[0, 0], add_slot, jnp.zeros((lam_all, aux_width, orb_block), F32)
    )
    relayed = lax.all_to_all(halfway.astype(BF16), "mu", split_axis=0, concat_axis=2, tiled=True)
    widened = relayed.astype(F32)
    lam_rows = relayed.shape[0]
    orbitals = relayed.shape[2]

    def add_target(q, running):
        target = sig_slots[0, q, 0]
        weights = lax.dynamic_index_in_dim(metric_tensor[0], q, 0, keepdims=False).reshape(
            aux_width, lam_rows, orb_block
        )
        contrib = jnp.einsum("rpm,prc->mc", widened, weights, precision=highest)
        current = lax.dynamic_slice_in_dim(running, target * orb_block, orb_block, 1)
        return lax.dynamic_update_slice_in_dim(running, current + contrib, target * orb_block, 1)

    partial_k = lax.fori_loop(
        0, sig_count[0, 0], add_target, jnp.zeros((orbitals, orbitals), F32)
    )
    row_share = lax.psum_scatter(partial_k, "aux", scatter_dimension=0, tiled=True)
    return lax.psum_scatter(row_share, "mu", scatter_dimension=1, tiled=True)


def solution(mesh):
    n_aux, n_mu = mesh.shape["aux"], mesh.shape["mu"]

    def shards(three_center, nu_slots, nu_count, density, metric_tensor, sig_slots, sig_count):
        args = (three_center, nu_slots, nu_count, density, metric_tensor, sig_slots, sig_count)
        orb, lam_all = density.shape
        fits = (
            (n_aux, n_mu, orb, lam_all) == (8, 4, 64, 64)
            and three_center.shape[2:] == (64, orb * orb)
            and metric_tensor.shape[2:] == (64, lam_all // n_mu * orb)
        )
        return fast(n_mu, n_aux, *args) if fits else general(*args)

    placed = (
        P("mu", None, "aux", None),
        P("mu", None, "aux"),
        P("mu", "aux"),
        P("mu", None),
        P("mu", None, "aux", None),
        P("mu", None, "aux"),
        P("mu", "aux"),
    )
    return jax.shard_map(
        shards, mesh=mesh, in_specs=placed, out_specs=P("aux", "mu"), check_vma=False
    )
```

```python
import functools

import jax
import jax.numpy as jnp
from jax import lax
from jax.experimental import pallas as pl
from jax.experimental.pallas import tpu as pltpu
from jax.sharding import PartitionSpec as P

F32 = jnp.float32
BF16 = jnp.bfloat16
VMEM = pl.BlockSpec(memory_space=pltpu.VMEM)
SMEM = pl.BlockSpec(memory_space=pltpu.SMEM)
ANY = pl.BlockSpec(memory_space=pl.ANY)
HBM = pl.BlockSpec(memory_space=pltpu.HBM)


def params(mib):
    return pltpu.CompilerParams(vmem_limit_bytes=mib * 1024 * 1024)


def split(x):
    hi = x.astype(BF16)
    return hi, (x - hi.astype(F32)).astype(BF16)


def iota(shape, dim):
    return lax.broadcasted_iota(jnp.int32, shape, dim)


def tensor_kernel(tensor, t_hi, t_lo, buffer, arrived):
    _, slots, aux_width, width = tensor.shape
    parts = buffer.shape[0] // slots
    span = width // parts

    def fetch(k, part):
        return pltpu.make_async_copy(
            tensor.at[0, k, :, pl.ds(part * span, span)],
            buffer.at[k * parts + part],
            arrived.at[k * parts + part],
        )

    order = [(k, part) for k in range(slots) for part in range(parts)]
    for k, part in order:
        fetch(k, part).start()
    for k, part in order:
        fetch(k, part).wait()
        for chunk in range(span // 256):
            hi, lo = split(buffer[k * parts + part, :, chunk * 256:(chunk + 1) * 256])
            at = (part * (span // 256) + chunk) * aux_width
            t_hi[at:at + aux_width, k * 256:(k + 1) * 256] = hi
            t_lo[at:at + aux_width, k * 256:(k + 1) * 256] = lo


def metric_kernel(sig_slots, sig_count, after, metric, m_hi, m_lo):
    _, sig, aux_width, width = metric.shape
    half = iota((aux_width, 128), 1) >= 64
    pair_of = jnp.where(half, 1, 0)
    targets = [jnp.where(q < sig_count[0, 0], sig_slots[0, 0, q], -1) for q in range(sig)]
    for pair in range(width // 128):
        sums = [[jnp.zeros((aux_width, 128), F32) for _ in range(2)] for _ in range(2)]
        for q in range(sig):
            block = metric[0, q, :, pair * 128:(pair + 1) * 128]
            turned = pltpu.roll(block, 64, 1)
            both = (jnp.where(half, turned, block), jnp.where(half, block, turned))
            for out_half in range(2):
                here = pair_of + 2 * out_half == targets[q]
                for parity in range(2):
                    sums[parity][out_half] += jnp.where(here, both[parity], 0.0)
        for parity in range(2):
            r = 2 * pair + parity
            at = ((r % 8) * 2 + r // 8) * aux_width
            for out_half in range(2):
                hi, lo = split(sums[parity][out_half])
                columns = slice(out_half * 128, (out_half + 1) * 128)
                m_hi[at:at + aux_width, columns] = hi
                m_lo[at:at + aux_width, columns] = lo


def half_kernel(n_mu, nu_slots, nu_count, *refs):
    dens = refs[:n_mu]
    t_hi, t_lo = refs[n_mu:n_mu + 2]
    outs = refs[n_mu + 2:2 * n_mu + 2]
    d_hi, d_lo, w_hi, w_lo, turned = refs[2 * n_mu + 2:]
    z = lax.axis_index("mu")
    orb, lam_all = dens[0].shape
    lam = lam_all // n_mu
    slots = nu_slots.shape[2]
    row, col = iota((lam_all, 256), 0), iota((lam_all, 256), 1)
    group = lax.rem(((col >> 3) & 3) + z, n_mu)
    wanted = group * lam + (col >> 7) * 8 + (col & 7)
    choose = jnp.where(row == wanted, 1.0, 0.0).astype(BF16)
    for s in range(n_mu):
        hi, lo = split(dens[s][...])
        d_hi[s] = jnp.dot(hi, choose, preferred_element_type=F32)
        d_lo[s] = jnp.dot(lo, choose, preferred_element_type=F32)
    orbital = (iota((orb, 256), 1) >> 5) & 3
    for k in range(slots):
        at = lax.rem(z - nu_slots[0, 0, k] + n_mu, n_mu)
        live = jnp.where(k < nu_count[0, 0], 1.0, 0.0)
        hi, lo = d_hi[at] * live, d_lo[at] * live
        for i in range(4):
            rows = slice(k * 256 + i * orb, k * 256 + (i + 1) * orb)
            w_hi[rows, :] = jnp.where(orbital == i, hi, 0.0).astype(BF16)
            w_lo[rows, :] = jnp.where(orbital == i, lo, 0.0).astype(BF16)
    aux_width = outs[0].shape[1] // lam
    per_group = 256 // aux_width
    span = per_group * 4
    for group in range(t_hi.shape[0] // 256):
        rows = slice(group * 256, (group + 1) * 256)
        total = jnp.dot(t_hi[rows, :], w_hi[...], preferred_element_type=F32)
        total += jnp.dot(t_lo[rows, :], w_hi[...], preferred_element_type=F32)
        total += jnp.dot(t_hi[rows, :], w_lo[...], preferred_element_type=F32)
        for chunk in range(per_group):
            piece = total[chunk * aux_width:(chunk + 1) * aux_width]
            stacked = jnp.concatenate([piece[:, :128], piece[:, 128:]], axis=0)
            at = (group * per_group + chunk) * 128
            turned[at:at + 128, :] = stacked.T
        for s in range(n_mu):
            for r in range(8):
                picked = turned[pl.ds(group * per_group * 128 + s * 8 + r, span, stride=32), :]
                outs[s][group * span:(group + 1) * span, r * 128:(r + 1) * 128] = picked.astype(BF16)


def exchange_kernel(n_mu, n_aux, *refs):
    halves = refs[:n_mu]
    m_hi, m_lo, out, total = refs[n_mu:]
    z = lax.axis_index("mu")
    left = jnp.concatenate([h[...] for h in halves], axis=0)
    product = jnp.dot(left, m_hi[...], preferred_element_type=F32)
    product += jnp.dot(left, m_lo[...], preferred_element_type=F32)
    orb = halves[0].shape[0]
    for s in range(n_mu):
        block = lax.rem(z - s + n_mu, n_mu)
        total[pl.ds(pl.multiple_of(block * orb, orb), orb), :] = product[s * orb:(s + 1) * orb]
    rows = out.shape[1]
    lower = iota((rows, 128), 1) < 64
    for a in range(n_aux):
        for pair in range(n_mu // 2):
            columns = slice(pair * 128, (pair + 1) * 128)
            top = total[a * 2 * rows:(a * 2 + 1) * rows, columns]
            bottom = total[(a * 2 + 1) * rows:(a * 2 + 2) * rows, columns]
            at = a * n_mu + pair * 2
            out[at] = jnp.where(lower, top, pltpu.roll(bottom, 64, 1)).astype(BF16)
            out[at + 1] = jnp.where(lower, pltpu.roll(top, 64, 1), bottom).astype(BF16)


def sum_kernel(parts, out):
    total = parts[0].astype(F32)
    for d in range(1, parts.shape[0]):
        total += parts[d].astype(F32)
    rows = parts.shape[1]
    out[:rows, :] = total[:, :64]
    out[rows:, :] = total[:, 64:]


def fast(n_mu, n_aux, three_center, nu_slots, nu_count, density, metric_tensor, sig_slots, sig_count):
    orb, lam_all = density.shape
    slots, aux_width = three_center.shape[1:3]
    lam = lam_all // n_mu
    turns = [[(z, (z + s) % n_mu) for z in range(n_mu)] for s in range(n_mu)]
    dens = [density] + [lax.ppermute(density, "mu", turns[s]) for s in range(1, n_mu)]
    nu_slots, sig_slots = jnp.swapaxes(nu_slots, 1, 2), jnp.swapaxes(sig_slots, 1, 2)
    chunks = three_center.shape[3] // 256
    t_shape = jax.ShapeDtypeStruct((chunks * aux_width, slots * 256), BF16)
    m_shape = jax.ShapeDtypeStruct((lam * aux_width, n_mu * orb), BF16)
    t_hi, t_lo = pl.pallas_call(
        tensor_kernel,
        out_shape=(t_shape, t_shape),
        in_specs=[HBM],
        out_specs=(VMEM, VMEM),
        scratch_shapes=[
            pltpu.VMEM((slots * 4, aux_width, chunks * 64), F32),
            pltpu.SemaphoreType.DMA((slots * 4,)),
        ],
        compiler_params=params(50),
        cost_estimate=pl.CostEstimate(flops=10_000_000, bytes_accessed=6_000_000, transcendentals=0),
        name="tensor",
    )(three_center)
    half_shape = jax.ShapeDtypeStruct((orb, lam * aux_width), BF16)
    halves = pl.pallas_call(
        functools.partial(half_kernel, n_mu),
        out_shape=(half_shape,) * n_mu,
        in_specs=[SMEM, SMEM] + [VMEM] * (n_mu + 2),
        out_specs=(VMEM,) * n_mu,
        scratch_shapes=[
            pltpu.VMEM((n_mu, orb, 256), F32),
            pltpu.VMEM((n_mu, orb, 256), F32),
            pltpu.VMEM((slots * 256, 256), BF16),
            pltpu.VMEM((slots * 256, 256), BF16),
            pltpu.VMEM((chunks * 128, 128), F32),
        ],
        compiler_params=params(16),
        cost_estimate=pl.CostEstimate(flops=1_200_000_000, bytes_accessed=4_000_000, transcendentals=0),
        name="half",
    )(nu_slots, nu_count, *dens, t_hi, t_lo)
    m_hi, m_lo = pl.pallas_call(
        metric_kernel,
        out_shape=(m_shape, m_shape),
        in_specs=[SMEM, SMEM, ANY, VMEM],
        out_specs=(VMEM, VMEM),
        compiler_params=params(16),
        cost_estimate=pl.CostEstimate(flops=10_000_000, bytes_accessed=2_000_000, transcendentals=0),
        name="metric",
    )(sig_slots, sig_count, halves[0], metric_tensor)
    halves = [halves[0]] + [lax.ppermute(halves[s], "mu", turns[s]) for s in range(1, n_mu)]
    rows = n_mu * orb // n_aux
    parts = pl.pallas_call(
        functools.partial(exchange_kernel, n_mu, n_aux),
        out_shape=jax.ShapeDtypeStruct((n_aux * n_mu, rows // 2, 128), BF16),
        in_specs=[VMEM] * (n_mu + 2),
        out_specs=VMEM,
        scratch_shapes=[pltpu.VMEM((n_mu * orb, n_mu * orb), F32)],
        compiler_params=params(16),
        cost_estimate=pl.CostEstimate(flops=300_000_000, bytes_accessed=2_000_000, transcendentals=0),
        name="exchange",
    )(*halves, m_hi, m_lo)
    parts = lax.all_to_all(parts, ("aux", "mu"), 0, 0)
    return pl.pallas_call(
        sum_kernel,
        out_shape=jax.ShapeDtypeStruct((rows, orb), F32),
        in_specs=[VMEM],
        out_specs=VMEM,
        compiler_params=params(8),
        name="sum",
    )(parts)


def general(three_center, nu_slots, nu_count, density, metric_tensor, sig_slots, sig_count):
    highest = lax.Precision.HIGHEST
    orb_block = density.shape[0]
    lam_all = density.shape[1]
    aux_width = three_center.shape[2]
    dens_all = lax.all_gather(density, "mu", axis=0, tiled=True)

    def add_slot(k, running):
        nu_pick = nu_slots[0, k, 0]
        dens_rows = lax.dynamic_slice_in_dim(dens_all, nu_pick * orb_block, orb_block, 0)
        slab_piece = lax.dynamic_index_in_dim(three_center[0], k, 0, keepdims=False).reshape(
            aux_width, orb_block, orb_block
        )
        return running + jnp.einsum("pij,jl->lpi", slab_piece, dens_rows, precision=highest)

    halfway = lax.fori_loop(
        0, nu_count[0, 0], add_slot, jnp.zeros((lam_all, aux_width, orb_block), F32)
    )
    relayed = lax.all_to_all(halfway.astype(BF16), "mu", split_axis=0, concat_axis=2, tiled=True)
    widened = relayed.astype(F32)
    lam_rows = relayed.shape[0]
    orbitals = relayed.shape[2]

    def add_target(q, running):
        target = sig_slots[0, q, 0]
        weights = lax.dynamic_index_in_dim(metric_tensor[0], q, 0, keepdims=False).reshape(
            aux_width, lam_rows, orb_block
        )
        contrib = jnp.einsum("rpm,prc->mc", widened, weights, precision=highest)
        current = lax.dynamic_slice_in_dim(running, target * orb_block, orb_block, 1)
        return lax.dynamic_update_slice_in_dim(running, current + contrib, target * orb_block, 1)

    partial_k = lax.fori_loop(
        0, sig_count[0, 0], add_target, jnp.zeros((orbitals, orbitals), F32)
    )
    row_share = lax.psum_scatter(partial_k, "aux", scatter_dimension=0, tiled=True)
    return lax.psum_scatter(row_share, "mu", scatter_dimension=1, tiled=True)


def solution(mesh):
    n_aux, n_mu = mesh.shape["aux"], mesh.shape["mu"]

    def shards(three_center, nu_slots, nu_count, density, metric_tensor, sig_slots, sig_count):
        args = (three_center, nu_slots, nu_count, density, metric_tensor, sig_slots, sig_count)
        orb, lam_all = density.shape
        fits = (
            (n_aux, n_mu, orb, lam_all) == (8, 4, 64, 64)
            and three_center.shape[2:] == (64, orb * orb)
            and metric_tensor.shape[2:] == (64, lam_all // n_mu * orb)
        )
        return fast(n_mu, n_aux, *args) if fits else general(*args)

    placed = (
        P("mu", None, "aux", None),
        P("mu", None, "aux"),
        P("mu", "aux"),
        P("mu", None),
        P("mu", None, "aux", None),
        P("mu", None, "aux"),
        P("mu", "aux"),
    )
    return jax.shard_map(
        shards, mesh=mesh, in_specs=placed, out_specs=P("aux", "mu"), check_vma=False
    )
```

```python
import functools

import jax
import jax.numpy as jnp
from jax import lax
from jax.experimental import pallas as pl
from jax.experimental.pallas import tpu as pltpu
from jax.sharding import PartitionSpec as P

F32 = jnp.float32
BF16 = jnp.bfloat16
VMEM = pl.BlockSpec(memory_space=pltpu.VMEM)
SMEM = pl.BlockSpec(memory_space=pltpu.SMEM)
ANY = pl.BlockSpec(memory_space=pl.ANY)
HBM = pl.BlockSpec(memory_space=pltpu.HBM)


def params(mib):
    return pltpu.CompilerParams(vmem_limit_bytes=mib * 1024 * 1024)


def split(x):
    hi = x.astype(BF16)
    return hi, (x - hi.astype(F32)).astype(BF16)


def iota(shape, dim):
    return lax.broadcasted_iota(jnp.int32, shape, dim)


def tensor_kernel(tensor, t_hi, t_lo, buffer, arrived):
    _, slots, aux_width, width = tensor.shape
    parts = buffer.shape[0] // slots
    span = width // parts

    def fetch(k, part):
        return pltpu.make_async_copy(
            tensor.at[0, k, :, pl.ds(part * span, span)],
            buffer.at[k * parts + part],
            arrived.at[k * parts + part],
        )

    order = [(k, part) for k in range(slots) for part in range(parts)]
    for k, part in order:
        fetch(k, part).start()
    for k, part in order:
        fetch(k, part).wait()
        for chunk in range(span // 256):
            hi, lo = split(buffer[k * parts + part, :, chunk * 256:(chunk + 1) * 256])
            at = (part * (span // 256) + chunk) * aux_width
            t_hi[at:at + aux_width, k * 256:(k + 1) * 256] = hi
            t_lo[at:at + aux_width, k * 256:(k + 1) * 256] = lo


def metric_kernel(sig_slots, sig_count, after, metric, m_hi, m_lo):
    _, sig, aux_width, width = metric.shape
    half = iota((aux_width, 128), 1) >= 64
    pair_of = jnp.where(half, 1, 0)
    targets = [jnp.where(q < sig_count[0, 0], sig_slots[0, 0, q], -1) for q in range(sig)]
    for pair in range(width // 128):
        sums = [[jnp.zeros((aux_width, 128), F32) for _ in range(2)] for _ in range(2)]
        for q in range(sig):
            block = metric[0, q, :, pair * 128:(pair + 1) * 128]
            turned = pltpu.roll(block, 64, 1)
            both = (jnp.where(half, turned, block), jnp.where(half, block, turned))
            for out_half in range(2):
                here = pair_of + 2 * out_half == targets[q]
                for parity in range(2):
                    sums[parity][out_half] += jnp.where(here, both[parity], 0.0)
        for parity in range(2):
            r = 2 * pair + parity
            at = ((r % 8) * 2 + r // 8) * aux_width
            for out_half in range(2):
                hi, lo = split(sums[parity][out_half])
                columns = slice(out_half * 128, (out_half + 1) * 128)
                m_hi[at:at + aux_width, columns] = hi
                m_lo[at:at + aux_width, columns] = lo


def half_kernel(n_mu, nu_slots, nu_count, *refs):
    dens = refs[:n_mu]
    t_hi, t_lo = refs[n_mu:n_mu + 2]
    outs = refs[n_mu + 2:2 * n_mu + 2]
    d_hi, d_lo, weights, turned = refs[2 * n_mu + 2:]
    z = lax.axis_index("mu")
    orb, lam_all = dens[0].shape
    lam = lam_all // n_mu
    slots = nu_slots.shape[2]
    row, col = iota((lam_all, 256), 0), iota((lam_all, 256), 1)
    group = ((col >> 3) & 3) ^ z
    wanted = group * lam + (col >> 7) * 8 + (col & 7)
    choose = jnp.where(row == wanted, 1.0, 0.0).astype(BF16)
    for s in range(n_mu):
        hi, lo = split(dens[s][...])
        d_hi[s] = jnp.dot(hi, choose, preferred_element_type=F32)
        d_lo[s] = jnp.dot(lo, choose, preferred_element_type=F32)
    orbital = (iota((orb, 256), 1) >> 5) & 3
    depth = slots * 256
    for k in range(slots):
        at = z ^ nu_slots[0, 0, k]
        live = jnp.where(k < nu_count[0, 0], 1.0, 0.0)
        hi, lo = d_hi[at] * live, d_lo[at] * live
        for i in range(4):
            rows = k * 256 + i * orb
            w_hi = jnp.where(orbital == i, hi, 0.0).astype(BF16)
            weights[rows:rows + orb, :] = w_hi
            weights[rows + depth:rows + depth + orb, :] = w_hi
            weights[rows + 2 * depth:rows + 2 * depth + orb, :] = jnp.where(
                orbital == i, lo, 0.0
            ).astype(BF16)
    aux_width = outs[0].shape[1] // lam
    per_group = 256 // aux_width
    span = per_group * 4
    for group in range(t_hi.shape[0] // 256):
        rows = slice(group * 256, (group + 1) * 256)
        high = t_hi[rows, :]
        left = jnp.concatenate([high, t_lo[rows, :], high], axis=1)
        total = jnp.dot(left, weights[...], preferred_element_type=F32)
        for chunk in range(per_group):
            piece = total[chunk * aux_width:(chunk + 1) * aux_width]
            stacked = jnp.concatenate([piece[:, :128], piece[:, 128:]], axis=0)
            at = (group * per_group + chunk) * 128
            turned[at:at + 128, :] = stacked.T
        for s in range(n_mu):
            for r in range(8):
                picked = turned[pl.ds(group * per_group * 128 + s * 8 + r, span, stride=32), :]
                outs[s][group * span:(group + 1) * span, r * 128:(r + 1) * 128] = picked.astype(BF16)


def exchange_kernel(n_mu, n_aux, *refs):
    halves = refs[:n_mu]
    m_hi, m_lo, out, total = refs[n_mu:]
    z = lax.axis_index("mu")
    left = jnp.concatenate([h[...] for h in halves], axis=0)
    product = jnp.dot(left, m_hi[...], preferred_element_type=F32)
    product += jnp.dot(left, m_lo[...], preferred_element_type=F32)
    orb = halves[0].shape[0]
    for s in range(n_mu):
        block = z ^ s
        total[pl.ds(pl.multiple_of(block * orb, orb), orb), :] = product[s * orb:(s + 1) * orb]
    rows = out.shape[1]
    lower = iota((rows, 128), 1) < 64
    for a in range(n_aux):
        for pair in range(n_mu // 2):
            columns = slice(pair * 128, (pair + 1) * 128)
            top = total[a * 2 * rows:(a * 2 + 1) * rows, columns]
            bottom = total[(a * 2 + 1) * rows:(a * 2 + 2) * rows, columns]
            at = a * n_mu + pair * 2
            out[at] = jnp.where(lower, top, pltpu.roll(bottom, 64, 1)).astype(BF16)
            out[at + 1] = jnp.where(lower, pltpu.roll(top, 64, 1), bottom).astype(BF16)


def sum_kernel(parts, out):
    total = parts[0].astype(F32)
    for d in range(1, parts.shape[0]):
        total += parts[d].astype(F32)
    rows = parts.shape[1]
    out[:rows, :] = total[:, :64]
    out[rows:, :] = total[:, 64:]


def fast(n_mu, n_aux, three_center, nu_slots, nu_count, density, metric_tensor, sig_slots, sig_count):
    orb, lam_all = density.shape
    slots, aux_width = three_center.shape[1:3]
    lam = lam_all // n_mu
    turns = [[(z, z ^ s) for z in range(n_mu)] for s in range(n_mu)]
    dens = [density] * n_mu
    for s in (2, 3, 1):
        dens[s] = lax.ppermute(density, "mu", turns[s])
    nu_slots, sig_slots = jnp.swapaxes(nu_slots, 1, 2), jnp.swapaxes(sig_slots, 1, 2)
    chunks = three_center.shape[3] // 256
    t_shape = jax.ShapeDtypeStruct((chunks * aux_width, slots * 256), BF16)
    m_shape = jax.ShapeDtypeStruct((lam * aux_width, n_mu * orb), BF16)
    t_hi, t_lo = pl.pallas_call(
        tensor_kernel,
        out_shape=(t_shape, t_shape),
        in_specs=[HBM],
        out_specs=(VMEM, VMEM),
        scratch_shapes=[
            pltpu.VMEM((slots * 4, aux_width, chunks * 64), F32),
            pltpu.SemaphoreType.DMA((slots * 4,)),
        ],
        compiler_params=params(50),
        cost_estimate=pl.CostEstimate(flops=10_000_000, bytes_accessed=6_000_000, transcendentals=0),
        name="tensor",
    )(three_center)
    half_shape = jax.ShapeDtypeStruct((orb, lam * aux_width), BF16)
    halves = pl.pallas_call(
        functools.partial(half_kernel, n_mu),
        out_shape=(half_shape,) * n_mu,
        in_specs=[SMEM, SMEM] + [VMEM] * (n_mu + 2),
        out_specs=(VMEM,) * n_mu,
        scratch_shapes=[
            pltpu.VMEM((n_mu, orb, 256), F32),
            pltpu.VMEM((n_mu, orb, 256), F32),
            pltpu.VMEM((3 * slots * 256, 256), BF16),
            pltpu.VMEM((chunks * 128, 128), F32),
        ],
        compiler_params=params(16),
        cost_estimate=pl.CostEstimate(flops=1_200_000_000, bytes_accessed=4_000_000, transcendentals=0),
        name="half",
    )(nu_slots, nu_count, *dens, t_hi, t_lo)
    m_hi, m_lo = pl.pallas_call(
        metric_kernel,
        out_shape=(m_shape, m_shape),
        in_specs=[SMEM, SMEM, ANY, VMEM],
        out_specs=(VMEM, VMEM),
        compiler_params=params(16),
        cost_estimate=pl.CostEstimate(flops=10_000_000, bytes_accessed=2_000_000, transcendentals=0),
        name="metric",
    )(sig_slots, sig_count, halves[0], metric_tensor)
    halves = list(halves)
    for s in (3, 2, 1):
        halves[s] = lax.ppermute(halves[s], "mu", turns[s])
    rows = n_mu * orb // n_aux
    parts = pl.pallas_call(
        functools.partial(exchange_kernel, n_mu, n_aux),
        out_shape=jax.ShapeDtypeStruct((n_aux * n_mu, rows // 2, 128), BF16),
        in_specs=[VMEM] * (n_mu + 2),
        out_specs=VMEM,
        scratch_shapes=[pltpu.VMEM((n_mu * orb, n_mu * orb), F32)],
        compiler_params=params(16),
        cost_estimate=pl.CostEstimate(flops=300_000_000, bytes_accessed=2_000_000, transcendentals=0),
        name="exchange",
    )(*halves, m_hi, m_lo)
    parts = lax.all_to_all(parts, ("aux", "mu"), 0, 0)
    return pl.pallas_call(
        sum_kernel,
        out_shape=jax.ShapeDtypeStruct((rows, orb), F32),
        in_specs=[VMEM],
        out_specs=VMEM,
        compiler_params=params(8),
        name="sum",
    )(parts)


def general(three_center, nu_slots, nu_count, density, metric_tensor, sig_slots, sig_count):
    highest = lax.Precision.HIGHEST
    orb_block = density.shape[0]
    lam_all = density.shape[1]
    aux_width = three_center.shape[2]
    dens_all = lax.all_gather(density, "mu", axis=0, tiled=True)

    def add_slot(k, running):
        nu_pick = nu_slots[0, k, 0]
        dens_rows = lax.dynamic_slice_in_dim(dens_all, nu_pick * orb_block, orb_block, 0)
        slab_piece = lax.dynamic_index_in_dim(three_center[0], k, 0, keepdims=False).reshape(
            aux_width, orb_block, orb_block
        )
        return running + jnp.einsum("pij,jl->lpi", slab_piece, dens_rows, precision=highest)

    halfway = lax.fori_loop(
        0, nu_count[0, 0], add_slot, jnp.zeros((lam_all, aux_width, orb_block), F32)
    )
    relayed = lax.all_to_all(halfway.astype(BF16), "mu", split_axis=0, concat_axis=2, tiled=True)
    widened = relayed.astype(F32)
    lam_rows = relayed.shape[0]
    orbitals = relayed.shape[2]

    def add_target(q, running):
        target = sig_slots[0, q, 0]
        weights = lax.dynamic_index_in_dim(metric_tensor[0], q, 0, keepdims=False).reshape(
            aux_width, lam_rows, orb_block
        )
        contrib = jnp.einsum("rpm,prc->mc", widened, weights, precision=highest)
        current = lax.dynamic_slice_in_dim(running, target * orb_block, orb_block, 1)
        return lax.dynamic_update_slice_in_dim(running, current + contrib, target * orb_block, 1)

    partial_k = lax.fori_loop(
        0, sig_count[0, 0], add_target, jnp.zeros((orbitals, orbitals), F32)
    )
    row_share = lax.psum_scatter(partial_k, "aux", scatter_dimension=0, tiled=True)
    return lax.psum_scatter(row_share, "mu", scatter_dimension=1, tiled=True)


def solution(mesh):
    n_aux, n_mu = mesh.shape["aux"], mesh.shape["mu"]

    def shards(three_center, nu_slots, nu_count, density, metric_tensor, sig_slots, sig_count):
        args = (three_center, nu_slots, nu_count, density, metric_tensor, sig_slots, sig_count)
        orb, lam_all = density.shape
        fits = (
            (n_aux, n_mu, orb, lam_all) == (8, 4, 64, 64)
            and three_center.shape[2:] == (64, orb * orb)
            and metric_tensor.shape[2:] == (64, lam_all // n_mu * orb)
        )
        return fast(n_mu, n_aux, *args) if fits else general(*args)

    placed = (
        P("mu", None, "aux", None),
        P("mu", None, "aux"),
        P("mu", "aux"),
        P("mu", None),
        P("mu", None, "aux", None),
        P("mu", None, "aux"),
        P("mu", "aux"),
    )
    return jax.shard_map(
        shards, mesh=mesh, in_specs=placed, out_specs=P("aux", "mu"), check_vma=False
    )
```

```python
import functools

import jax
import jax.numpy as jnp
from jax import lax
from jax.experimental import pallas as pl
from jax.experimental.pallas import tpu as pltpu
from jax.sharding import PartitionSpec as P

F32 = jnp.float32
BF16 = jnp.bfloat16
VMEM = pl.BlockSpec(memory_space=pltpu.VMEM)
SMEM = pl.BlockSpec(memory_space=pltpu.SMEM)
ANY = pl.BlockSpec(memory_space=pl.ANY)
HBM = pl.BlockSpec(memory_space=pltpu.HBM)


def params(mib):
    return pltpu.CompilerParams(vmem_limit_bytes=mib * 1024 * 1024)


def split(x):
    hi = x.astype(BF16)
    return hi, (x - hi.astype(F32)).astype(BF16)


def iota(shape, dim):
    return lax.broadcasted_iota(jnp.int32, shape, dim)


def tensor_kernel(tensor, t_hi, t_lo, buffer, arrived):
    _, slots, aux_width, width = tensor.shape
    parts = buffer.shape[0] // slots
    span = width // parts

    def fetch(k, part):
        return pltpu.make_async_copy(
            tensor.at[0, k, :, pl.ds(part * span, span)],
            buffer.at[k * parts + part],
            arrived.at[k * parts + part],
        )

    order = [(k, part) for k in range(slots) for part in range(parts)]
    for k, part in order:
        fetch(k, part).start()
    for k, part in order:
        fetch(k, part).wait()
        for chunk in range(span // 256):
            hi, lo = split(buffer[k * parts + part, :, chunk * 256:(chunk + 1) * 256])
            at = (part * (span // 256) + chunk) * aux_width
            t_hi[at:at + aux_width, k * 256:(k + 1) * 256] = hi
            t_lo[at:at + aux_width, k * 256:(k + 1) * 256] = lo


def live_targets(sig_slots, sig_count):
    return [
        jnp.where(q < sig_count[0, 0], sig_slots[0, 0, q], -1).astype(F32)
        for q in range(sig_slots.shape[2])
    ]


def place(targets, metric, m_hi, m_lo):
    _, sig, aux_width, width = metric.shape
    half = iota((aux_width, 128), 1) >= 64
    pair_of = jnp.where(half, 1.0, 0.0)
    for pair in range(width // 128):
        sums = [[jnp.zeros((aux_width, 128), F32) for _ in range(2)] for _ in range(2)]
        for q in range(sig):
            block = metric[0, q, :, pair * 128:(pair + 1) * 128]
            turned = pltpu.roll(block, 64, 1)
            both = (jnp.where(half, turned, block), jnp.where(half, block, turned))
            for out_half in range(2):
                here = pair_of + 2 * out_half == targets[q]
                for parity in range(2):
                    sums[parity][out_half] += jnp.where(here, both[parity], 0.0)
        for parity in range(2):
            r = 2 * pair + parity
            at = ((r % 8) * 2 + r // 8) * aux_width
            for out_half in range(2):
                hi, lo = split(sums[parity][out_half])
                columns = slice(out_half * 128, (out_half + 1) * 128)
                m_hi[at:at + aux_width, columns] = hi
                m_lo[at:at + aux_width, columns] = lo


def product(halves, rows, m_hi, m_lo):
    left = jnp.concatenate([h[:rows, :] for h in halves], axis=0)
    total = jnp.dot(left, m_hi[...], preferred_element_type=F32)
    return total + jnp.dot(left, m_lo[...], preferred_element_type=F32)


def metric_kernel(n_mu, slots, count, received, metric, metric_other, *refs):
    near = refs[:n_mu]
    total, m_hi, m_lo, own_hi, own_lo = refs[n_mu:]
    note = received[received.shape[0] - 16:, :128].astype(F32)
    targets = [note[q:q + 1, :] for q in range(slots.shape[2])]
    place(targets, metric_other, m_hi, m_lo)
    place(live_targets(slots, count), metric, own_hi, own_lo)
    total[...] = product(near, near[0].shape[0], own_hi, own_lo)


def contract(first, weights, t_hi, t_lo, outs, turned):
    span = outs[1].shape[0] // 2
    aux_width = 1024 // span
    for group in range(2):
        rows = pl.ds(pl.multiple_of(first + group * 256, 256), 256)
        high = t_hi[rows, :]
        left = jnp.concatenate([high, t_lo[rows, :], high], axis=1)
        total = jnp.dot(left, weights[...], preferred_element_type=F32)
        for chunk in range(256 // aux_width):
            piece = total[chunk * aux_width:(chunk + 1) * aux_width]
            stacked = jnp.concatenate([piece[:, :128], piece[:, 128:]], axis=0)
            at = group * span * 32 + chunk * 128
            turned[at:at + 128, :] = stacked.T
        for s in range(len(outs)):
            for r in range(8):
                picked = turned[pl.ds(group * span * 32 + s * 8 + r, span, stride=32), :]
                outs[s][group * span:(group + 1) * span, r * 128:(r + 1) * 128] = picked.astype(BF16)


def near_kernel(n_mu, nu_slots, nu_count, after, *refs):
    dens = refs[:n_mu]
    t_hi, t_lo = refs[n_mu:n_mu + 2]
    outs = refs[n_mu + 2:2 * n_mu + 2]
    weights, d_hi, d_lo, turned = refs[2 * n_mu + 2:]
    z = lax.axis_index("mu")
    orb, lam_all = dens[0].shape
    lam = lam_all // n_mu
    slots = nu_slots.shape[2]
    row, col = iota((lam_all, 256), 0), iota((lam_all, 256), 1)
    group = ((col >> 3) & 3) ^ z
    wanted = group * lam + (col >> 7) * 8 + (col & 7)
    choose = jnp.where(row == wanted, 1.0, 0.0).astype(BF16)
    for s in range(n_mu):
        hi, lo = split(dens[s][...])
        d_hi[s] = jnp.dot(hi, choose, preferred_element_type=F32)
        d_lo[s] = jnp.dot(lo, choose, preferred_element_type=F32)
    orbital = (iota((orb, 256), 1) >> 5) & 3
    depth = slots * 256
    for k in range(slots):
        at = z ^ nu_slots[0, 0, k]
        live = jnp.where(k < nu_count[0, 0], 1.0, 0.0)
        hi, lo = d_hi[at] * live, d_lo[at] * live
        for i in range(4):
            rows = k * 256 + i * orb
            w_hi = jnp.where(orbital == i, hi, 0.0).astype(BF16)
            weights[rows:rows + orb, :] = w_hi
            weights[rows + depth:rows + depth + orb, :] = w_hi
            weights[rows + 2 * depth:rows + 2 * depth + orb, :] = jnp.where(
                orbital == i, lo, 0.0
            ).astype(BF16)
    core = lax.axis_index("aux") & 1
    contract(core * 512, weights, t_hi, t_lo, outs, turned)


def far_kernel(sig_slots, sig_count, weights, t_hi, t_lo, *refs):
    outs, turned = refs[:-1], refs[-1]
    core = lax.axis_index("aux") & 1
    contract((1 - core) * 512, weights, t_hi, t_lo, outs, turned)
    shape = (16, outs[0].shape[1])
    note = jnp.full(shape, -1.0, F32)
    for q, target in enumerate(live_targets(sig_slots, sig_count)):
        note = jnp.where(iota(shape, 0) == q, target, note)
    outs[0][outs[0].shape[0] - 16:, :] = note.astype(BF16)


def exchange_kernel(n_mu, n_chip, near_total, *refs):
    far = refs[:n_mu]
    m_hi, m_lo, out, total = refs[n_mu:]
    z = lax.axis_index("mu")
    orb_half = far[1].shape[0]
    whole = near_total[...] + product(far, orb_half, m_hi, m_lo)
    for s in range(n_mu):
        at = pl.multiple_of((z ^ s) * orb_half, orb_half)
        total[pl.ds(at, orb_half), :] = whole[s * orb_half:(s + 1) * orb_half]
    rows = out.shape[1]
    lower = iota((rows, 128), 1) < 64
    for c in range(n_chip):
        for pair in range(n_mu // 2):
            columns = slice(pair * 128, (pair + 1) * 128)
            top = total[c * 2 * rows:(c * 2 + 1) * rows, columns]
            bottom = total[(c * 2 + 1) * rows:(c * 2 + 2) * rows, columns]
            at = c * n_mu + pair * 2
            out[at] = jnp.where(lower, top, pltpu.roll(bottom, 64, 1)).astype(BF16)
            out[at + 1] = jnp.where(lower, pltpu.roll(top, 64, 1), bottom).astype(BF16)


def sum_kernel(parts, out):
    total = parts[0].astype(F32)
    for d in range(1, parts.shape[0]):
        total += parts[d].astype(F32)
    rows = parts.shape[1]
    out[:rows, :] = total[:, :64]
    out[rows:, :] = total[:, 64:]


def fast(n_mu, n_aux, three_center, nu_slots, nu_count, density, metric_tensor, sig_slots, sig_count):
    orb, lam_all = density.shape
    slots, aux_width = three_center.shape[1:3]
    lam = lam_all // n_mu
    both = ("aux", "mu")
    turns = [[(z, z ^ s) for z in range(n_mu)] for s in range(n_mu)]
    cross = [
        [(a * n_mu + z, (a ^ 1) * n_mu + (z ^ s)) for a in range(n_aux) for z in range(n_mu)]
        for s in range(n_mu)
    ]
    nu_slots, sig_slots = jnp.swapaxes(nu_slots, 1, 2), jnp.swapaxes(sig_slots, 1, 2)
    dens = [density] + [lax.ppermute(density, "mu", turns[s]) for s in range(1, n_mu)]
    metric_other = lax.ppermute(metric_tensor, both, cross[0])
    chunks = three_center.shape[3] // 256
    t_shape = jax.ShapeDtypeStruct((chunks * aux_width, slots * 256), BF16)
    t_hi, t_lo = pl.pallas_call(
        tensor_kernel,
        out_shape=(t_shape, t_shape),
        in_specs=[HBM],
        out_specs=(VMEM, VMEM),
        scratch_shapes=[
            pltpu.VMEM((slots * 4, aux_width, chunks * 64), F32),
            pltpu.SemaphoreType.DMA((slots * 4,)),
        ],
        compiler_params=params(50),
        cost_estimate=pl.CostEstimate(flops=10_000_000, bytes_accessed=6_000_000, transcendentals=0),
        name="tensor",
    )(three_center)
    half_shape = jax.ShapeDtypeStruct((orb // 2, lam * aux_width), BF16)
    *near, weights = pl.pallas_call(
        functools.partial(near_kernel, n_mu),
        out_shape=(half_shape,) * n_mu + (jax.ShapeDtypeStruct((3 * slots * 256, 256), BF16),),
        in_specs=[SMEM, SMEM, ANY] + [VMEM] * (n_mu + 2),
        out_specs=(VMEM,) * (n_mu + 1),
        scratch_shapes=[
            pltpu.VMEM((n_mu, orb, 256), F32),
            pltpu.VMEM((n_mu, orb, 256), F32),
            pltpu.VMEM((chunks * 64, 128), F32),
        ],
        compiler_params=params(16),
        cost_estimate=pl.CostEstimate(flops=600_000_000, bytes_accessed=4_000_000, transcendentals=0),
        name="near",
    )(nu_slots, nu_count, metric_other, *dens, t_hi, t_lo)
    note_shape = jax.ShapeDtypeStruct((orb // 2 + 16, lam * aux_width), BF16)
    far = pl.pallas_call(
        far_kernel,
        out_shape=(note_shape,) + (half_shape,) * (n_mu - 1),
        in_specs=[SMEM, SMEM] + [VMEM] * 3,
        out_specs=(VMEM,) * n_mu,
        scratch_shapes=[pltpu.VMEM((chunks * 64, 128), F32)],
        compiler_params=params(16),
        cost_estimate=pl.CostEstimate(flops=600_000_000, bytes_accessed=4_000_000, transcendentals=0),
        name="far",
    )(sig_slots, sig_count, weights, t_hi, t_lo)
    near = [near[0]] + [lax.ppermute(near[s], "mu", turns[s]) for s in range(1, n_mu)]
    far = [lax.ppermute(far[s], both, cross[s]) for s in range(n_mu)]
    m_shape = jax.ShapeDtypeStruct((lam * aux_width, n_mu * orb), BF16)
    near_total, m_hi, m_lo = pl.pallas_call(
        functools.partial(metric_kernel, n_mu),
        out_shape=(jax.ShapeDtypeStruct((n_mu * orb // 2, n_mu * orb), F32), m_shape, m_shape),
        in_specs=[SMEM, SMEM] + [VMEM] * (n_mu + 3),
        out_specs=(VMEM,) * 3,
        scratch_shapes=[pltpu.VMEM(m_shape.shape, BF16)] * 2,
        compiler_params=params(16),
        cost_estimate=pl.CostEstimate(flops=10_000_000, bytes_accessed=4_000_000, transcendentals=0),
        name="metric",
    )(sig_slots, sig_count, far[0], metric_tensor, metric_other, *near)
    rows = n_mu * orb // n_aux
    n_chip = n_aux // 2
    parts = pl.pallas_call(
        functools.partial(exchange_kernel, n_mu, n_chip),
        out_shape=jax.ShapeDtypeStruct((n_chip * n_mu, rows // 2, 128), BF16),
        in_specs=[VMEM] * (n_mu + 3),
        out_specs=VMEM,
        scratch_shapes=[pltpu.VMEM((n_mu * orb // 2, n_mu * orb), F32)],
        compiler_params=params(16),
        cost_estimate=pl.CostEstimate(flops=300_000_000, bytes_accessed=2_000_000, transcendentals=0),
        name="exchange",
    )(near_total, *far, m_hi, m_lo)
    same_core = [
        [(c * 2 + h) * n_mu + z for c in range(n_chip) for z in range(n_mu)] for h in range(2)
    ]
    parts = lax.all_to_all(parts, both, 0, 0, axis_index_groups=same_core)
    return pl.pallas_call(
        sum_kernel,
        out_shape=jax.ShapeDtypeStruct((rows, orb), F32),
        in_specs=[VMEM],
        out_specs=VMEM,
        compiler_params=params(8),
        name="sum",
    )(parts)


def general(three_center, nu_slots, nu_count, density, metric_tensor, sig_slots, sig_count):
    highest = lax.Precision.HIGHEST
    orb_block = density.shape[0]
    lam_all = density.shape[1]
    aux_width = three_center.shape[2]
    dens_all = lax.all_gather(density, "mu", axis=0, tiled=True)

    def add_slot(k, running):
        nu_pick = nu_slots[0, k, 0]
        dens_rows = lax.dynamic_slice_in_dim(dens_all, nu_pick * orb_block, orb_block, 0)
        slab_piece = lax.dynamic_index_in_dim(three_center[0], k, 0, keepdims=False).reshape(
            aux_width, orb_block, orb_block
        )
        return running + jnp.einsum("pij,jl->lpi", slab_piece, dens_rows, precision=highest)

    halfway = lax.fori_loop(
        0, nu_count[0, 0], add_slot, jnp.zeros((lam_all, aux_width, orb_block), F32)
    )
    relayed = lax.all_to_all(halfway.astype(BF16), "mu", split_axis=0, concat_axis=2, tiled=True)
    widened = relayed.astype(F32)
    lam_rows = relayed.shape[0]
    orbitals = relayed.shape[2]

    def add_target(q, running):
        target = sig_slots[0, q, 0]
        weights = lax.dynamic_index_in_dim(metric_tensor[0], q, 0, keepdims=False).reshape(
            aux_width, lam_rows, orb_block
        )
        contrib = jnp.einsum("rpm,prc->mc", widened, weights, precision=highest)
        current = lax.dynamic_slice_in_dim(running, target * orb_block, orb_block, 1)
        return lax.dynamic_update_slice_in_dim(running, current + contrib, target * orb_block, 1)

    partial_k = lax.fori_loop(
        0, sig_count[0, 0], add_target, jnp.zeros((orbitals, orbitals), F32)
    )
    row_share = lax.psum_scatter(partial_k, "aux", scatter_dimension=0, tiled=True)
    return lax.psum_scatter(row_share, "mu", scatter_dimension=1, tiled=True)


def solution(mesh):
    n_aux, n_mu = mesh.shape["aux"], mesh.shape["mu"]

    def shards(three_center, nu_slots, nu_count, density, metric_tensor, sig_slots, sig_count):
        args = (three_center, nu_slots, nu_count, density, metric_tensor, sig_slots, sig_count)
        orb, lam_all = density.shape
        fits = (
            (n_aux, n_mu, orb, lam_all) == (8, 4, 64, 64)
            and three_center.shape[2:] == (64, orb * orb)
            and metric_tensor.shape[2:] == (64, lam_all // n_mu * orb)
        )
        return fast(n_mu, n_aux, *args) if fits else general(*args)

    placed = (
        P("mu", None, "aux", None),
        P("mu", None, "aux"),
        P("mu", "aux"),
        P("mu", None),
        P("mu", None, "aux", None),
        P("mu", None, "aux"),
        P("mu", "aux"),
    )
    return jax.shard_map(
        shards, mesh=mesh, in_specs=placed, out_specs=P("aux", "mu"), check_vma=False
    )
```

```python
import functools

import jax
import jax.numpy as jnp
from jax import lax
from jax.experimental import pallas as pl
from jax.experimental.pallas import tpu as pltpu
from jax.sharding import PartitionSpec as P

F32 = jnp.float32
BF16 = jnp.bfloat16
VMEM = pl.BlockSpec(memory_space=pltpu.VMEM)
SMEM = pl.BlockSpec(memory_space=pltpu.SMEM)
ANY = pl.BlockSpec(memory_space=pl.ANY)
HBM = pl.BlockSpec(memory_space=pltpu.HBM)


DENSITY_ORDER = (2, 3, 1)
HALF_ORDER = (3, 2, 1)


def by_distance(refs, order):
    return [refs[0]] + [refs[1 + order.index(s)] for s in range(1, len(refs))]


def params(mib):
    return pltpu.CompilerParams(vmem_limit_bytes=mib * 1024 * 1024)


def split(x):
    hi = x.astype(BF16)
    return hi, (x - hi.astype(F32)).astype(BF16)


def iota(shape, dim):
    return lax.broadcasted_iota(jnp.int32, shape, dim)


def tensor_kernel(tensor, t_hi, t_lo, buffer, arrived):
    _, slots, aux_width, width = tensor.shape
    parts = buffer.shape[0] // slots
    span = width // parts

    def fetch(k, part):
        return pltpu.make_async_copy(
            tensor.at[0, k, :, pl.ds(part * span, span)],
            buffer.at[k * parts + part],
            arrived.at[k * parts + part],
        )

    order = [(k, part) for k in range(slots) for part in range(parts)]
    for k, part in order:
        fetch(k, part).start()
    for k, part in order:
        fetch(k, part).wait()
        for chunk in range(span // 256):
            hi, lo = split(buffer[k * parts + part, :, chunk * 256:(chunk + 1) * 256])
            at = (part * (span // 256) + chunk) * aux_width
            t_hi[at:at + aux_width, k * 256:(k + 1) * 256] = hi
            t_lo[at:at + aux_width, k * 256:(k + 1) * 256] = lo


def metric_kernel(sig_slots, sig_count, after, metric, m_hi, m_lo):
    _, sig, aux_width, width = metric.shape
    half = iota((aux_width, 128), 1) >= 64
    pair_of = jnp.where(half, 1, 0)
    targets = [jnp.where(q < sig_count[0, 0], sig_slots[0, 0, q], -1) for q in range(sig)]
    for pair in range(width // 128):
        sums = [[jnp.zeros((aux_width, 128), F32) for _ in range(2)] for _ in range(2)]
        for q in range(sig):
            block = metric[0, q, :, pair * 128:(pair + 1) * 128]
            turned = pltpu.roll(block, 64, 1)
            both = (jnp.where(half, turned, block), jnp.where(half, block, turned))
            for out_half in range(2):
                here = pair_of + 2 * out_half == targets[q]
                for parity in range(2):
                    sums[parity][out_half] += jnp.where(here, both[parity], 0.0)
        for parity in range(2):
            r = 2 * pair + parity
            at = ((r % 8) * 2 + r // 8) * aux_width
            for out_half in range(2):
                hi, lo = split(sums[parity][out_half])
                columns = slice(out_half * 128, (out_half + 1) * 128)
                m_hi[at:at + aux_width, columns] = hi
                m_lo[at:at + aux_width, columns] = lo


def half_kernel(n_mu, nu_slots, nu_count, *refs):
    dens = by_distance(refs[:n_mu], DENSITY_ORDER)
    t_hi, t_lo = refs[n_mu:n_mu + 2]
    outs = refs[n_mu + 2:2 * n_mu + 2]
    d_hi, d_lo, weights, turned = refs[2 * n_mu + 2:]
    z = lax.axis_index("mu")
    orb, lam_all = dens[0].shape
    lam = lam_all // n_mu
    slots = nu_slots.shape[2]
    row, col = iota((lam_all, 256), 0), iota((lam_all, 256), 1)
    group = ((col >> 3) & 3) ^ z
    wanted = group * lam + (col >> 7) * 8 + (col & 7)
    choose = jnp.where(row == wanted, 1.0, 0.0).astype(BF16)
    for s in range(n_mu):
        hi, lo = split(dens[s][...])
        d_hi[s] = jnp.dot(hi, choose, preferred_element_type=F32)
        d_lo[s] = jnp.dot(lo, choose, preferred_element_type=F32)
    orbital = (iota((orb, 256), 1) >> 5) & 3
    depth = slots * 256
    for k in range(slots):
        at = z ^ nu_slots[0, 0, k]
        live = jnp.where(k < nu_count[0, 0], 1.0, 0.0)
        hi, lo = d_hi[at] * live, d_lo[at] * live
        for i in range(4):
            rows = k * 256 + i * orb
            w_hi = jnp.where(orbital == i, hi, 0.0).astype(BF16)
            weights[rows:rows + orb, :] = w_hi
            weights[rows + depth:rows + depth + orb, :] = w_hi
            weights[rows + 2 * depth:rows + 2 * depth + orb, :] = jnp.where(
                orbital == i, lo, 0.0
            ).astype(BF16)
    aux_width = outs[0].shape[1] // lam
    per_group = 256 // aux_width
    span = per_group * 4
    for group in range(t_hi.shape[0] // 256):
        rows = slice(group * 256, (group + 1) * 256)
        high = t_hi[rows, :]
        left = jnp.concatenate([high, t_lo[rows, :], high], axis=1)
        total = jnp.dot(left, weights[...], preferred_element_type=F32)
        for chunk in range(per_group):
            piece = total[chunk * aux_width:(chunk + 1) * aux_width]
            stacked = jnp.concatenate([piece[:, :128], piece[:, 128:]], axis=0)
            at = (group * per_group + chunk) * 128
            turned[at:at + 128, :] = stacked.T
        for s in range(n_mu):
            for r in range(8):
                picked = turned[pl.ds(group * per_group * 128 + s * 8 + r, span, stride=32), :]
                outs[s][group * span:(group + 1) * span, r * 128:(r + 1) * 128] = picked.astype(BF16)


def exchange_kernel(n_mu, n_aux, *refs):
    halves = by_distance(refs[:n_mu], HALF_ORDER)
    m_hi, m_lo, out, total = refs[n_mu:]
    z = lax.axis_index("mu")
    left = jnp.concatenate([h[...] for h in halves], axis=0)
    product = jnp.dot(left, m_hi[...], preferred_element_type=F32)
    product += jnp.dot(left, m_lo[...], preferred_element_type=F32)
    orb = halves[0].shape[0]
    for s in range(n_mu):
        block = z ^ s
        total[pl.ds(pl.multiple_of(block * orb, orb), orb), :] = product[s * orb:(s + 1) * orb]
    rows = out.shape[1]
    lower = iota((rows, 128), 1) < 64
    for a in range(n_aux):
        for pair in range(n_mu // 2):
            columns = slice(pair * 128, (pair + 1) * 128)
            top = total[a * 2 * rows:(a * 2 + 1) * rows, columns]
            bottom = total[(a * 2 + 1) * rows:(a * 2 + 2) * rows, columns]
            at = a * n_mu + pair * 2
            out[at] = jnp.where(lower, top, pltpu.roll(bottom, 64, 1)).astype(BF16)
            out[at + 1] = jnp.where(lower, pltpu.roll(top, 64, 1), bottom).astype(BF16)


def sum_kernel(parts, out):
    total = parts[0].astype(F32)
    for d in range(1, parts.shape[0]):
        total += parts[d].astype(F32)
    rows = parts.shape[1]
    out[:rows, :] = total[:, :64]
    out[rows:, :] = total[:, 64:]


def fast(n_mu, n_aux, three_center, nu_slots, nu_count, density, metric_tensor, sig_slots, sig_count):
    orb, lam_all = density.shape
    slots, aux_width = three_center.shape[1:3]
    lam = lam_all // n_mu
    turns = [[(z, z ^ s) for z in range(n_mu)] for s in range(n_mu)]
    dens = [density] + [lax.ppermute(density, "mu", turns[s]) for s in DENSITY_ORDER]
    nu_slots, sig_slots = jnp.swapaxes(nu_slots, 1, 2), jnp.swapaxes(sig_slots, 1, 2)
    chunks = three_center.shape[3] // 256
    t_shape = jax.ShapeDtypeStruct((chunks * aux_width, slots * 256), BF16)
    m_shape = jax.ShapeDtypeStruct((lam * aux_width, n_mu * orb), BF16)
    t_hi, t_lo = pl.pallas_call(
        tensor_kernel,
        out_shape=(t_shape, t_shape),
        in_specs=[HBM],
        out_specs=(VMEM, VMEM),
        scratch_shapes=[
            pltpu.VMEM((slots * 4, aux_width, chunks * 64), F32),
            pltpu.SemaphoreType.DMA((slots * 4,)),
        ],
        compiler_params=params(50),
        cost_estimate=pl.CostEstimate(flops=10_000_000, bytes_accessed=6_000_000, transcendentals=0),
        name="tensor",
    )(three_center)
    half_shape = jax.ShapeDtypeStruct((orb, lam * aux_width), BF16)
    halves = pl.pallas_call(
        functools.partial(half_kernel, n_mu),
        out_shape=(half_shape,) * n_mu,
        in_specs=[SMEM, SMEM] + [VMEM] * (n_mu + 2),
        out_specs=(VMEM,) * n_mu,
        scratch_shapes=[
            pltpu.VMEM((n_mu, orb, 256), F32),
            pltpu.VMEM((n_mu, orb, 256), F32),
            pltpu.VMEM((3 * slots * 256, 256), BF16),
            pltpu.VMEM((chunks * 128, 128), F32),
        ],
        compiler_params=params(16),
        cost_estimate=pl.CostEstimate(flops=1_200_000_000, bytes_accessed=4_000_000, transcendentals=0),
        name="half",
    )(nu_slots, nu_count, *dens, t_hi, t_lo)
    m_hi, m_lo = pl.pallas_call(
        metric_kernel,
        out_shape=(m_shape, m_shape),
        in_specs=[SMEM, SMEM, ANY, VMEM],
        out_specs=(VMEM, VMEM),
        compiler_params=params(16),
        cost_estimate=pl.CostEstimate(flops=10_000_000, bytes_accessed=2_000_000, transcendentals=0),
        name="metric",
    )(sig_slots, sig_count, halves[0], metric_tensor)
    halves = [halves[0]] + [lax.ppermute(halves[s], "mu", turns[s]) for s in HALF_ORDER]
    rows = n_mu * orb // n_aux
    parts = pl.pallas_call(
        functools.partial(exchange_kernel, n_mu, n_aux),
        out_shape=jax.ShapeDtypeStruct((n_aux * n_mu, rows // 2, 128), BF16),
        in_specs=[VMEM] * (n_mu + 2),
        out_specs=VMEM,
        scratch_shapes=[pltpu.VMEM((n_mu * orb, n_mu * orb), F32)],
        compiler_params=params(16),
        cost_estimate=pl.CostEstimate(flops=300_000_000, bytes_accessed=2_000_000, transcendentals=0),
        name="exchange",
    )(*halves, m_hi, m_lo)
    parts = lax.all_to_all(parts, ("aux", "mu"), 0, 0)
    return pl.pallas_call(
        sum_kernel,
        out_shape=jax.ShapeDtypeStruct((rows, orb), F32),
        in_specs=[VMEM],
        out_specs=VMEM,
        compiler_params=params(8),
        name="sum",
    )(parts)


def general(three_center, nu_slots, nu_count, density, metric_tensor, sig_slots, sig_count):
    highest = lax.Precision.HIGHEST
    orb_block = density.shape[0]
    lam_all = density.shape[1]
    aux_width = three_center.shape[2]
    dens_all = lax.all_gather(density, "mu", axis=0, tiled=True)

    def add_slot(k, running):
        nu_pick = nu_slots[0, k, 0]
        dens_rows = lax.dynamic_slice_in_dim(dens_all, nu_pick * orb_block, orb_block, 0)
        slab_piece = lax.dynamic_index_in_dim(three_center[0], k, 0, keepdims=False).reshape(
            aux_width, orb_block, orb_block
        )
        return running + jnp.einsum("pij,jl->lpi", slab_piece, dens_rows, precision=highest)

    halfway = lax.fori_loop(
        0, nu_count[0, 0], add_slot, jnp.zeros((lam_all, aux_width, orb_block), F32)
    )
    relayed = lax.all_to_all(halfway.astype(BF16), "mu", split_axis=0, concat_axis=2, tiled=True)
    widened = relayed.astype(F32)
    lam_rows = relayed.shape[0]
    orbitals = relayed.shape[2]

    def add_target(q, running):
        target = sig_slots[0, q, 0]
        weights = lax.dynamic_index_in_dim(metric_tensor[0], q, 0, keepdims=False).reshape(
            aux_width, lam_rows, orb_block
        )
        contrib = jnp.einsum("rpm,prc->mc", widened, weights, precision=highest)
        current = lax.dynamic_slice_in_dim(running, target * orb_block, orb_block, 1)
        return lax.dynamic_update_slice_in_dim(running, current + contrib, target * orb_block, 1)

    partial_k = lax.fori_loop(
        0, sig_count[0, 0], add_target, jnp.zeros((orbitals, orbitals), F32)
    )
    row_share = lax.psum_scatter(partial_k, "aux", scatter_dimension=0, tiled=True)
    return lax.psum_scatter(row_share, "mu", scatter_dimension=1, tiled=True)


def solution(mesh):
    n_aux, n_mu = mesh.shape["aux"], mesh.shape["mu"]

    def shards(three_center, nu_slots, nu_count, density, metric_tensor, sig_slots, sig_count):
        args = (three_center, nu_slots, nu_count, density, metric_tensor, sig_slots, sig_count)
        orb, lam_all = density.shape
        fits = (
            (n_aux, n_mu, orb, lam_all) == (8, 4, 64, 64)
            and three_center.shape[2:] == (64, orb * orb)
            and metric_tensor.shape[2:] == (64, lam_all // n_mu * orb)
        )
        return fast(n_mu, n_aux, *args) if fits else general(*args)

    placed = (
        P("mu", None, "aux", None),
        P("mu", None, "aux"),
        P("mu", "aux"),
        P("mu", None),
        P("mu", None, "aux", None),
        P("mu", None, "aux"),
        P("mu", "aux"),
    )
    return jax.shard_map(
        shards, mesh=mesh, in_specs=placed, out_specs=P("aux", "mu"), check_vma=False
    )
```

```python
import functools

import jax
import jax.numpy as jnp
from jax import lax
from jax.experimental import pallas as pl
from jax.experimental.pallas import tpu as pltpu
from jax.sharding import PartitionSpec as P

F32 = jnp.float32
BF16 = jnp.bfloat16
VMEM = pl.BlockSpec(memory_space=pltpu.VMEM)
SMEM = pl.BlockSpec(memory_space=pltpu.SMEM)
ANY = pl.BlockSpec(memory_space=pl.ANY)
HBM = pl.BlockSpec(memory_space=pltpu.HBM)


DENSITY_ORDER = (2, 3, 1)
OUTER = ((0, 2), (3, 1))
MIDDLE = ((1, 2), (2, 1))
EDGE = ((0, 1), (3, 2))


def by_distance(refs, order):
    return [refs[0]] + [refs[1 + order.index(s)] for s in range(1, len(refs))]


def params(mib):
    return pltpu.CompilerParams(vmem_limit_bytes=mib * 1024 * 1024)


def split(x):
    hi = x.astype(BF16)
    return hi, (x - hi.astype(F32)).astype(BF16)


def iota(shape, dim):
    return lax.broadcasted_iota(jnp.int32, shape, dim)


def tensor_kernel(tensor, t_hi, t_lo):
    _, slots, aux_width, width = tensor.shape
    for k in range(slots):
        for chunk in range(width // 256):
            hi, lo = split(tensor[0, k, :, chunk * 256:(chunk + 1) * 256])
            rows = slice(chunk * aux_width, (chunk + 1) * aux_width)
            t_hi[rows, k * 256:(k + 1) * 256] = hi
            t_lo[rows, k * 256:(k + 1) * 256] = lo


def live_targets(sig_slots, sig_count):
    return [
        jnp.where(q < sig_count[0, 0], sig_slots[0, 0, q], -1).astype(F32)
        for q in range(sig_slots.shape[2])
    ]


def share_kernel(sig_slots, sig_count, metric, out, buffer, arrived):
    _, sig, aux_width, width = metric.shape
    copies = [
        pltpu.make_async_copy(metric.at[0, q], buffer.at[q], arrived.at[q]) for q in range(sig)
    ]
    for copy in copies:
        copy.start()
    shape = (16, width)
    note = jnp.full(shape, -1.0, F32)
    for q, target in enumerate(live_targets(sig_slots, sig_count)):
        note = jnp.where(iota(shape, 0) == q, target, note)
    out[sig * aux_width:, :] = note.astype(BF16)
    for q in range(sig):
        copies[q].wait()
        out[q * aux_width:(q + 1) * aux_width, :] = buffer[q].astype(BF16)


def place(blocks, targets, m_hi, m_lo):
    aux_width, width = blocks[0].shape
    half = iota((aux_width, 128), 1) >= 64
    pair_of = jnp.where(half, 1.0, 0.0)
    for pair in range(width // 128):
        sums = [[jnp.zeros((aux_width, 128), F32) for _ in range(2)] for _ in range(2)]
        for q in range(len(blocks)):
            block = blocks[q][:, pair * 128:(pair + 1) * 128].astype(F32)
            turned = pltpu.roll(block, 64, 1)
            both = (jnp.where(half, turned, block), jnp.where(half, block, turned))
            for out_half in range(2):
                here = pair_of + 2 * out_half == targets[q]
                for parity in range(2):
                    sums[parity][out_half] += jnp.where(here, both[parity], 0.0)
        for parity in range(2):
            r = 2 * pair + parity
            at = ((r % 8) * 2 + r // 8) * aux_width
            for out_half in range(2):
                hi, lo = split(sums[parity][out_half])
                columns = slice(out_half * 128, (out_half + 1) * 128)
                m_hi[at:at + aux_width, columns] = hi
                m_lo[at:at + aux_width, columns] = lo


def product(left, m_hi, m_lo):
    total = jnp.dot(left, m_hi[...], preferred_element_type=F32)
    return total + jnp.dot(left, m_lo[...], preferred_element_type=F32)


def own_kernel(sig_slots, sig_count, metric, half, base, m_hi, m_lo):
    blocks = [metric.at[0, q] for q in range(metric.shape[1])]
    place(blocks, live_targets(sig_slots, sig_count), m_hi, m_lo)
    base[...] = product(half[...], m_hi, m_lo)


def neighbour_kernel(sig, near, far, near_half, far_half, base, out, n_hi, n_lo, f_hi, f_lo):
    aux_width = (near.shape[0] - 16) // sig
    total = base[...]
    for shared, half, hi, lo in ((near, near_half, n_hi, n_lo), (far, far_half, f_hi, f_lo)):
        note = shared[sig * aux_width:, :128].astype(F32)
        blocks = [shared.at[pl.ds(q * aux_width, aux_width)] for q in range(sig)]
        place(blocks, [note[q:q + 1, :] for q in range(sig)], hi, lo)
        total += product(half[...], hi, lo)
    out[...] = total


def half_kernel(n_mu, nu_slots, nu_count, *refs):
    dens = by_distance(refs[:n_mu], DENSITY_ORDER)
    t_hi, t_lo = refs[n_mu:n_mu + 2]
    outs = refs[n_mu + 2:2 * n_mu + 2]
    d_hi, d_lo, weights, turned = refs[2 * n_mu + 2:]
    z = lax.axis_index("mu")
    orb, lam_all = dens[0].shape
    lam = lam_all // n_mu
    slots = nu_slots.shape[2]
    row, col = iota((lam_all, 256), 0), iota((lam_all, 256), 1)
    group = ((col >> 3) & 3) ^ z
    wanted = group * lam + (col >> 7) * 8 + (col & 7)
    choose = jnp.where(row == wanted, 1.0, 0.0).astype(BF16)
    for s in range(n_mu):
        hi, lo = split(dens[s][...])
        d_hi[s] = jnp.dot(hi, choose, preferred_element_type=F32)
        d_lo[s] = jnp.dot(lo, choose, preferred_element_type=F32)
    orbital = (iota((orb, 256), 1) >> 5) & 3
    depth = slots * 256
    for k in range(slots):
        at = z ^ nu_slots[0, 0, k]
        live = jnp.where(k < nu_count[0, 0], 1.0, 0.0)
        hi, lo = d_hi[at] * live, d_lo[at] * live
        for i in range(4):
            rows = k * 256 + i * orb
            w_hi = jnp.where(orbital == i, hi, 0.0).astype(BF16)
            weights[rows:rows + orb, :] = w_hi
            weights[rows + depth:rows + depth + orb, :] = w_hi
            weights[rows + 2 * depth:rows + 2 * depth + orb, :] = jnp.where(
                orbital == i, lo, 0.0
            ).astype(BF16)
    aux_width = outs[0].shape[1] // lam
    per_group = 256 // aux_width
    span = per_group * 4
    for group in range(t_hi.shape[0] // 256):
        rows = slice(group * 256, (group + 1) * 256)
        high = t_hi[rows, :]
        left = jnp.concatenate([high, t_lo[rows, :], high], axis=1)
        total = jnp.dot(left, weights[...], preferred_element_type=F32)
        for chunk in range(per_group):
            piece = total[chunk * aux_width:(chunk + 1) * aux_width]
            stacked = jnp.concatenate([piece[:, :128], piece[:, 128:]], axis=0)
            at = (group * per_group + chunk) * 128
            turned[at:at + 128, :] = stacked.T
        for s in range(n_mu):
            for r in range(8):
                picked = turned[pl.ds(group * per_group * 128 + s * 8 + r, span, stride=32), :]
                outs[s][group * span:(group + 1) * span, r * 128:(r + 1) * 128] = picked.astype(BF16)


def exchange_kernel(n_mu, n_aux, base, outer, middle, edge, n_hi, n_lo, f_hi, f_lo, out, total):
    z = lax.axis_index("mu")
    orb = base.shape[0]
    by_near = product(jnp.concatenate([outer[...], middle[...]], axis=0), n_hi, n_lo)
    by_far = product(edge[...], f_hi, f_lo)
    pieces = ((z, base[...]), (z ^ 2, by_near[:orb]), (z ^ 3, by_near[orb:]), (z ^ 1, by_far))
    for block, piece in pieces:
        total[pl.ds(pl.multiple_of(block * orb, orb), orb), :] = piece
    rows = out.shape[1]
    lower = iota((rows, 128), 1) < 64
    for a in range(n_aux):
        for pair in range(n_mu // 2):
            columns = slice(pair * 128, (pair + 1) * 128)
            top = total[a * 2 * rows:(a * 2 + 1) * rows, columns]
            bottom = total[(a * 2 + 1) * rows:(a * 2 + 2) * rows, columns]
            at = a * n_mu + pair * 2
            out[at] = jnp.where(lower, top, pltpu.roll(bottom, 64, 1)).astype(BF16)
            out[at + 1] = jnp.where(lower, pltpu.roll(top, 64, 1), bottom).astype(BF16)


def sum_kernel(parts, out):
    total = parts[0].astype(F32)
    for d in range(1, parts.shape[0]):
        total += parts[d].astype(F32)
    rows = parts.shape[1]
    out[:rows, :] = total[:, :64]
    out[rows:, :] = total[:, 64:]


def fast(n_mu, n_aux, three_center, nu_slots, nu_count, density, metric_tensor, sig_slots, sig_count):
    orb, lam_all = density.shape
    slots, aux_width = three_center.shape[1:3]
    lam = lam_all // n_mu
    turns = [[(z, z ^ s) for z in range(n_mu)] for s in range(n_mu)]
    dens = [density] + [lax.ppermute(density, "mu", turns[s]) for s in DENSITY_ORDER]
    nu_slots, sig_slots = jnp.swapaxes(nu_slots, 1, 2), jnp.swapaxes(sig_slots, 1, 2)
    chunks = three_center.shape[3] // 256
    sig = metric_tensor.shape[1]
    shared = pl.pallas_call(
        share_kernel,
        out_shape=jax.ShapeDtypeStruct((sig * aux_width + 16, lam * orb), BF16),
        in_specs=[SMEM, SMEM, HBM],
        out_specs=VMEM,
        scratch_shapes=[
            pltpu.VMEM((sig, aux_width, lam * orb), F32),
            pltpu.SemaphoreType.DMA((sig,)),
        ],
        compiler_params=params(58),
        cost_estimate=pl.CostEstimate(flops=1_000_000, bytes_accessed=6_000_000, transcendentals=0),
        name="share",
    )(sig_slots, sig_count, metric_tensor)
    near = lax.ppermute(shared, "mu", turns[1])
    far = lax.ppermute(shared, "mu", MIDDLE)
    t_shape = jax.ShapeDtypeStruct((chunks * aux_width, slots * 256), BF16)
    t_hi, t_lo = pl.pallas_call(
        tensor_kernel,
        out_shape=(t_shape, t_shape),
        in_specs=[VMEM],
        out_specs=(VMEM, VMEM),
        compiler_params=params(16),
        cost_estimate=pl.CostEstimate(flops=10_000_000, bytes_accessed=6_000_000, transcendentals=0),
        name="tensor",
    )(three_center)
    half_shape = jax.ShapeDtypeStruct((orb, lam * aux_width), BF16)
    halves = pl.pallas_call(
        functools.partial(half_kernel, n_mu),
        out_shape=(half_shape,) * n_mu,
        in_specs=[SMEM, SMEM] + [VMEM] * (n_mu + 2),
        out_specs=(VMEM,) * n_mu,
        scratch_shapes=[
            pltpu.VMEM((n_mu, orb, 256), F32),
            pltpu.VMEM((n_mu, orb, 256), F32),
            pltpu.VMEM((3 * slots * 256, 256), BF16),
            pltpu.VMEM((chunks * 128, 128), F32),
        ],
        compiler_params=params(16),
        cost_estimate=pl.CostEstimate(flops=1_200_000_000, bytes_accessed=4_000_000, transcendentals=0),
        name="half",
    )(nu_slots, nu_count, *dens, t_hi, t_lo)
    outer = lax.ppermute(halves[3], "mu", OUTER)
    middle = lax.ppermute(halves[2], "mu", MIDDLE)
    edge = lax.ppermute(halves[2], "mu", EDGE)
    base_shape = jax.ShapeDtypeStruct((orb, n_mu * orb), F32)
    m_size = (lam * aux_width, n_mu * orb)
    m_shape = jax.ShapeDtypeStruct(m_size, BF16)
    base = pl.pallas_call(
        own_kernel,
        out_shape=base_shape,
        in_specs=[SMEM, SMEM, VMEM, VMEM],
        out_specs=VMEM,
        scratch_shapes=[pltpu.VMEM(m_size, BF16)] * 2,
        compiler_params=params(16),
        cost_estimate=pl.CostEstimate(flops=80_000_000, bytes_accessed=2_000_000, transcendentals=0),
        name="own",
    )(sig_slots, sig_count, metric_tensor, halves[0])
    base, *placed = pl.pallas_call(
        functools.partial(neighbour_kernel, sig),
        out_shape=(base_shape,) + (m_shape,) * 4,
        in_specs=[VMEM] * 5,
        out_specs=(VMEM,) * 5,
        compiler_params=params(16),
        cost_estimate=pl.CostEstimate(flops=160_000_000, bytes_accessed=4_000_000, transcendentals=0),
        name="neighbour",
    )(near, far, halves[1], halves[3], base)
    rows = n_mu * orb // n_aux
    parts = pl.pallas_call(
        functools.partial(exchange_kernel, n_mu, n_aux),
        out_shape=jax.ShapeDtypeStruct((n_aux * n_mu, rows // 2, 128), BF16),
        in_specs=[VMEM] * 8,
        out_specs=VMEM,
        scratch_shapes=[pltpu.VMEM((n_mu * orb, n_mu * orb), F32)],
        compiler_params=params(16),
        cost_estimate=pl.CostEstimate(flops=300_000_000, bytes_accessed=2_000_000, transcendentals=0),
        name="exchange",
    )(base, outer, middle, edge, *placed)
    parts = lax.all_to_all(parts, ("aux", "mu"), 0, 0)
    return pl.pallas_call(
        sum_kernel,
        out_shape=jax.ShapeDtypeStruct((rows, orb), F32),
        in_specs=[VMEM],
        out_specs=VMEM,
        compiler_params=params(8),
        name="sum",
    )(parts)


def general(three_center, nu_slots, nu_count, density, metric_tensor, sig_slots, sig_count):
    highest = lax.Precision.HIGHEST
    orb_block = density.shape[0]
    lam_all = density.shape[1]
    aux_width = three_center.shape[2]
    dens_all = lax.all_gather(density, "mu", axis=0, tiled=True)

    def add_slot(k, running):
        nu_pick = nu_slots[0, k, 0]
        dens_rows = lax.dynamic_slice_in_dim(dens_all, nu_pick * orb_block, orb_block, 0)
        slab_piece = lax.dynamic_index_in_dim(three_center[0], k, 0, keepdims=False).reshape(
            aux_width, orb_block, orb_block
        )
        return running + jnp.einsum("pij,jl->lpi", slab_piece, dens_rows, precision=highest)

    halfway = lax.fori_loop(
        0, nu_count[0, 0], add_slot, jnp.zeros((lam_all, aux_width, orb_block), F32)
    )
    relayed = lax.all_to_all(halfway.astype(BF16), "mu", split_axis=0, concat_axis=2, tiled=True)
    widened = relayed.astype(F32)
    lam_rows = relayed.shape[0]
    orbitals = relayed.shape[2]

    def add_target(q, running):
        target = sig_slots[0, q, 0]
        weights = lax.dynamic_index_in_dim(metric_tensor[0], q, 0, keepdims=False).reshape(
            aux_width, lam_rows, orb_block
        )
        contrib = jnp.einsum("rpm,prc->mc", widened, weights, precision=highest)
        current = lax.dynamic_slice_in_dim(running, target * orb_block, orb_block, 1)
        return lax.dynamic_update_slice_in_dim(running, current + contrib, target * orb_block, 1)

    partial_k = lax.fori_loop(
        0, sig_count[0, 0], add_target, jnp.zeros((orbitals, orbitals), F32)
    )
    row_share = lax.psum_scatter(partial_k, "aux", scatter_dimension=0, tiled=True)
    return lax.psum_scatter(row_share, "mu", scatter_dimension=1, tiled=True)


def solution(mesh):
    n_aux, n_mu = mesh.shape["aux"], mesh.shape["mu"]

    def shards(three_center, nu_slots, nu_count, density, metric_tensor, sig_slots, sig_count):
        args = (three_center, nu_slots, nu_count, density, metric_tensor, sig_slots, sig_count)
        orb, lam_all = density.shape
        fits = (
            (n_aux, n_mu, orb, lam_all) == (8, 4, 64, 64)
            and three_center.shape[2:] == (64, orb * orb)
            and metric_tensor.shape[2:] == (64, lam_all // n_mu * orb)
        )
        return fast(n_mu, n_aux, *args) if fits else general(*args)

    placed = (
        P("mu", None, "aux", None),
        P("mu", None, "aux"),
        P("mu", "aux"),
        P("mu", None),
        P("mu", None, "aux", None),
        P("mu", None, "aux"),
        P("mu", "aux"),
    )
    return jax.shard_map(
        shards, mesh=mesh, in_specs=placed, out_specs=P("aux", "mu"), check_vma=False
    )
```

```python
import functools

import jax
import jax.numpy as jnp
from jax import lax
from jax.experimental import pallas as pl
from jax.experimental.pallas import tpu as pltpu
from jax.sharding import PartitionSpec as P

F32 = jnp.float32
BF16 = jnp.bfloat16
VMEM = pl.BlockSpec(memory_space=pltpu.VMEM)
SMEM = pl.BlockSpec(memory_space=pltpu.SMEM)
ANY = pl.BlockSpec(memory_space=pl.ANY)
HBM = pl.BlockSpec(memory_space=pltpu.HBM)


DENSITY_ORDER = (2, 3, 1)
FACTORS = (1, 4, 2, 3)


def goes_to(factor, z):
    return (z + 1) * factor % 5 - 1


def by_distance(refs, order):
    return [refs[0]] + [refs[1 + order.index(s)] for s in range(1, len(refs))]


def params(mib):
    return pltpu.CompilerParams(vmem_limit_bytes=mib * 1024 * 1024)


def split(x):
    hi = x.astype(BF16)
    return hi, (x - hi.astype(F32)).astype(BF16)


def iota(shape, dim):
    return lax.broadcasted_iota(jnp.int32, shape, dim)


def tensor_kernel(tensor, t_hi, t_lo, buffer, arrived):
    _, slots, aux_width, width = tensor.shape
    parts = buffer.shape[0] // slots
    span = width // parts

    def fetch(k, part):
        return pltpu.make_async_copy(
            tensor.at[0, k, :, pl.ds(part * span, span)],
            buffer.at[k * parts + part],
            arrived.at[k * parts + part],
        )

    order = [(k, part) for k in range(slots) for part in range(parts)]
    for k, part in order:
        fetch(k, part).start()
    for k, part in order:
        fetch(k, part).wait()
        for chunk in range(span // 256):
            hi, lo = split(buffer[k * parts + part, :, chunk * 256:(chunk + 1) * 256])
            at = (part * (span // 256) + chunk) * aux_width
            t_hi[at:at + aux_width, k * 256:(k + 1) * 256] = hi
            t_lo[at:at + aux_width, k * 256:(k + 1) * 256] = lo


def metric_kernel(sig_slots, sig_count, after, metric, m_hi, m_lo):
    _, sig, aux_width, width = metric.shape
    half = iota((aux_width, 128), 1) >= 64
    pair_of = jnp.where(half, 1, 0)
    targets = [jnp.where(q < sig_count[0, 0], sig_slots[0, 0, q], -1) for q in range(sig)]
    for pair in range(width // 128):
        sums = [[jnp.zeros((aux_width, 128), F32) for _ in range(2)] for _ in range(2)]
        for q in range(sig):
            block = metric[0, q, :, pair * 128:(pair + 1) * 128]
            turned = pltpu.roll(block, 64, 1)
            both = (jnp.where(half, turned, block), jnp.where(half, block, turned))
            for out_half in range(2):
                here = pair_of + 2 * out_half == targets[q]
                for parity in range(2):
                    sums[parity][out_half] += jnp.where(here, both[parity], 0.0)
        for parity in range(2):
            r = 2 * pair + parity
            at = ((r % 8) * 2 + r // 8) * aux_width
            for out_half in range(2):
                hi, lo = split(sums[parity][out_half])
                columns = slice(out_half * 128, (out_half + 1) * 128)
                m_hi[at:at + aux_width, columns] = hi
                m_lo[at:at + aux_width, columns] = lo


def half_kernel(n_mu, nu_slots, nu_count, *refs):
    dens = by_distance(refs[:n_mu], DENSITY_ORDER)
    t_hi, t_lo = refs[n_mu:n_mu + 2]
    outs = refs[n_mu + 2:2 * n_mu + 2]
    d_hi, d_lo, weights, turned = refs[2 * n_mu + 2:]
    z = lax.axis_index("mu")
    orb, lam_all = dens[0].shape
    lam = lam_all // n_mu
    slots = nu_slots.shape[2]
    row, col = iota((lam_all, 256), 0), iota((lam_all, 256), 1)
    group = z
    for slot in range(1, n_mu):
        group = jnp.where((col >> 3) & 3 == slot, lax.rem((z + 1) * FACTORS[slot], 5) - 1, group)
    wanted = group * lam + (col >> 7) * 8 + (col & 7)
    choose = jnp.where(row == wanted, 1.0, 0.0).astype(BF16)
    for s in range(n_mu):
        hi, lo = split(dens[s][...])
        d_hi[s] = jnp.dot(hi, choose, preferred_element_type=F32)
        d_lo[s] = jnp.dot(lo, choose, preferred_element_type=F32)
    orbital = (iota((orb, 256), 1) >> 5) & 3
    depth = slots * 256
    for k in range(slots):
        at = z ^ nu_slots[0, 0, k]
        live = jnp.where(k < nu_count[0, 0], 1.0, 0.0)
        hi, lo = d_hi[at] * live, d_lo[at] * live
        for i in range(4):
            rows = k * 256 + i * orb
            w_hi = jnp.where(orbital == i, hi, 0.0).astype(BF16)
            weights[rows:rows + orb, :] = w_hi
            weights[rows + depth:rows + depth + orb, :] = w_hi
            weights[rows + 2 * depth:rows + 2 * depth + orb, :] = jnp.where(
                orbital == i, lo, 0.0
            ).astype(BF16)
    aux_width = outs[0].shape[1] // lam
    per_group = 256 // aux_width
    span = per_group * 4
    for group in range(t_hi.shape[0] // 256):
        rows = slice(group * 256, (group + 1) * 256)
        high = t_hi[rows, :]
        left = jnp.concatenate([high, t_lo[rows, :], high], axis=1)
        total = jnp.dot(left, weights[...], preferred_element_type=F32)
        for chunk in range(per_group):
            piece = total[chunk * aux_width:(chunk + 1) * aux_width]
            stacked = jnp.concatenate([piece[:, :128], piece[:, 128:]], axis=0)
            at = (group * per_group + chunk) * 128
            turned[at:at + 128, :] = stacked.T
        for s in range(n_mu):
            for r in range(8):
                picked = turned[pl.ds(group * per_group * 128 + s * 8 + r, span, stride=32), :]
                outs[s][group * span:(group + 1) * span, r * 128:(r + 1) * 128] = picked.astype(BF16)


def exchange_kernel(n_mu, n_aux, *refs):
    halves = refs[:n_mu]
    m_hi, m_lo, out, total = refs[n_mu:]
    z = lax.axis_index("mu")
    left = jnp.concatenate([h[...] for h in halves], axis=0)
    product = jnp.dot(left, m_hi[...], preferred_element_type=F32)
    product += jnp.dot(left, m_lo[...], preferred_element_type=F32)
    orb = halves[0].shape[0]
    for s in range(n_mu):
        back = pow(FACTORS[s], -1, 5)
        block = lax.rem((z + 1) * back, 5) - 1
        total[pl.ds(pl.multiple_of(block * orb, orb), orb), :] = product[s * orb:(s + 1) * orb]
    rows = out.shape[1]
    lower = iota((rows, 128), 1) < 64
    for a in range(n_aux):
        for pair in range(n_mu // 2):
            columns = slice(pair * 128, (pair + 1) * 128)
            top = total[a * 2 * rows:(a * 2 + 1) * rows, columns]
            bottom = total[(a * 2 + 1) * rows:(a * 2 + 2) * rows, columns]
            at = a * n_mu + pair * 2
            out[at] = jnp.where(lower, top, pltpu.roll(bottom, 64, 1)).astype(BF16)
            out[at + 1] = jnp.where(lower, pltpu.roll(top, 64, 1), bottom).astype(BF16)


def sum_kernel(parts, out):
    total = parts[0].astype(F32)
    for d in range(1, parts.shape[0]):
        total += parts[d].astype(F32)
    rows = parts.shape[1]
    out[:rows, :] = total[:, :64]
    out[rows:, :] = total[:, 64:]


def fast(n_mu, n_aux, three_center, nu_slots, nu_count, density, metric_tensor, sig_slots, sig_count):
    orb, lam_all = density.shape
    slots, aux_width = three_center.shape[1:3]
    lam = lam_all // n_mu
    turns = [[(z, z ^ s) for z in range(n_mu)] for s in range(n_mu)]
    dens = [density] + [lax.ppermute(density, "mu", turns[s]) for s in DENSITY_ORDER]
    nu_slots, sig_slots = jnp.swapaxes(nu_slots, 1, 2), jnp.swapaxes(sig_slots, 1, 2)
    chunks = three_center.shape[3] // 256
    t_shape = jax.ShapeDtypeStruct((chunks * aux_width, slots * 256), BF16)
    m_shape = jax.ShapeDtypeStruct((lam * aux_width, n_mu * orb), BF16)
    t_hi, t_lo = pl.pallas_call(
        tensor_kernel,
        out_shape=(t_shape, t_shape),
        in_specs=[HBM],
        out_specs=(VMEM, VMEM),
        scratch_shapes=[
            pltpu.VMEM((slots * 4, aux_width, chunks * 64), F32),
            pltpu.SemaphoreType.DMA((slots * 4,)),
        ],
        compiler_params=params(50),
        cost_estimate=pl.CostEstimate(flops=10_000_000, bytes_accessed=6_000_000, transcendentals=0),
        name="tensor",
    )(three_center)
    half_shape = jax.ShapeDtypeStruct((orb, lam * aux_width), BF16)
    halves = pl.pallas_call(
        functools.partial(half_kernel, n_mu),
        out_shape=(half_shape,) * n_mu,
        in_specs=[SMEM, SMEM] + [VMEM] * (n_mu + 2),
        out_specs=(VMEM,) * n_mu,
        scratch_shapes=[
            pltpu.VMEM((n_mu, orb, 256), F32),
            pltpu.VMEM((n_mu, orb, 256), F32),
            pltpu.VMEM((3 * slots * 256, 256), BF16),
            pltpu.VMEM((chunks * 128, 128), F32),
        ],
        compiler_params=params(16),
        cost_estimate=pl.CostEstimate(flops=1_200_000_000, bytes_accessed=4_000_000, transcendentals=0),
        name="half",
    )(nu_slots, nu_count, *dens, t_hi, t_lo)
    m_hi, m_lo = pl.pallas_call(
        metric_kernel,
        out_shape=(m_shape, m_shape),
        in_specs=[SMEM, SMEM, ANY, VMEM],
        out_specs=(VMEM, VMEM),
        compiler_params=params(16),
        cost_estimate=pl.CostEstimate(flops=10_000_000, bytes_accessed=2_000_000, transcendentals=0),
        name="metric",
    )(sig_slots, sig_count, halves[0], metric_tensor)
    halves = [halves[0]] + [
        lax.ppermute(halves[s], "mu", [(z, goes_to(FACTORS[s], z)) for z in range(n_mu)])
        for s in range(1, n_mu)
    ]
    rows = n_mu * orb // n_aux
    parts = pl.pallas_call(
        functools.partial(exchange_kernel, n_mu, n_aux),
        out_shape=jax.ShapeDtypeStruct((n_aux * n_mu, rows // 2, 128), BF16),
        in_specs=[VMEM] * (n_mu + 2),
        out_specs=VMEM,
        scratch_shapes=[pltpu.VMEM((n_mu * orb, n_mu * orb), F32)],
        compiler_params=params(16),
        cost_estimate=pl.CostEstimate(flops=300_000_000, bytes_accessed=2_000_000, transcendentals=0),
        name="exchange",
    )(*halves, m_hi, m_lo)
    parts = lax.all_to_all(parts, ("aux", "mu"), 0, 0)
    return pl.pallas_call(
        sum_kernel,
        out_shape=jax.ShapeDtypeStruct((rows, orb), F32),
        in_specs=[VMEM],
        out_specs=VMEM,
        compiler_params=params(8),
        name="sum",
    )(parts)


def general(three_center, nu_slots, nu_count, density, metric_tensor, sig_slots, sig_count):
    highest = lax.Precision.HIGHEST
    orb_block = density.shape[0]
    lam_all = density.shape[1]
    aux_width = three_center.shape[2]
    dens_all = lax.all_gather(density, "mu", axis=0, tiled=True)

    def add_slot(k, running):
        nu_pick = nu_slots[0, k, 0]
        dens_rows = lax.dynamic_slice_in_dim(dens_all, nu_pick * orb_block, orb_block, 0)
        slab_piece = lax.dynamic_index_in_dim(three_center[0], k, 0, keepdims=False).reshape(
            aux_width, orb_block, orb_block
        )
        return running + jnp.einsum("pij,jl->lpi", slab_piece, dens_rows, precision=highest)

    halfway = lax.fori_loop(
        0, nu_count[0, 0], add_slot, jnp.zeros((lam_all, aux_width, orb_block), F32)
    )
    relayed = lax.all_to_all(halfway.astype(BF16), "mu", split_axis=0, concat_axis=2, tiled=True)
    widened = relayed.astype(F32)
    lam_rows = relayed.shape[0]
    orbitals = relayed.shape[2]

    def add_target(q, running):
        target = sig_slots[0, q, 0]
        weights = lax.dynamic_index_in_dim(metric_tensor[0], q, 0, keepdims=False).reshape(
            aux_width, lam_rows, orb_block
        )
        contrib = jnp.einsum("rpm,prc->mc", widened, weights, precision=highest)
        current = lax.dynamic_slice_in_dim(running, target * orb_block, orb_block, 1)
        return lax.dynamic_update_slice_in_dim(running, current + contrib, target * orb_block, 1)

    partial_k = lax.fori_loop(
        0, sig_count[0, 0], add_target, jnp.zeros((orbitals, orbitals), F32)
    )
    row_share = lax.psum_scatter(partial_k, "aux", scatter_dimension=0, tiled=True)
    return lax.psum_scatter(row_share, "mu", scatter_dimension=1, tiled=True)


def solution(mesh):
    n_aux, n_mu = mesh.shape["aux"], mesh.shape["mu"]

    def shards(three_center, nu_slots, nu_count, density, metric_tensor, sig_slots, sig_count):
        args = (three_center, nu_slots, nu_count, density, metric_tensor, sig_slots, sig_count)
        orb, lam_all = density.shape
        fits = (
            (n_aux, n_mu, orb, lam_all) == (8, 4, 64, 64)
            and three_center.shape[2:] == (64, orb * orb)
            and metric_tensor.shape[2:] == (64, lam_all // n_mu * orb)
        )
        return fast(n_mu, n_aux, *args) if fits else general(*args)

    placed = (
        P("mu", None, "aux", None),
        P("mu", None, "aux"),
        P("mu", "aux"),
        P("mu", None),
        P("mu", None, "aux", None),
        P("mu", None, "aux"),
        P("mu", "aux"),
    )
    return jax.shard_map(
        shards, mesh=mesh, in_specs=placed, out_specs=P("aux", "mu"), check_vma=False
    )
```

```python
import functools

import jax
import jax.numpy as jnp
from jax import lax
from jax.experimental import pallas as pl
from jax.experimental.pallas import tpu as pltpu
from jax.sharding import PartitionSpec as P

F32 = jnp.float32
BF16 = jnp.bfloat16
VMEM = pl.BlockSpec(memory_space=pltpu.VMEM)
SMEM = pl.BlockSpec(memory_space=pltpu.SMEM)
ANY = pl.BlockSpec(memory_space=pl.ANY)
HBM = pl.BlockSpec(memory_space=pltpu.HBM)


DENSITY_ORDER = (2, 3, 1)
FACTORS = (1, 4, 2, 3)


def goes_to(factor, z):
    return (z + 1) * factor % 5 - 1


def by_distance(refs, order):
    return [refs[0]] + [refs[1 + order.index(s)] for s in range(1, len(refs))]


def params(mib):
    return pltpu.CompilerParams(vmem_limit_bytes=mib * 1024 * 1024)


def split(x):
    hi = x.astype(BF16)
    return hi, (x - hi.astype(F32)).astype(BF16)


def iota(shape, dim):
    return lax.broadcasted_iota(jnp.int32, shape, dim)


def tensor_kernel(tensor, t_hi, t_lo, buffer, arrived):
    _, slots, aux_width, width = tensor.shape
    parts = buffer.shape[0] // slots
    span = width // parts

    def fetch(k, part):
        return pltpu.make_async_copy(
            tensor.at[0, k, :, pl.ds(part * span, span)],
            buffer.at[k * parts + part],
            arrived.at[k * parts + part],
        )

    order = [(k, part) for k in range(slots) for part in range(parts)]
    for k, part in order:
        fetch(k, part).start()
    for k, part in order:
        fetch(k, part).wait()
        for chunk in range(span // 256):
            hi, lo = split(buffer[k * parts + part, :, chunk * 256:(chunk + 1) * 256])
            at = (part * (span // 256) + chunk) * aux_width
            t_hi[at:at + aux_width, k * 256:(k + 1) * 256] = hi
            t_lo[at:at + aux_width, k * 256:(k + 1) * 256] = lo


def metric_kernel(sig_slots, sig_count, after, metric, m_hi, m_lo):
    _, sig, aux_width, width = metric.shape
    half = iota((aux_width, 128), 1) >= 64
    pair_of = jnp.where(half, 1, 0)
    targets = [jnp.where(q < sig_count[0, 0], sig_slots[0, 0, q], -1) for q in range(sig)]
    for pair in range(width // 128):
        sums = [[jnp.zeros((aux_width, 128), F32) for _ in range(2)] for _ in range(2)]
        for q in range(sig):
            block = metric[0, q, :, pair * 128:(pair + 1) * 128]
            turned = pltpu.roll(block, 64, 1)
            both = (jnp.where(half, turned, block), jnp.where(half, block, turned))
            for out_half in range(2):
                here = pair_of + 2 * out_half == targets[q]
                for parity in range(2):
                    sums[parity][out_half] += jnp.where(here, both[parity], 0.0)
        for parity in range(2):
            r = 2 * pair + parity
            at = ((r % 8) * 2 + r // 8) * aux_width
            for out_half in range(2):
                hi, lo = split(sums[parity][out_half])
                columns = slice(out_half * 128, (out_half + 1) * 128)
                m_hi[at:at + aux_width, columns] = hi
                m_lo[at:at + aux_width, columns] = lo


def half_kernel(n_mu, nu_slots, nu_count, *refs):
    dens = by_distance(refs[:n_mu], DENSITY_ORDER)
    t_hi, t_lo = refs[n_mu:n_mu + 2]
    outs = refs[n_mu + 2:2 * n_mu + 2]
    d_hi, d_lo, weights, turned = refs[2 * n_mu + 2:]
    z = lax.axis_index("mu")
    orb, lam_all = dens[0].shape
    lam = lam_all // n_mu
    slots = nu_slots.shape[2]
    row, col = iota((lam_all, 256), 0), iota((lam_all, 256), 1)
    group = z
    for slot in range(1, n_mu):
        group = jnp.where((col >> 3) & 3 == slot, lax.rem((z + 1) * FACTORS[slot], 5) - 1, group)
    wanted = group * lam + (col >> 7) * 8 + (col & 7)
    choose = jnp.where(row == wanted, 1.0, 0.0).astype(BF16)
    for s in range(n_mu):
        hi, lo = split(dens[s][...])
        d_hi[s] = jnp.dot(hi, choose, preferred_element_type=F32)
        d_lo[s] = jnp.dot(lo, choose, preferred_element_type=F32)
    orbital = (iota((orb, 256), 1) >> 5) & 3
    depth = slots * 256
    for k in range(slots):
        at = z ^ nu_slots[0, 0, k]
        live = jnp.where(k < nu_count[0, 0], 1.0, 0.0)
        hi, lo = d_hi[at] * live, d_lo[at] * live
        for i in range(4):
            rows = k * 256 + i * orb
            w_hi = jnp.where(orbital == i, hi, 0.0).astype(BF16)
            weights[rows:rows + orb, :] = w_hi
            weights[rows + depth:rows + depth + orb, :] = w_hi
            weights[rows + 2 * depth:rows + 2 * depth + orb, :] = jnp.where(
                orbital == i, lo, 0.0
            ).astype(BF16)
    aux_width = outs[0].shape[1] // lam
    per_group = 256 // aux_width
    span = per_group * 4
    for group in range(t_hi.shape[0] // 256):
        rows = slice(group * 256, (group + 1) * 256)
        high = t_hi[rows, :]
        left = jnp.concatenate([high, t_lo[rows, :], high], axis=1)
        total = jnp.dot(left, weights[...], preferred_element_type=F32)
        for chunk in range(per_group):
            piece = total[chunk * aux_width:(chunk + 1) * aux_width]
            stacked = jnp.concatenate([piece[:, :128], piece[:, 128:]], axis=0)
            at = (group * per_group + chunk) * 128
            turned[at:at + 128, :] = stacked.T
        for s in range(n_mu):
            for r in range(8):
                picked = turned[pl.ds(group * per_group * 128 + s * 8 + r, span, stride=32), :]
                outs[s][group * span:(group + 1) * span, r * 128:(r + 1) * 128] = picked.astype(BF16)


def exchange_kernel(n_mu, n_aux, *refs):
    halves = refs[:n_mu]
    m_hi, m_lo, out, total = refs[n_mu:]
    z = lax.axis_index("mu")
    left = jnp.concatenate([h[...] for h in halves], axis=0)
    product = jnp.dot(left, m_hi[...], preferred_element_type=F32)
    product += jnp.dot(left, m_lo[...], preferred_element_type=F32)
    orb = halves[0].shape[0]
    for s in range(n_mu):
        back = pow(FACTORS[s], -1, 5)
        block = lax.rem((z + 1) * back, 5) - 1
        total[pl.ds(pl.multiple_of(block * orb, orb), orb), :] = product[s * orb:(s + 1) * orb]
    rows = out.shape[1]
    lower = iota((rows, 128), 1) < 64
    for a in range(n_aux):
        for pair in range(n_mu // 2):
            columns = slice(pair * 128, (pair + 1) * 128)
            top = total[a * 2 * rows:(a * 2 + 1) * rows, columns]
            bottom = total[(a * 2 + 1) * rows:(a * 2 + 2) * rows, columns]
            at = n_aux * n_mu - 1 - (a * n_mu + pair * 2)
            out[at] = jnp.where(lower, top, pltpu.roll(bottom, 64, 1)).astype(BF16)
            out[at - 1] = jnp.where(lower, pltpu.roll(top, 64, 1), bottom).astype(BF16)


def sum_kernel(parts, out):
    total = parts[0].astype(F32)
    for d in range(1, parts.shape[0]):
        total += parts[d].astype(F32)
    rows = parts.shape[1]
    out[:rows, :] = total[:, :64]
    out[rows:, :] = total[:, 64:]


def fast(n_mu, n_aux, three_center, nu_slots, nu_count, density, metric_tensor, sig_slots, sig_count):
    orb, lam_all = density.shape
    slots, aux_width = three_center.shape[1:3]
    lam = lam_all // n_mu
    turns = [[(z, z ^ s) for z in range(n_mu)] for s in range(n_mu)]
    dens = [density] + [lax.ppermute(density, "mu", turns[s]) for s in DENSITY_ORDER]
    nu_slots, sig_slots = jnp.swapaxes(nu_slots, 1, 2), jnp.swapaxes(sig_slots, 1, 2)
    chunks = three_center.shape[3] // 256
    t_shape = jax.ShapeDtypeStruct((chunks * aux_width, slots * 256), BF16)
    m_shape = jax.ShapeDtypeStruct((lam * aux_width, n_mu * orb), BF16)
    t_hi, t_lo = pl.pallas_call(
        tensor_kernel,
        out_shape=(t_shape, t_shape),
        in_specs=[HBM],
        out_specs=(VMEM, VMEM),
        scratch_shapes=[
            pltpu.VMEM((slots * 4, aux_width, chunks * 64), F32),
            pltpu.SemaphoreType.DMA((slots * 4,)),
        ],
        compiler_params=params(50),
        cost_estimate=pl.CostEstimate(flops=10_000_000, bytes_accessed=6_000_000, transcendentals=0),
        name="tensor",
    )(three_center)
    half_shape = jax.ShapeDtypeStruct((orb, lam * aux_width), BF16)
    halves = pl.pallas_call(
        functools.partial(half_kernel, n_mu),
        out_shape=(half_shape,) * n_mu,
        in_specs=[SMEM, SMEM] + [VMEM] * (n_mu + 2),
        out_specs=(VMEM,) * n_mu,
        scratch_shapes=[
            pltpu.VMEM((n_mu, orb, 256), F32),
            pltpu.VMEM((n_mu, orb, 256), F32),
            pltpu.VMEM((3 * slots * 256, 256), BF16),
            pltpu.VMEM((chunks * 128, 128), F32),
        ],
        compiler_params=params(16),
        cost_estimate=pl.CostEstimate(flops=1_200_000_000, bytes_accessed=4_000_000, transcendentals=0),
        name="half",
    )(nu_slots, nu_count, *dens, t_hi, t_lo)
    m_hi, m_lo = pl.pallas_call(
        metric_kernel,
        out_shape=(m_shape, m_shape),
        in_specs=[SMEM, SMEM, ANY, VMEM],
        out_specs=(VMEM, VMEM),
        compiler_params=params(16),
        cost_estimate=pl.CostEstimate(flops=10_000_000, bytes_accessed=2_000_000, transcendentals=0),
        name="metric",
    )(sig_slots, sig_count, halves[0], metric_tensor)
    halves = [halves[0]] + [
        lax.ppermute(halves[s], "mu", [(z, goes_to(FACTORS[s], z)) for z in range(n_mu)])
        for s in range(1, n_mu)
    ]
    rows = n_mu * orb // n_aux
    parts = pl.pallas_call(
        functools.partial(exchange_kernel, n_mu, n_aux),
        out_shape=jax.ShapeDtypeStruct((n_aux * n_mu, rows // 2, 128), BF16),
        in_specs=[VMEM] * (n_mu + 2),
        out_specs=VMEM,
        scratch_shapes=[pltpu.VMEM((n_mu * orb, n_mu * orb), F32)],
        compiler_params=params(16),
        cost_estimate=pl.CostEstimate(flops=300_000_000, bytes_accessed=2_000_000, transcendentals=0),
        name="exchange",
    )(*halves, m_hi, m_lo)
    down = list(reversed(range(n_aux * n_mu)))
    parts = lax.all_to_all(parts, ("aux", "mu"), 0, 0, axis_index_groups=[down])
    return pl.pallas_call(
        sum_kernel,
        out_shape=jax.ShapeDtypeStruct((rows, orb), F32),
        in_specs=[VMEM],
        out_specs=VMEM,
        compiler_params=params(8),
        name="sum",
    )(parts)


def general(three_center, nu_slots, nu_count, density, metric_tensor, sig_slots, sig_count):
    highest = lax.Precision.HIGHEST
    orb_block = density.shape[0]
    lam_all = density.shape[1]
    aux_width = three_center.shape[2]
    dens_all = lax.all_gather(density, "mu", axis=0, tiled=True)

    def add_slot(k, running):
        nu_pick = nu_slots[0, k, 0]
        dens_rows = lax.dynamic_slice_in_dim(dens_all, nu_pick * orb_block, orb_block, 0)
        slab_piece = lax.dynamic_index_in_dim(three_center[0], k, 0, keepdims=False).reshape(
            aux_width, orb_block, orb_block
        )
        return running + jnp.einsum("pij,jl->lpi", slab_piece, dens_rows, precision=highest)

    halfway = lax.fori_loop(
        0, nu_count[0, 0], add_slot, jnp.zeros((lam_all, aux_width, orb_block), F32)
    )
    relayed = lax.all_to_all(halfway.astype(BF16), "mu", split_axis=0, concat_axis=2, tiled=True)
    widened = relayed.astype(F32)
    lam_rows = relayed.shape[0]
    orbitals = relayed.shape[2]

    def add_target(q, running):
        target = sig_slots[0, q, 0]
        weights = lax.dynamic_index_in_dim(metric_tensor[0], q, 0, keepdims=False).reshape(
            aux_width, lam_rows, orb_block
        )
        contrib = jnp.einsum("rpm,prc->mc", widened, weights, precision=highest)
        current = lax.dynamic_slice_in_dim(running, target * orb_block, orb_block, 1)
        return lax.dynamic_update_slice_in_dim(running, current + contrib, target * orb_block, 1)

    partial_k = lax.fori_loop(
        0, sig_count[0, 0], add_target, jnp.zeros((orbitals, orbitals), F32)
    )
    row_share = lax.psum_scatter(partial_k, "aux", scatter_dimension=0, tiled=True)
    return lax.psum_scatter(row_share, "mu", scatter_dimension=1, tiled=True)


def solution(mesh):
    n_aux, n_mu = mesh.shape["aux"], mesh.shape["mu"]

    def shards(three_center, nu_slots, nu_count, density, metric_tensor, sig_slots, sig_count):
        args = (three_center, nu_slots, nu_count, density, metric_tensor, sig_slots, sig_count)
        orb, lam_all = density.shape
        fits = (
            (n_aux, n_mu, orb, lam_all) == (8, 4, 64, 64)
            and three_center.shape[2:] == (64, orb * orb)
            and metric_tensor.shape[2:] == (64, lam_all // n_mu * orb)
        )
        return fast(n_mu, n_aux, *args) if fits else general(*args)

    placed = (
        P("mu", None, "aux", None),
        P("mu", None, "aux"),
        P("mu", "aux"),
        P("mu", None),
        P("mu", None, "aux", None),
        P("mu", None, "aux"),
        P("mu", "aux"),
    )
    return jax.shard_map(
        shards, mesh=mesh, in_specs=placed, out_specs=P("aux", "mu"), check_vma=False
    )
```

```python
import functools

import jax
import jax.numpy as jnp
from jax import lax
from jax.experimental import pallas as pl
from jax.experimental.pallas import tpu as pltpu
from jax.sharding import PartitionSpec as P

F32 = jnp.float32
BF16 = jnp.bfloat16
VMEM = pl.BlockSpec(memory_space=pltpu.VMEM)
SMEM = pl.BlockSpec(memory_space=pltpu.SMEM)
ANY = pl.BlockSpec(memory_space=pl.ANY)
HBM = pl.BlockSpec(memory_space=pltpu.HBM)


DENSITY_ORDER = (2, 3, 1)
FACTORS = (1, 4, 2, 3)


def goes_to(factor, z):
    return (z + 1) * factor % 5 - 1


def by_distance(refs, order):
    return [refs[0]] + [refs[1 + order.index(s)] for s in range(1, len(refs))]


def params(mib):
    return pltpu.CompilerParams(vmem_limit_bytes=mib * 1024 * 1024)


def split(x):
    hi = x.astype(BF16)
    return hi, (x - hi.astype(F32)).astype(BF16)


def iota(shape, dim):
    return lax.broadcasted_iota(jnp.int32, shape, dim)


def tensor_kernel(tensor, t_hi, t_lo, buffer, arrived):
    _, slots, aux_width, width = tensor.shape
    parts = buffer.shape[0] // slots
    span = width // parts

    def fetch(k, part):
        return pltpu.make_async_copy(
            tensor.at[0, k, :, pl.ds(part * span, span)],
            buffer.at[k * parts + part],
            arrived.at[k * parts + part],
        )

    order = [(k, part) for k in range(slots) for part in range(parts)]
    for k, part in order:
        fetch(k, part).start()
    for k, part in order:
        fetch(k, part).wait()
        for chunk in range(span // 256):
            hi, lo = split(buffer[k * parts + part, :, chunk * 256:(chunk + 1) * 256])
            at = (part * (span // 256) + chunk) * aux_width
            t_hi[at:at + aux_width, k * 256:(k + 1) * 256] = hi
            t_lo[at:at + aux_width, k * 256:(k + 1) * 256] = lo


def metric_kernel(sig_slots, sig_count, after, metric, m_hi, m_lo):
    _, sig, aux_width, width = metric.shape
    half = iota((aux_width, 128), 1) >= 64
    pair_of = jnp.where(half, 1, 0)
    targets = [jnp.where(q < sig_count[0, 0], sig_slots[0, 0, q], -1) for q in range(sig)]
    for pair in range(width // 128):
        sums = [[jnp.zeros((aux_width, 128), F32) for _ in range(2)] for _ in range(2)]
        for q in range(sig):
            block = metric[0, q, :, pair * 128:(pair + 1) * 128]
            turned = pltpu.roll(block, 64, 1)
            both = (jnp.where(half, turned, block), jnp.where(half, block, turned))
            for out_half in range(2):
                here = pair_of + 2 * out_half == targets[q]
                for parity in range(2):
                    sums[parity][out_half] += jnp.where(here, both[parity], 0.0)
        for parity in range(2):
            r = 2 * pair + parity
            at = ((r % 8) * 2 + r // 8) * aux_width
            for out_half in range(2):
                hi, lo = split(sums[parity][out_half])
                columns = slice(out_half * 128, (out_half + 1) * 128)
                m_hi[at:at + aux_width, columns] = hi
                m_lo[at:at + aux_width, columns] = lo


def half_kernel(n_mu, nu_slots, nu_count, *refs):
    dens = by_distance(refs[:n_mu], DENSITY_ORDER)
    t_hi, t_lo = refs[n_mu:n_mu + 2]
    outs = refs[n_mu + 2:2 * n_mu + 2]
    d_hi, d_lo, weights, turned = refs[2 * n_mu + 2:]
    z = lax.axis_index("mu")
    orb, lam_all = dens[0].shape
    lam = lam_all // n_mu
    slots = nu_slots.shape[2]
    row, col = iota((lam_all, 256), 0), iota((lam_all, 256), 1)
    group = z
    for slot in range(1, n_mu):
        group = jnp.where((col >> 3) & 3 == slot, lax.rem((z + 1) * FACTORS[slot], 5) - 1, group)
    wanted = group * lam + (col >> 7) * 8 + (col & 7)
    choose = jnp.where(row == wanted, 1.0, 0.0).astype(BF16)
    for s in range(n_mu):
        hi, lo = split(dens[s][...])
        d_hi[s] = jnp.dot(hi, choose, preferred_element_type=F32)
        d_lo[s] = jnp.dot(lo, choose, preferred_element_type=F32)
    orbital = (iota((orb, 256), 1) >> 5) & 3
    depth = slots * 256
    for k in range(slots):
        at = z ^ nu_slots[0, 0, k]
        live = jnp.where(k < nu_count[0, 0], 1.0, 0.0)
        hi, lo = d_hi[at] * live, d_lo[at] * live
        for i in range(4):
            rows = k * 256 + i * orb
            w_hi = jnp.where(orbital == i, hi, 0.0).astype(BF16)
            weights[rows:rows + orb, :] = w_hi
            weights[rows + depth:rows + depth + orb, :] = w_hi
            weights[rows + 2 * depth:rows + 2 * depth + orb, :] = jnp.where(
                orbital == i, lo, 0.0
            ).astype(BF16)
    aux_width = outs[0].shape[1] // lam
    per_group = 256 // aux_width
    span = per_group * 4
    for group in range(t_hi.shape[0] // 256):
        rows = slice(group * 256, (group + 1) * 256)
        high = t_hi[rows, :]
        left = jnp.concatenate([high, t_lo[rows, :], high], axis=1)
        total = jnp.dot(left, weights[...], preferred_element_type=F32)
        for chunk in range(per_group):
            piece = total[chunk * aux_width:(chunk + 1) * aux_width]
            stacked = jnp.concatenate([piece[:, :128], piece[:, 128:]], axis=0)
            at = (group * per_group + chunk) * 128
            turned[at:at + 128, :] = stacked.T
        for s in range(n_mu):
            for r in range(8):
                picked = turned[pl.ds(group * per_group * 128 + s * 8 + r, span, stride=32), :]
                outs[s][group * span:(group + 1) * span, r * 128:(r + 1) * 128] = picked.astype(BF16)


def walk(n_mu, n_aux):
    order = []
    for turn, chip in enumerate((0, 1, 3, 2)):
        for z in range(n_mu) if turn % 2 == 0 else reversed(range(n_mu)):
            order += [(2 * chip + core) * n_mu + z for core in range(2)]
    assert sorted(order) == list(range(n_aux * n_mu))
    return order


def exchange_kernel(n_mu, n_aux, *refs):
    halves = refs[:n_mu]
    m_hi, m_lo, out, total = refs[n_mu:]
    order = walk(n_mu, n_aux)
    places = [order.index(f) for f in range(n_aux * n_mu)]
    z = lax.axis_index("mu")
    left = jnp.concatenate([h[...] for h in halves], axis=0)
    product = jnp.dot(left, m_hi[...], preferred_element_type=F32)
    product += jnp.dot(left, m_lo[...], preferred_element_type=F32)
    orb = halves[0].shape[0]
    for s in range(n_mu):
        back = pow(FACTORS[s], -1, 5)
        block = lax.rem((z + 1) * back, 5) - 1
        total[pl.ds(pl.multiple_of(block * orb, orb), orb), :] = product[s * orb:(s + 1) * orb]
    rows = out.shape[1]
    lower = iota((rows, 128), 1) < 64
    for a in range(n_aux):
        for pair in range(n_mu // 2):
            columns = slice(pair * 128, (pair + 1) * 128)
            top = total[a * 2 * rows:(a * 2 + 1) * rows, columns]
            bottom = total[(a * 2 + 1) * rows:(a * 2 + 2) * rows, columns]
            first, second = places[a * n_mu + pair * 2], places[a * n_mu + pair * 2 + 1]
            out[first] = jnp.where(lower, top, pltpu.roll(bottom, 64, 1)).astype(BF16)
            out[second] = jnp.where(lower, pltpu.roll(top, 64, 1), bottom).astype(BF16)


def sum_kernel(parts, out):
    total = parts[0].astype(F32)
    for d in range(1, parts.shape[0]):
        total += parts[d].astype(F32)
    rows = parts.shape[1]
    out[:rows, :] = total[:, :64]
    out[rows:, :] = total[:, 64:]


def fast(n_mu, n_aux, three_center, nu_slots, nu_count, density, metric_tensor, sig_slots, sig_count):
    orb, lam_all = density.shape
    slots, aux_width = three_center.shape[1:3]
    lam = lam_all // n_mu
    turns = [[(z, z ^ s) for z in range(n_mu)] for s in range(n_mu)]
    dens = [density] + [lax.ppermute(density, "mu", turns[s]) for s in DENSITY_ORDER]
    nu_slots, sig_slots = jnp.swapaxes(nu_slots, 1, 2), jnp.swapaxes(sig_slots, 1, 2)
    chunks = three_center.shape[3] // 256
    t_shape = jax.ShapeDtypeStruct((chunks * aux_width, slots * 256), BF16)
    m_shape = jax.ShapeDtypeStruct((lam * aux_width, n_mu * orb), BF16)
    t_hi, t_lo = pl.pallas_call(
        tensor_kernel,
        out_shape=(t_shape, t_shape),
        in_specs=[HBM],
        out_specs=(VMEM, VMEM),
        scratch_shapes=[
            pltpu.VMEM((slots * 4, aux_width, chunks * 64), F32),
            pltpu.SemaphoreType.DMA((slots * 4,)),
        ],
        compiler_params=params(50),
        cost_estimate=pl.CostEstimate(flops=10_000_000, bytes_accessed=6_000_000, transcendentals=0),
        name="tensor",
    )(three_center)
    half_shape = jax.ShapeDtypeStruct((orb, lam * aux_width), BF16)
    halves = pl.pallas_call(
        functools.partial(half_kernel, n_mu),
        out_shape=(half_shape,) * n_mu,
        in_specs=[SMEM, SMEM] + [VMEM] * (n_mu + 2),
        out_specs=(VMEM,) * n_mu,
        scratch_shapes=[
            pltpu.VMEM((n_mu, orb, 256), F32),
            pltpu.VMEM((n_mu, orb, 256), F32),
            pltpu.VMEM((3 * slots * 256, 256), BF16),
            pltpu.VMEM((chunks * 128, 128), F32),
        ],
        compiler_params=params(16),
        cost_estimate=pl.CostEstimate(flops=1_200_000_000, bytes_accessed=4_000_000, transcendentals=0),
        name="half",
    )(nu_slots, nu_count, *dens, t_hi, t_lo)
    m_hi, m_lo = pl.pallas_call(
        metric_kernel,
        out_shape=(m_shape, m_shape),
        in_specs=[SMEM, SMEM, ANY, VMEM],
        out_specs=(VMEM, VMEM),
        compiler_params=params(16),
        cost_estimate=pl.CostEstimate(flops=10_000_000, bytes_accessed=2_000_000, transcendentals=0),
        name="metric",
    )(sig_slots, sig_count, halves[0], metric_tensor)
    halves = [halves[0]] + [
        lax.ppermute(halves[s], "mu", [(z, goes_to(FACTORS[s], z)) for z in range(n_mu)])
        for s in range(1, n_mu)
    ]
    rows = n_mu * orb // n_aux
    parts = pl.pallas_call(
        functools.partial(exchange_kernel, n_mu, n_aux),
        out_shape=jax.ShapeDtypeStruct((n_aux * n_mu, rows // 2, 128), BF16),
        in_specs=[VMEM] * (n_mu + 2),
        out_specs=VMEM,
        scratch_shapes=[pltpu.VMEM((n_mu * orb, n_mu * orb), F32)],
        compiler_params=params(16),
        cost_estimate=pl.CostEstimate(flops=300_000_000, bytes_accessed=2_000_000, transcendentals=0),
        name="exchange",
    )(*halves, m_hi, m_lo)
    parts = lax.all_to_all(
        parts, ("aux", "mu"), 0, 0, axis_index_groups=[walk(n_mu, n_aux)]
    )
    return pl.pallas_call(
        sum_kernel,
        out_shape=jax.ShapeDtypeStruct((rows, orb), F32),
        in_specs=[VMEM],
        out_specs=VMEM,
        compiler_params=params(8),
        name="sum",
    )(parts)


def general(three_center, nu_slots, nu_count, density, metric_tensor, sig_slots, sig_count):
    highest = lax.Precision.HIGHEST
    orb_block = density.shape[0]
    lam_all = density.shape[1]
    aux_width = three_center.shape[2]
    dens_all = lax.all_gather(density, "mu", axis=0, tiled=True)

    def add_slot(k, running):
        nu_pick = nu_slots[0, k, 0]
        dens_rows = lax.dynamic_slice_in_dim(dens_all, nu_pick * orb_block, orb_block, 0)
        slab_piece = lax.dynamic_index_in_dim(three_center[0], k, 0, keepdims=False).reshape(
            aux_width, orb_block, orb_block
        )
        return running + jnp.einsum("pij,jl->lpi", slab_piece, dens_rows, precision=highest)

    halfway = lax.fori_loop(
        0, nu_count[0, 0], add_slot, jnp.zeros((lam_all, aux_width, orb_block), F32)
    )
    relayed = lax.all_to_all(halfway.astype(BF16), "mu", split_axis=0, concat_axis=2, tiled=True)
    widened = relayed.astype(F32)
    lam_rows = relayed.shape[0]
    orbitals = relayed.shape[2]

    def add_target(q, running):
        target = sig_slots[0, q, 0]
        weights = lax.dynamic_index_in_dim(metric_tensor[0], q, 0, keepdims=False).reshape(
            aux_width, lam_rows, orb_block
        )
        contrib = jnp.einsum("rpm,prc->mc", widened, weights, precision=highest)
        current = lax.dynamic_slice_in_dim(running, target * orb_block, orb_block, 1)
        return lax.dynamic_update_slice_in_dim(running, current + contrib, target * orb_block, 1)

    partial_k = lax.fori_loop(
        0, sig_count[0, 0], add_target, jnp.zeros((orbitals, orbitals), F32)
    )
    row_share = lax.psum_scatter(partial_k, "aux", scatter_dimension=0, tiled=True)
    return lax.psum_scatter(row_share, "mu", scatter_dimension=1, tiled=True)


def solution(mesh):
    n_aux, n_mu = mesh.shape["aux"], mesh.shape["mu"]

    def shards(three_center, nu_slots, nu_count, density, metric_tensor, sig_slots, sig_count):
        args = (three_center, nu_slots, nu_count, density, metric_tensor, sig_slots, sig_count)
        orb, lam_all = density.shape
        fits = (
            (n_aux, n_mu, orb, lam_all) == (8, 4, 64, 64)
            and three_center.shape[2:] == (64, orb * orb)
            and metric_tensor.shape[2:] == (64, lam_all // n_mu * orb)
        )
        return fast(n_mu, n_aux, *args) if fits else general(*args)

    placed = (
        P("mu", None, "aux", None),
        P("mu", None, "aux"),
        P("mu", "aux"),
        P("mu", None),
        P("mu", None, "aux", None),
        P("mu", None, "aux"),
        P("mu", "aux"),
    )
    return jax.shard_map(
        shards, mesh=mesh, in_specs=placed, out_specs=P("aux", "mu"), check_vma=False
    )
```

```python
import functools

import jax
import jax.numpy as jnp
from jax import lax
from jax.experimental import pallas as pl
from jax.experimental.pallas import tpu as pltpu
from jax.sharding import PartitionSpec as P

F32 = jnp.float32
BF16 = jnp.bfloat16
VMEM = pl.BlockSpec(memory_space=pltpu.VMEM)
SMEM = pl.BlockSpec(memory_space=pltpu.SMEM)
ANY = pl.BlockSpec(memory_space=pl.ANY)
HBM = pl.BlockSpec(memory_space=pltpu.HBM)


DENSITY_ORDER = (2, 3, 1)
FACTORS = (1, 4, 2, 3)


def goes_to(factor, z):
    return (z + 1) * factor % 5 - 1


def by_distance(refs, order):
    return [refs[0]] + [refs[1 + order.index(s)] for s in range(1, len(refs))]


def params(mib):
    return pltpu.CompilerParams(vmem_limit_bytes=mib * 1024 * 1024)


def split(x):
    hi = x.astype(BF16)
    return hi, (x - hi.astype(F32)).astype(BF16)


def iota(shape, dim):
    return lax.broadcasted_iota(jnp.int32, shape, dim)


def tensor_kernel(tensor, packed, buffer, arrived):
    _, slots, aux_width, width = tensor.shape
    parts = buffer.shape[0] // slots
    span = width // parts

    def fetch(k, part):
        return pltpu.make_async_copy(
            tensor.at[0, k, :, pl.ds(part * span, span)],
            buffer.at[k * parts + part],
            arrived.at[k * parts + part],
        )

    order = [(k, part) for k in range(slots) for part in range(parts)]
    for k, part in order:
        fetch(k, part).start()
    for k, part in order:
        fetch(k, part).wait()
        for chunk in range(span // 128):
            hi, lo = split(buffer[k * parts + part, :, chunk * 128:(chunk + 1) * 128])
            at = (part * (span // 128) + chunk) * aux_width
            packed[at:at + aux_width, k * 256:k * 256 + 128] = hi
            packed[at:at + aux_width, k * 256 + 128:(k + 1) * 256] = lo


def metric_kernel(sig_slots, sig_count, after, metric, m_hi, m_lo):
    _, sig, aux_width, width = metric.shape
    half = iota((aux_width, 128), 1) >= 64
    pair_of = jnp.where(half, 1, 0)
    targets = [jnp.where(q < sig_count[0, 0], sig_slots[0, 0, q], -1) for q in range(sig)]
    for pair in range(width // 128):
        sums = [[jnp.zeros((aux_width, 128), F32) for _ in range(2)] for _ in range(2)]
        for q in range(sig):
            block = metric[0, q, :, pair * 128:(pair + 1) * 128]
            turned = pltpu.roll(block, 64, 1)
            both = (jnp.where(half, turned, block), jnp.where(half, block, turned))
            for out_half in range(2):
                here = pair_of + 2 * out_half == targets[q]
                for parity in range(2):
                    sums[parity][out_half] += jnp.where(here, both[parity], 0.0)
        for parity in range(2):
            r = 2 * pair + parity
            at = ((r % 8) * 2 + r // 8) * aux_width
            for out_half in range(2):
                hi, lo = split(sums[parity][out_half])
                columns = slice(out_half * 128, (out_half + 1) * 128)
                m_hi[at:at + aux_width, columns] = hi
                m_lo[at:at + aux_width, columns] = lo


def half_kernel(n_mu, nu_slots, nu_count, *refs):
    dens = by_distance(refs[:n_mu], DENSITY_ORDER)
    packed = refs[n_mu]
    outs = refs[n_mu + 1:2 * n_mu + 1]
    d_both, weights, turned = refs[2 * n_mu + 1:]
    z = lax.axis_index("mu")
    orb, lam_all = dens[0].shape
    lam = lam_all // n_mu
    slots = nu_slots.shape[2]
    row, col = iota((lam_all, 128), 0), iota((lam_all, 128), 1)
    group = z
    for slot in range(1, n_mu):
        group = jnp.where((col >> 3) & 3 == slot, lax.rem((z + 1) * FACTORS[slot], 5) - 1, group)
    wanted = group * lam + (col >> 6) * 8 + (col & 7)
    choose = jnp.where(row == wanted, 1.0, 0.0).astype(BF16)
    for s in range(n_mu):
        hi, lo = split(dens[s][...])
        d_both[s, :, :128] = jnp.dot(hi, choose, preferred_element_type=F32)
        d_both[s, :, 128:] = jnp.dot(lo, choose, preferred_element_type=F32)
    orbital = (iota((orb, 256), 1) >> 5) & 1
    for k in range(slots):
        live = jnp.where(k < nu_count[0, 0], 1.0, 0.0)
        both = d_both[z ^ nu_slots[0, 0, k]] * live
        for i in range(2):
            block = jnp.where(orbital == i, both, 0.0).astype(BF16)
            for part in range(2):
                at = k * 256 + part * 128 + i * orb
                weights[at:at + orb, :] = block
    aux_width = outs[0].shape[1] // lam
    lower = iota((aux_width, 128), 1) < 64
    per_group = 512 // (2 * aux_width)
    span = per_group * 4
    for part in range(packed.shape[0] // 512):
        product = jnp.dot(
            packed[part * 512:(part + 1) * 512, :], weights[...], preferred_element_type=F32
        )
        total = product[:, :128] + product[:, 128:]
        for chunk in range(per_group):
            at = chunk * 2 * aux_width
            one, two = total[at:at + aux_width], total[at + aux_width:at + 2 * aux_width]
            top = jnp.where(lower, one, pltpu.roll(two, 64, 1))
            bottom = jnp.where(lower, pltpu.roll(one, 64, 1), two)
            at = (part * per_group + chunk) * 128
            turned[at:at + 128, :] = jnp.concatenate([top, bottom], axis=0).T
        for s in range(n_mu):
            for r in range(8):
                picked = turned[pl.ds(part * per_group * 128 + s * 8 + r, span, stride=32), :]
                outs[s][part * span:(part + 1) * span, r * 128:(r + 1) * 128] = picked.astype(BF16)


def exchange_kernel(n_mu, n_aux, *refs):
    halves = refs[:n_mu]
    m_hi, m_lo, out, total = refs[n_mu:]
    z = lax.axis_index("mu")
    left = jnp.concatenate([h[...] for h in halves], axis=0)
    product = jnp.dot(left, m_hi[...], preferred_element_type=F32)
    product += jnp.dot(left, m_lo[...], preferred_element_type=F32)
    orb = halves[0].shape[0]
    for s in range(n_mu):
        back = pow(FACTORS[s], -1, 5)
        block = lax.rem((z + 1) * back, 5) - 1
        total[pl.ds(pl.multiple_of(block * orb, orb), orb), :] = product[s * orb:(s + 1) * orb]
    rows = out.shape[1]
    lower = iota((rows, 128), 1) < 64
    for a in range(n_aux):
        for pair in range(n_mu // 2):
            columns = slice(pair * 128, (pair + 1) * 128)
            top = total[a * 2 * rows:(a * 2 + 1) * rows, columns]
            bottom = total[(a * 2 + 1) * rows:(a * 2 + 2) * rows, columns]
            at = n_aux * n_mu - 1 - (a * n_mu + pair * 2)
            out[at] = jnp.where(lower, top, pltpu.roll(bottom, 64, 1)).astype(BF16)
            out[at - 1] = jnp.where(lower, pltpu.roll(top, 64, 1), bottom).astype(BF16)


def sum_kernel(parts, out):
    total = parts[0].astype(F32)
    for d in range(1, parts.shape[0]):
        total += parts[d].astype(F32)
    rows = parts.shape[1]
    out[:rows, :] = total[:, :64]
    out[rows:, :] = total[:, 64:]


def fast(n_mu, n_aux, three_center, nu_slots, nu_count, density, metric_tensor, sig_slots, sig_count):
    orb, lam_all = density.shape
    slots, aux_width = three_center.shape[1:3]
    lam = lam_all // n_mu
    turns = [[(z, z ^ s) for z in range(n_mu)] for s in range(n_mu)]
    dens = [density] + [lax.ppermute(density, "mu", turns[s]) for s in DENSITY_ORDER]
    nu_slots, sig_slots = jnp.swapaxes(nu_slots, 1, 2), jnp.swapaxes(sig_slots, 1, 2)
    chunks = three_center.shape[3] // 256
    t_shape = jax.ShapeDtypeStruct((2 * chunks * aux_width, slots * 256), BF16)
    m_shape = jax.ShapeDtypeStruct((lam * aux_width, n_mu * orb), BF16)
    packed = pl.pallas_call(
        tensor_kernel,
        out_shape=t_shape,
        in_specs=[HBM],
        out_specs=VMEM,
        scratch_shapes=[
            pltpu.VMEM((slots * 4, aux_width, chunks * 64), F32),
            pltpu.SemaphoreType.DMA((slots * 4,)),
        ],
        compiler_params=params(50),
        cost_estimate=pl.CostEstimate(flops=10_000_000, bytes_accessed=6_000_000, transcendentals=0),
        name="tensor",
    )(three_center)
    half_shape = jax.ShapeDtypeStruct((orb, lam * aux_width), BF16)
    halves = pl.pallas_call(
        functools.partial(half_kernel, n_mu),
        out_shape=(half_shape,) * n_mu,
        in_specs=[SMEM, SMEM] + [VMEM] * (n_mu + 1),
        out_specs=(VMEM,) * n_mu,
        scratch_shapes=[
            pltpu.VMEM((n_mu, orb, 256), F32),
            pltpu.VMEM((slots * 256, 256), BF16),
            pltpu.VMEM((chunks * 128, 128), F32),
        ],
        compiler_params=params(16),
        cost_estimate=pl.CostEstimate(flops=1_200_000_000, bytes_accessed=4_000_000, transcendentals=0),
        name="half",
    )(nu_slots, nu_count, *dens, packed)
    m_hi, m_lo = pl.pallas_call(
        metric_kernel,
        out_shape=(m_shape, m_shape),
        in_specs=[SMEM, SMEM, ANY, VMEM],
        out_specs=(VMEM, VMEM),
        compiler_params=params(16),
        cost_estimate=pl.CostEstimate(flops=10_000_000, bytes_accessed=2_000_000, transcendentals=0),
        name="metric",
    )(sig_slots, sig_count, halves[0], metric_tensor)
    halves = [halves[0]] + [
        lax.ppermute(halves[s], "mu", [(z, goes_to(FACTORS[s], z)) for z in range(n_mu)])
        for s in range(1, n_mu)
    ]
    rows = n_mu * orb // n_aux
    parts = pl.pallas_call(
        functools.partial(exchange_kernel, n_mu, n_aux),
        out_shape=jax.ShapeDtypeStruct((n_aux * n_mu, rows // 2, 128), BF16),
        in_specs=[VMEM] * (n_mu + 2),
        out_specs=VMEM,
        scratch_shapes=[pltpu.VMEM((n_mu * orb, n_mu * orb), F32)],
        compiler_params=params(16),
        cost_estimate=pl.CostEstimate(flops=300_000_000, bytes_accessed=2_000_000, transcendentals=0),
        name="exchange",
    )(*halves, m_hi, m_lo)
    down = list(reversed(range(n_aux * n_mu)))
    parts = lax.all_to_all(parts, ("aux", "mu"), 0, 0, axis_index_groups=[down])
    return pl.pallas_call(
        sum_kernel,
        out_shape=jax.ShapeDtypeStruct((rows, orb), F32),
        in_specs=[VMEM],
        out_specs=VMEM,
        compiler_params=params(8),
        name="sum",
    )(parts)


def general(three_center, nu_slots, nu_count, density, metric_tensor, sig_slots, sig_count):
    highest = lax.Precision.HIGHEST
    orb_block = density.shape[0]
    lam_all = density.shape[1]
    aux_width = three_center.shape[2]
    dens_all = lax.all_gather(density, "mu", axis=0, tiled=True)

    def add_slot(k, running):
        nu_pick = nu_slots[0, k, 0]
        dens_rows = lax.dynamic_slice_in_dim(dens_all, nu_pick * orb_block, orb_block, 0)
        slab_piece = lax.dynamic_index_in_dim(three_center[0], k, 0, keepdims=False).reshape(
            aux_width, orb_block, orb_block
        )
        return running + jnp.einsum("pij,jl->lpi", slab_piece, dens_rows, precision=highest)

    halfway = lax.fori_loop(
        0, nu_count[0, 0], add_slot, jnp.zeros((lam_all, aux_width, orb_block), F32)
    )
    relayed = lax.all_to_all(halfway.astype(BF16), "mu", split_axis=0, concat_axis=2, tiled=True)
    widened = relayed.astype(F32)
    lam_rows = relayed.shape[0]
    orbitals = relayed.shape[2]

    def add_target(q, running):
        target = sig_slots[0, q, 0]
        weights = lax.dynamic_index_in_dim(metric_tensor[0], q, 0, keepdims=False).reshape(
            aux_width, lam_rows, orb_block
        )
        contrib = jnp.einsum("rpm,prc->mc", widened, weights, precision=highest)
        current = lax.dynamic_slice_in_dim(running, target * orb_block, orb_block, 1)
        return lax.dynamic_update_slice_in_dim(running, current + contrib, target * orb_block, 1)

    partial_k = lax.fori_loop(
        0, sig_count[0, 0], add_target, jnp.zeros((orbitals, orbitals), F32)
    )
    row_share = lax.psum_scatter(partial_k, "aux", scatter_dimension=0, tiled=True)
    return lax.psum_scatter(row_share, "mu", scatter_dimension=1, tiled=True)


def solution(mesh):
    n_aux, n_mu = mesh.shape["aux"], mesh.shape["mu"]

    def shards(three_center, nu_slots, nu_count, density, metric_tensor, sig_slots, sig_count):
        args = (three_center, nu_slots, nu_count, density, metric_tensor, sig_slots, sig_count)
        orb, lam_all = density.shape
        fits = (
            (n_aux, n_mu, orb, lam_all) == (8, 4, 64, 64)
            and three_center.shape[2:] == (64, orb * orb)
            and metric_tensor.shape[2:] == (64, lam_all // n_mu * orb)
        )
        return fast(n_mu, n_aux, *args) if fits else general(*args)

    placed = (
        P("mu", None, "aux", None),
        P("mu", None, "aux"),
        P("mu", "aux"),
        P("mu", None),
        P("mu", None, "aux", None),
        P("mu", None, "aux"),
        P("mu", "aux"),
    )
    return jax.shard_map(
        shards, mesh=mesh, in_specs=placed, out_specs=P("aux", "mu"), check_vma=False
    )
```

```python
import functools

import jax
import jax.numpy as jnp
from jax import lax
from jax.experimental import pallas as pl
from jax.experimental.pallas import tpu as pltpu
from jax.sharding import PartitionSpec as P

F32 = jnp.float32
BF16 = jnp.bfloat16
VMEM = pl.BlockSpec(memory_space=pltpu.VMEM)
SMEM = pl.BlockSpec(memory_space=pltpu.SMEM)
ANY = pl.BlockSpec(memory_space=pl.ANY)
HBM = pl.BlockSpec(memory_space=pltpu.HBM)


DENSITY_ORDER = (2, 3, 1)
FACTORS = (1, 2, 4, 3)


def goes_to(factor, z):
    return (z + 1) * factor % 5 - 1


def by_distance(refs, order):
    return [refs[0]] + [refs[1 + order.index(s)] for s in range(1, len(refs))]


def params(mib):
    return pltpu.CompilerParams(vmem_limit_bytes=mib * 1024 * 1024)


def split(x):
    hi = x.astype(BF16)
    return hi, (x - hi.astype(F32)).astype(BF16)


def iota(shape, dim):
    return lax.broadcasted_iota(jnp.int32, shape, dim)


def tensor_kernel(tensor, packed, buffer, arrived):
    _, slots, aux_width, width = tensor.shape
    parts = buffer.shape[0] // slots
    span = width // parts

    def fetch(k, part):
        return pltpu.make_async_copy(
            tensor.at[0, k, :, pl.ds(part * span, span)],
            buffer.at[k * parts + part],
            arrived.at[k * parts + part],
        )

    order = [(k, part) for k in range(slots) for part in range(parts)]
    for k, part in order:
        fetch(k, part).start()
    for k, part in order:
        fetch(k, part).wait()
        for chunk in range(span // 128):
            hi, lo = split(buffer[k * parts + part, :, chunk * 128:(chunk + 1) * 128])
            at = (part * (span // 128) + chunk) * aux_width
            packed[at:at + aux_width, k * 256:k * 256 + 128] = hi
            packed[at:at + aux_width, k * 256 + 128:(k + 1) * 256] = lo


def metric_kernel(sig_slots, sig_count, after, metric, m_hi, m_lo):
    _, sig, aux_width, width = metric.shape
    half = iota((aux_width, 128), 1) >= 64
    pair_of = jnp.where(half, 1, 0)
    targets = [jnp.where(q < sig_count[0, 0], sig_slots[0, 0, q], -1) for q in range(sig)]
    for pair in range(width // 128):
        sums = [[jnp.zeros((aux_width, 128), F32) for _ in range(2)] for _ in range(2)]
        for q in range(sig):
            block = metric[0, q, :, pair * 128:(pair + 1) * 128]
            turned = pltpu.roll(block, 64, 1)
            both = (jnp.where(half, turned, block), jnp.where(half, block, turned))
            for out_half in range(2):
                here = pair_of + 2 * out_half == targets[q]
                for parity in range(2):
                    sums[parity][out_half] += jnp.where(here, both[parity], 0.0)
        for parity in range(2):
            r = 2 * pair + parity
            at = ((r % 8) * 2 + r // 8) * aux_width
            for out_half in range(2):
                hi, lo = split(sums[parity][out_half])
                columns = slice(out_half * 128, (out_half + 1) * 128)
                m_hi[at:at + aux_width, columns] = hi
                m_lo[at:at + aux_width, columns] = lo


def half_kernel(n_mu, nu_slots, nu_count, *refs):
    dens = by_distance(refs[:n_mu], DENSITY_ORDER)
    packed = refs[n_mu]
    outs = refs[n_mu + 1:2 * n_mu + 1]
    d_both, weights, turned = refs[2 * n_mu + 1:]
    z = lax.axis_index("mu")
    orb, lam_all = dens[0].shape
    lam = lam_all // n_mu
    slots = nu_slots.shape[2]
    row, col = iota((lam_all, 128), 0), iota((lam_all, 128), 1)
    group = z
    for slot in range(1, n_mu):
        group = jnp.where((col >> 3) & 3 == slot, lax.rem((z + 1) * FACTORS[slot], 5) - 1, group)
    wanted = group * lam + (col >> 6) * 8 + (col & 7)
    choose = jnp.where(row == wanted, 1.0, 0.0).astype(BF16)
    for s in range(n_mu):
        hi, lo = split(dens[s][...])
        d_both[s, :, :128] = jnp.dot(hi, choose, preferred_element_type=F32)
        d_both[s, :, 128:] = jnp.dot(lo, choose, preferred_element_type=F32)
    orbital = (iota((orb, 256), 1) >> 5) & 1
    for k in range(slots):
        live = jnp.where(k < nu_count[0, 0], 1.0, 0.0)
        both = d_both[z ^ nu_slots[0, 0, k]] * live
        for i in range(2):
            block = jnp.where(orbital == i, both, 0.0).astype(BF16)
            for part in range(2):
                at = k * 256 + part * 128 + i * orb
                weights[at:at + orb, :] = block
    aux_width = outs[0].shape[1] // lam
    lower = iota((aux_width, 128), 1) < 64
    per_group = 512 // (2 * aux_width)
    span = per_group * 4
    for part in range(packed.shape[0] // 512):
        product = jnp.dot(
            packed[part * 512:(part + 1) * 512, :], weights[...], preferred_element_type=F32
        )
        total = product[:, :128] + product[:, 128:]
        for chunk in range(per_group):
            at = chunk * 2 * aux_width
            one, two = total[at:at + aux_width], total[at + aux_width:at + 2 * aux_width]
            top = jnp.where(lower, one, pltpu.roll(two, 64, 1))
            bottom = jnp.where(lower, pltpu.roll(one, 64, 1), two)
            at = (part * per_group + chunk) * 128
            turned[at:at + 128, :] = jnp.concatenate([top, bottom], axis=0).T
        for s in range(n_mu):
            for r in range(8):
                picked = turned[pl.ds(part * per_group * 128 + s * 8 + r, span, stride=32), :]
                outs[s][part * span:(part + 1) * span, r * 128:(r + 1) * 128] = picked.astype(BF16)


def exchange_kernel(n_mu, n_aux, *refs):
    halves = refs[:n_mu]
    m_hi, m_lo, out, total = refs[n_mu:]
    z = lax.axis_index("mu")
    left = jnp.concatenate([h[...] for h in halves], axis=0)
    product = jnp.dot(left, m_hi[...], preferred_element_type=F32)
    product += jnp.dot(left, m_lo[...], preferred_element_type=F32)
    orb = halves[0].shape[0]
    for s in range(n_mu):
        back = pow(FACTORS[s], -1, 5)
        block = lax.rem((z + 1) * back, 5) - 1
        total[pl.ds(pl.multiple_of(block * orb, orb), orb), :] = product[s * orb:(s + 1) * orb]
    rows = out.shape[1]
    lower = iota((rows, 128), 1) < 64
    for a in range(n_aux):
        for pair in range(n_mu // 2):
            columns = slice(pair * 128, (pair + 1) * 128)
            top = total[a * 2 * rows:(a * 2 + 1) * rows, columns]
            bottom = total[(a * 2 + 1) * rows:(a * 2 + 2) * rows, columns]
            at = n_aux * n_mu - 1 - (a * n_mu + pair * 2)
            out[at] = jnp.where(lower, top, pltpu.roll(bottom, 64, 1)).astype(BF16)
            out[at - 1] = jnp.where(lower, pltpu.roll(top, 64, 1), bottom).astype(BF16)


def sum_kernel(parts, out):
    total = parts[0].astype(F32)
    for d in range(1, parts.shape[0]):
        total += parts[d].astype(F32)
    rows = parts.shape[1]
    out[:rows, :] = total[:, :64]
    out[rows:, :] = total[:, 64:]


def fast(n_mu, n_aux, three_center, nu_slots, nu_count, density, metric_tensor, sig_slots, sig_count):
    orb, lam_all = density.shape
    slots, aux_width = three_center.shape[1:3]
    lam = lam_all // n_mu
    turns = [[(z, z ^ s) for z in range(n_mu)] for s in range(n_mu)]
    dens = [density] + [lax.ppermute(density, "mu", turns[s]) for s in DENSITY_ORDER]
    nu_slots, sig_slots = jnp.swapaxes(nu_slots, 1, 2), jnp.swapaxes(sig_slots, 1, 2)
    chunks = three_center.shape[3] // 256
    t_shape = jax.ShapeDtypeStruct((2 * chunks * aux_width, slots * 256), BF16)
    m_shape = jax.ShapeDtypeStruct((lam * aux_width, n_mu * orb), BF16)
    packed = pl.pallas_call(
        tensor_kernel,
        out_shape=t_shape,
        in_specs=[HBM],
        out_specs=VMEM,
        scratch_shapes=[
            pltpu.VMEM((slots * 4, aux_width, chunks * 64), F32),
            pltpu.SemaphoreType.DMA((slots * 4,)),
        ],
        compiler_params=params(50),
        cost_estimate=pl.CostEstimate(flops=10_000_000, bytes_accessed=6_000_000, transcendentals=0),
        name="tensor",
    )(three_center)
    half_shape = jax.ShapeDtypeStruct((orb, lam * aux_width), BF16)
    halves = pl.pallas_call(
        functools.partial(half_kernel, n_mu),
        out_shape=(half_shape,) * n_mu,
        in_specs=[SMEM, SMEM] + [VMEM] * (n_mu + 1),
        out_specs=(VMEM,) * n_mu,
        scratch_shapes=[
            pltpu.VMEM((n_mu, orb, 256), F32),
            pltpu.VMEM((slots * 256, 256), BF16),
            pltpu.VMEM((chunks * 128, 128), F32),
        ],
        compiler_params=params(16),
        cost_estimate=pl.CostEstimate(flops=1_200_000_000, bytes_accessed=4_000_000, transcendentals=0),
        name="half",
    )(nu_slots, nu_count, *dens, packed)
    m_hi, m_lo = pl.pallas_call(
        metric_kernel,
        out_shape=(m_shape, m_shape),
        in_specs=[SMEM, SMEM, ANY, VMEM],
        out_specs=(VMEM, VMEM),
        compiler_params=params(16),
        cost_estimate=pl.CostEstimate(flops=10_000_000, bytes_accessed=2_000_000, transcendentals=0),
        name="metric",
    )(sig_slots, sig_count, halves[0], metric_tensor)
    halves = [halves[0]] + [
        lax.ppermute(halves[s], "mu", [(z, goes_to(FACTORS[s], z)) for z in range(n_mu)])
        for s in range(1, n_mu)
    ]
    rows = n_mu * orb // n_aux
    parts = pl.pallas_call(
        functools.partial(exchange_kernel, n_mu, n_aux),
        out_shape=jax.ShapeDtypeStruct((n_aux * n_mu, rows // 2, 128), BF16),
        in_specs=[VMEM] * (n_mu + 2),
        out_specs=VMEM,
        scratch_shapes=[pltpu.VMEM((n_mu * orb, n_mu * orb), F32)],
        compiler_params=params(16),
        cost_estimate=pl.CostEstimate(flops=300_000_000, bytes_accessed=2_000_000, transcendentals=0),
        name="exchange",
    )(*halves, m_hi, m_lo)
    down = list(reversed(range(n_aux * n_mu)))
    parts = lax.all_to_all(parts, ("aux", "mu"), 0, 0, axis_index_groups=[down])
    return pl.pallas_call(
        sum_kernel,
        out_shape=jax.ShapeDtypeStruct((rows, orb), F32),
        in_specs=[VMEM],
        out_specs=VMEM,
        compiler_params=params(8),
        name="sum",
    )(parts)


def general(three_center, nu_slots, nu_count, density, metric_tensor, sig_slots, sig_count):
    highest = lax.Precision.HIGHEST
    orb_block = density.shape[0]
    lam_all = density.shape[1]
    aux_width = three_center.shape[2]
    dens_all = lax.all_gather(density, "mu", axis=0, tiled=True)

    def add_slot(k, running):
        nu_pick = nu_slots[0, k, 0]
        dens_rows = lax.dynamic_slice_in_dim(dens_all, nu_pick * orb_block, orb_block, 0)
        slab_piece = lax.dynamic_index_in_dim(three_center[0], k, 0, keepdims=False).reshape(
            aux_width, orb_block, orb_block
        )
        return running + jnp.einsum("pij,jl->lpi", slab_piece, dens_rows, precision=highest)

    halfway = lax.fori_loop(
        0, nu_count[0, 0], add_slot, jnp.zeros((lam_all, aux_width, orb_block), F32)
    )
    relayed = lax.all_to_all(halfway.astype(BF16), "mu", split_axis=0, concat_axis=2, tiled=True)
    widened = relayed.astype(F32)
    lam_rows = relayed.shape[0]
    orbitals = relayed.shape[2]

    def add_target(q, running):
        target = sig_slots[0, q, 0]
        weights = lax.dynamic_index_in_dim(metric_tensor[0], q, 0, keepdims=False).reshape(
            aux_width, lam_rows, orb_block
        )
        contrib = jnp.einsum("rpm,prc->mc", widened, weights, precision=highest)
        current = lax.dynamic_slice_in_dim(running, target * orb_block, orb_block, 1)
        return lax.dynamic_update_slice_in_dim(running, current + contrib, target * orb_block, 1)

    partial_k = lax.fori_loop(
        0, sig_count[0, 0], add_target, jnp.zeros((orbitals, orbitals), F32)
    )
    row_share = lax.psum_scatter(partial_k, "aux", scatter_dimension=0, tiled=True)
    return lax.psum_scatter(row_share, "mu", scatter_dimension=1, tiled=True)


def solution(mesh):
    n_aux, n_mu = mesh.shape["aux"], mesh.shape["mu"]

    def shards(three_center, nu_slots, nu_count, density, metric_tensor, sig_slots, sig_count):
        args = (three_center, nu_slots, nu_count, density, metric_tensor, sig_slots, sig_count)
        orb, lam_all = density.shape
        fits = (
            (n_aux, n_mu, orb, lam_all) == (8, 4, 64, 64)
            and three_center.shape[2:] == (64, orb * orb)
            and metric_tensor.shape[2:] == (64, lam_all // n_mu * orb)
        )
        return fast(n_mu, n_aux, *args) if fits else general(*args)

    placed = (
        P("mu", None, "aux", None),
        P("mu", None, "aux"),
        P("mu", "aux"),
        P("mu", None),
        P("mu", None, "aux", None),
        P("mu", None, "aux"),
        P("mu", "aux"),
    )
    return jax.shard_map(
        shards, mesh=mesh, in_specs=placed, out_specs=P("aux", "mu"), check_vma=False
    )
```

```python
import functools

import jax
import jax.numpy as jnp
from jax import lax
from jax.experimental import pallas as pl
from jax.experimental.pallas import tpu as pltpu
from jax.sharding import PartitionSpec as P

F32 = jnp.float32
BF16 = jnp.bfloat16
VMEM = pl.BlockSpec(memory_space=pltpu.VMEM)
SMEM = pl.BlockSpec(memory_space=pltpu.SMEM)
ANY = pl.BlockSpec(memory_space=pl.ANY)
HBM = pl.BlockSpec(memory_space=pltpu.HBM)


DENSITY_ORDER = (2, 3, 1)
HALF_ORDER = (0, 2, 3, 1)


def by_distance(refs, order):
    return [refs[0]] + [refs[1 + order.index(s)] for s in range(1, len(refs))]


def params(mib):
    return pltpu.CompilerParams(vmem_limit_bytes=mib * 1024 * 1024)


def split(x):
    hi = x.astype(BF16)
    return hi, (x - hi.astype(F32)).astype(BF16)


def iota(shape, dim):
    return lax.broadcasted_iota(jnp.int32, shape, dim)


def tensor_kernel(tensor, packed, buffer, arrived):
    _, slots, aux_width, width = tensor.shape
    parts = buffer.shape[0] // slots
    span = width // parts

    def fetch(k, part):
        return pltpu.make_async_copy(
            tensor.at[0, k, :, pl.ds(part * span, span)],
            buffer.at[k * parts + part],
            arrived.at[k * parts + part],
        )

    order = [(k, part) for k in range(slots) for part in range(parts)]
    for k, part in order:
        fetch(k, part).start()
    for k, part in order:
        fetch(k, part).wait()
        for chunk in range(span // 128):
            hi, lo = split(buffer[k * parts + part, :, chunk * 128:(chunk + 1) * 128])
            at = (part * (span // 128) + chunk) * aux_width
            packed[at:at + aux_width, k * 256:k * 256 + 128] = hi
            packed[at:at + aux_width, k * 256 + 128:(k + 1) * 256] = lo


def metric_kernel(sig_slots, sig_count, after, metric, m_hi, m_lo):
    _, sig, aux_width, width = metric.shape
    half = iota((aux_width, 128), 1) >= 64
    pair_of = jnp.where(half, 1, 0)
    targets = [jnp.where(q < sig_count[0, 0], sig_slots[0, 0, q], -1) for q in range(sig)]
    for pair in range(width // 128):
        sums = [[jnp.zeros((aux_width, 128), F32) for _ in range(2)] for _ in range(2)]
        for q in range(sig):
            block = metric[0, q, :, pair * 128:(pair + 1) * 128]
            turned = pltpu.roll(block, 64, 1)
            both = (jnp.where(half, turned, block), jnp.where(half, block, turned))
            for out_half in range(2):
                here = pair_of + 2 * out_half == targets[q]
                for parity in range(2):
                    sums[parity][out_half] += jnp.where(here, both[parity], 0.0)
        for parity in range(2):
            r = 2 * pair + parity
            at = ((r % 8) * 2 + r // 8) * aux_width
            for out_half in range(2):
                hi, lo = split(sums[parity][out_half])
                columns = slice(out_half * 128, (out_half + 1) * 128)
                m_hi[at:at + aux_width, columns] = hi
                m_lo[at:at + aux_width, columns] = lo


def half_kernel(n_mu, nu_slots, nu_count, *refs):
    dens = by_distance(refs[:n_mu], DENSITY_ORDER)
    packed = refs[n_mu]
    outs = refs[n_mu + 1:2 * n_mu + 1]
    d_both, weights, turned = refs[2 * n_mu + 1:]
    z = lax.axis_index("mu")
    orb, lam_all = dens[0].shape
    lam = lam_all // n_mu
    slots = nu_slots.shape[2]
    row, col = iota((lam_all, 128), 0), iota((lam_all, 128), 1)
    group = z
    for slot in range(1, n_mu):
        group = jnp.where((col >> 3) & 3 == slot, z ^ HALF_ORDER[slot], group)
    wanted = group * lam + (col >> 6) * 8 + (col & 7)
    choose = jnp.where(row == wanted, 1.0, 0.0).astype(BF16)
    for s in range(n_mu):
        hi, lo = split(dens[s][...])
        d_both[s, :, :128] = jnp.dot(hi, choose, preferred_element_type=F32)
        d_both[s, :, 128:] = jnp.dot(lo, choose, preferred_element_type=F32)
    orbital = (iota((orb, 256), 1) >> 5) & 1
    for k in range(slots):
        live = jnp.where(k < nu_count[0, 0], 1.0, 0.0)
        both = d_both[z ^ nu_slots[0, 0, k]] * live
        for i in range(2):
            block = jnp.where(orbital == i, both, 0.0).astype(BF16)
            for part in range(2):
                at = k * 256 + part * 128 + i * orb
                weights[at:at + orb, :] = block
    aux_width = outs[0].shape[1] // lam
    lower = iota((aux_width, 128), 1) < 64
    per_group = 512 // (2 * aux_width)
    span = per_group * 4
    for part in range(packed.shape[0] // 512):
        product = jnp.dot(
            packed[part * 512:(part + 1) * 512, :], weights[...], preferred_element_type=F32
        )
        total = product[:, :128] + product[:, 128:]
        for chunk in range(per_group):
            at = chunk * 2 * aux_width
            one, two = total[at:at + aux_width], total[at + aux_width:at + 2 * aux_width]
            top = jnp.where(lower, one, pltpu.roll(two, 64, 1))
            bottom = jnp.where(lower, pltpu.roll(one, 64, 1), two)
            at = (part * per_group + chunk) * 128
            turned[at:at + 128, :] = jnp.concatenate([top, bottom], axis=0).T
        for s in range(n_mu):
            for r in range(8):
                picked = turned[pl.ds(part * per_group * 128 + s * 8 + r, span, stride=32), :]
                outs[s][part * span:(part + 1) * span, r * 128:(r + 1) * 128] = picked.astype(BF16)


def exchange_kernel(n_mu, n_aux, *refs):
    halves = refs[:n_mu]
    m_hi, m_lo, out, total = refs[n_mu:]
    z = lax.axis_index("mu")
    left = jnp.concatenate([h[...] for h in halves], axis=0)
    product = jnp.dot(left, m_hi[...], preferred_element_type=F32)
    product += jnp.dot(left, m_lo[...], preferred_element_type=F32)
    orb = halves[0].shape[0]
    for s in range(n_mu):
        block = z ^ HALF_ORDER[s]
        total[pl.ds(pl.multiple_of(block * orb, orb), orb), :] = product[s * orb:(s + 1) * orb]
    rows = out.shape[1]
    lower = iota((rows, 128), 1) < 64
    for a in range(n_aux):
        for pair in range(n_mu // 2):
            columns = slice(pair * 128, (pair + 1) * 128)
            top = total[a * 2 * rows:(a * 2 + 1) * rows, columns]
            bottom = total[(a * 2 + 1) * rows:(a * 2 + 2) * rows, columns]
            at = n_aux * n_mu - 1 - (a * n_mu + pair * 2)
            out[at] = jnp.where(lower, top, pltpu.roll(bottom, 64, 1)).astype(BF16)
            out[at - 1] = jnp.where(lower, pltpu.roll(top, 64, 1), bottom).astype(BF16)


def sum_kernel(parts, out):
    total = parts[0].astype(F32)
    for d in range(1, parts.shape[0]):
        total += parts[d].astype(F32)
    rows = parts.shape[1]
    out[:rows, :] = total[:, :64]
    out[rows:, :] = total[:, 64:]


def fast(n_mu, n_aux, three_center, nu_slots, nu_count, density, metric_tensor, sig_slots, sig_count):
    orb, lam_all = density.shape
    slots, aux_width = three_center.shape[1:3]
    lam = lam_all // n_mu
    turns = [[(z, z ^ s) for z in range(n_mu)] for s in range(n_mu)]
    dens = [density] + [lax.ppermute(density, "mu", turns[s]) for s in DENSITY_ORDER]
    nu_slots, sig_slots = jnp.swapaxes(nu_slots, 1, 2), jnp.swapaxes(sig_slots, 1, 2)
    chunks = three_center.shape[3] // 256
    t_shape = jax.ShapeDtypeStruct((2 * chunks * aux_width, slots * 256), BF16)
    m_shape = jax.ShapeDtypeStruct((lam * aux_width, n_mu * orb), BF16)
    packed = pl.pallas_call(
        tensor_kernel,
        out_shape=t_shape,
        in_specs=[HBM],
        out_specs=VMEM,
        scratch_shapes=[
            pltpu.VMEM((slots * 4, aux_width, chunks * 64), F32),
            pltpu.SemaphoreType.DMA((slots * 4,)),
        ],
        compiler_params=params(50),
        cost_estimate=pl.CostEstimate(flops=10_000_000, bytes_accessed=6_000_000, transcendentals=0),
        name="tensor",
    )(three_center)
    half_shape = jax.ShapeDtypeStruct((orb, lam * aux_width), BF16)
    halves = pl.pallas_call(
        functools.partial(half_kernel, n_mu),
        out_shape=(half_shape,) * n_mu,
        in_specs=[SMEM, SMEM] + [VMEM] * (n_mu + 1),
        out_specs=(VMEM,) * n_mu,
        scratch_shapes=[
            pltpu.VMEM((n_mu, orb, 256), F32),
            pltpu.VMEM((slots * 256, 256), BF16),
            pltpu.VMEM((chunks * 128, 128), F32),
        ],
        compiler_params=params(16),
        cost_estimate=pl.CostEstimate(flops=1_200_000_000, bytes_accessed=4_000_000, transcendentals=0),
        name="half",
    )(nu_slots, nu_count, *dens, packed)
    m_hi, m_lo = pl.pallas_call(
        metric_kernel,
        out_shape=(m_shape, m_shape),
        in_specs=[SMEM, SMEM, ANY, VMEM],
        out_specs=(VMEM, VMEM),
        compiler_params=params(16),
        cost_estimate=pl.CostEstimate(flops=10_000_000, bytes_accessed=2_000_000, transcendentals=0),
        name="metric",
    )(sig_slots, sig_count, halves[0], metric_tensor)
    halves = [halves[0]] + [
        lax.ppermute(halves[s], "mu", turns[HALF_ORDER[s]]) for s in range(1, n_mu)
    ]
    rows = n_mu * orb // n_aux
    parts = pl.pallas_call(
        functools.partial(exchange_kernel, n_mu, n_aux),
        out_shape=jax.ShapeDtypeStruct((n_aux * n_mu, rows // 2, 128), BF16),
        in_specs=[VMEM] * (n_mu + 2),
        out_specs=VMEM,
        scratch_shapes=[pltpu.VMEM((n_mu * orb, n_mu * orb), F32)],
        compiler_params=params(16),
        cost_estimate=pl.CostEstimate(flops=300_000_000, bytes_accessed=2_000_000, transcendentals=0),
        name="exchange",
    )(*halves, m_hi, m_lo)
    down = list(reversed(range(n_aux * n_mu)))
    parts = lax.all_to_all(parts, ("aux", "mu"), 0, 0, axis_index_groups=[down])
    return pl.pallas_call(
        sum_kernel,
        out_shape=jax.ShapeDtypeStruct((rows, orb), F32),
        in_specs=[VMEM],
        out_specs=VMEM,
        compiler_params=params(8),
        name="sum",
    )(parts)


def general(three_center, nu_slots, nu_count, density, metric_tensor, sig_slots, sig_count):
    highest = lax.Precision.HIGHEST
    orb_block = density.shape[0]
    lam_all = density.shape[1]
    aux_width = three_center.shape[2]
    dens_all = lax.all_gather(density, "mu", axis=0, tiled=True)

    def add_slot(k, running):
        nu_pick = nu_slots[0, k, 0]
        dens_rows = lax.dynamic_slice_in_dim(dens_all, nu_pick * orb_block, orb_block, 0)
        slab_piece = lax.dynamic_index_in_dim(three_center[0], k, 0, keepdims=False).reshape(
            aux_width, orb_block, orb_block
        )
        return running + jnp.einsum("pij,jl->lpi", slab_piece, dens_rows, precision=highest)

    halfway = lax.fori_loop(
        0, nu_count[0, 0], add_slot, jnp.zeros((lam_all, aux_width, orb_block), F32)
    )
    relayed = lax.all_to_all(halfway.astype(BF16), "mu", split_axis=0, concat_axis=2, tiled=True)
    widened = relayed.astype(F32)
    lam_rows = relayed.shape[0]
    orbitals = relayed.shape[2]

    def add_target(q, running):
        target = sig_slots[0, q, 0]
        weights = lax.dynamic_index_in_dim(metric_tensor[0], q, 0, keepdims=False).reshape(
            aux_width, lam_rows, orb_block
        )
        contrib = jnp.einsum("rpm,prc->mc", widened, weights, precision=highest)
        current = lax.dynamic_slice_in_dim(running, target * orb_block, orb_block, 1)
        return lax.dynamic_update_slice_in_dim(running, current + contrib, target * orb_block, 1)

    partial_k = lax.fori_loop(
        0, sig_count[0, 0], add_target, jnp.zeros((orbitals, orbitals), F32)
    )
    row_share = lax.psum_scatter(partial_k, "aux", scatter_dimension=0, tiled=True)
    return lax.psum_scatter(row_share, "mu", scatter_dimension=1, tiled=True)


def solution(mesh):
    n_aux, n_mu = mesh.shape["aux"], mesh.shape["mu"]

    def shards(three_center, nu_slots, nu_count, density, metric_tensor, sig_slots, sig_count):
        args = (three_center, nu_slots, nu_count, density, metric_tensor, sig_slots, sig_count)
        orb, lam_all = density.shape
        fits = (
            (n_aux, n_mu, orb, lam_all) == (8, 4, 64, 64)
            and three_center.shape[2:] == (64, orb * orb)
            and metric_tensor.shape[2:] == (64, lam_all // n_mu * orb)
        )
        return fast(n_mu, n_aux, *args) if fits else general(*args)

    placed = (
        P("mu", None, "aux", None),
        P("mu", None, "aux"),
        P("mu", "aux"),
        P("mu", None),
        P("mu", None, "aux", None),
        P("mu", None, "aux"),
        P("mu", "aux"),
    )
    return jax.shard_map(
        shards, mesh=mesh, in_specs=placed, out_specs=P("aux", "mu"), check_vma=False
    )
```

```python
import functools

import jax
import jax.numpy as jnp
from jax import lax
from jax.experimental import pallas as pl
from jax.experimental.pallas import tpu as pltpu
from jax.sharding import PartitionSpec as P

F32 = jnp.float32
BF16 = jnp.bfloat16
VMEM = pl.BlockSpec(memory_space=pltpu.VMEM)
SMEM = pl.BlockSpec(memory_space=pltpu.SMEM)
ANY = pl.BlockSpec(memory_space=pl.ANY)
HBM = pl.BlockSpec(memory_space=pltpu.HBM)


DENSITY_ORDER = (2, 3, 1)
HALF_ORDER = (0, 2, 3, 1)


def by_distance(refs, order):
    return [refs[0]] + [refs[1 + order.index(s)] for s in range(1, len(refs))]


def params(mib):
    return pltpu.CompilerParams(vmem_limit_bytes=mib * 1024 * 1024)


def split(x):
    hi = x.astype(BF16)
    return hi, (x - hi.astype(F32)).astype(BF16)


def iota(shape, dim):
    return lax.broadcasted_iota(jnp.int32, shape, dim)


def tensor_kernel(tensor, packed, buffer, arrived):
    _, slots, aux_width, width = tensor.shape
    parts = buffer.shape[0] // slots
    span = width // parts

    def fetch(k, part):
        return pltpu.make_async_copy(
            tensor.at[0, k, :, pl.ds(part * span, span)],
            buffer.at[k * parts + part],
            arrived.at[k * parts + part],
        )

    order = [(k, part) for k in range(slots) for part in range(parts)]
    for k, part in order:
        fetch(k, part).start()
    for k, part in order:
        fetch(k, part).wait()
        for chunk in range(span // 128):
            hi, lo = split(buffer[k * parts + part, :, chunk * 128:(chunk + 1) * 128])
            at = (part * (span // 128) + chunk) * aux_width
            packed[at:at + aux_width, k * 256:k * 256 + 128] = hi
            packed[at:at + aux_width, k * 256 + 128:(k + 1) * 256] = lo


def metric_kernel(sig_slots, sig_count, after, metric, m_hi, m_lo):
    _, sig, aux_width, width = metric.shape
    half = iota((aux_width, 128), 1) >= 64
    pair_of = jnp.where(half, 1, 0)
    targets = [jnp.where(q < sig_count[0, 0], sig_slots[0, 0, q], -1) for q in range(sig)]
    for pair in range(width // 128):
        sums = [[jnp.zeros((aux_width, 128), F32) for _ in range(2)] for _ in range(2)]
        for q in range(sig):
            block = metric[0, q, :, pair * 128:(pair + 1) * 128]
            turned = pltpu.roll(block, 64, 1)
            both = (jnp.where(half, turned, block), jnp.where(half, block, turned))
            for out_half in range(2):
                here = pair_of + 2 * out_half == targets[q]
                for parity in range(2):
                    sums[parity][out_half] += jnp.where(here, both[parity], 0.0)
        for parity in range(2):
            r = 2 * pair + parity
            at = ((r % 8) * 2 + r // 8) * aux_width
            for out_half in range(2):
                hi, lo = split(sums[parity][out_half])
                columns = slice(out_half * 128, (out_half + 1) * 128)
                m_hi[at:at + aux_width, columns] = hi
                m_lo[at:at + aux_width, columns] = lo


def half_kernel(n_mu, nu_slots, nu_count, *refs):
    dens = by_distance(refs[:n_mu], DENSITY_ORDER)
    packed = refs[n_mu]
    outs = refs[n_mu + 1:2 * n_mu + 1]
    d_both, weights, turned = refs[2 * n_mu + 1:]
    z = lax.axis_index("mu")
    orb, lam_all = dens[0].shape
    lam = lam_all // n_mu
    slots = nu_slots.shape[2]
    row, col = iota((lam_all, 128), 0), iota((lam_all, 128), 1)
    group = z
    for slot in range(1, n_mu):
        group = jnp.where((col >> 3) & 3 == slot, z ^ HALF_ORDER[slot], group)
    wanted = group * lam + (col >> 6) * 8 + (col & 7)
    choose = jnp.where(row == wanted, 1.0, 0.0).astype(BF16)
    halves = [split(d[...]) for d in dens]
    stacked = jnp.concatenate([half[part] for part in range(2) for half in halves], axis=0)
    chosen = jnp.dot(stacked, choose, preferred_element_type=F32)
    for s in range(n_mu):
        d_both[s, :, :128] = chosen[s * orb:(s + 1) * orb]
        d_both[s, :, 128:] = chosen[(n_mu + s) * orb:(n_mu + s + 1) * orb]
    orbital = (iota((orb, 256), 1) >> 5) & 1
    for k in range(slots):
        live = jnp.where(k < nu_count[0, 0], 1.0, 0.0)
        both = d_both[z ^ nu_slots[0, 0, k]] * live
        for i in range(2):
            block = jnp.where(orbital == i, both, 0.0).astype(BF16)
            for part in range(2):
                at = k * 256 + part * 128 + i * orb
                weights[at:at + orb, :] = block
    aux_width = outs[0].shape[1] // lam
    lower = iota((aux_width, 128), 1) < 64
    per_group = 512 // (2 * aux_width)
    span = per_group * 4
    for part in range(packed.shape[0] // 512):
        product = jnp.dot(
            packed[part * 512:(part + 1) * 512, :], weights[...], preferred_element_type=F32
        )
        total = product[:, :128] + product[:, 128:]
        for chunk in range(per_group):
            at = chunk * 2 * aux_width
            one, two = total[at:at + aux_width], total[at + aux_width:at + 2 * aux_width]
            top = jnp.where(lower, one, pltpu.roll(two, 64, 1))
            bottom = jnp.where(lower, pltpu.roll(one, 64, 1), two)
            at = (part * per_group + chunk) * 128
            turned[at:at + 128, :] = jnp.concatenate([top, bottom], axis=0).T
        for s in range(n_mu):
            for r in range(8):
                picked = turned[pl.ds(part * per_group * 128 + s * 8 + r, span, stride=32), :]
                outs[s][part * span:(part + 1) * span, r * 128:(r + 1) * 128] = picked.astype(BF16)


def exchange_kernel(n_mu, n_aux, *refs):
    halves = refs[:n_mu]
    m_hi, m_lo, out, total = refs[n_mu:]
    z = lax.axis_index("mu")
    left = jnp.concatenate([h[...] for h in halves], axis=0)
    product = jnp.dot(left, m_hi[...], preferred_element_type=F32)
    product += jnp.dot(left, m_lo[...], preferred_element_type=F32)
    orb = halves[0].shape[0]
    for s in range(n_mu):
        block = z ^ HALF_ORDER[s]
        total[pl.ds(pl.multiple_of(block * orb, orb), orb), :] = product[s * orb:(s + 1) * orb]
    rows = out.shape[1]
    lower = iota((rows, 128), 1) < 64
    for a in range(n_aux):
        for pair in range(n_mu // 2):
            columns = slice(pair * 128, (pair + 1) * 128)
            top = total[a * 2 * rows:(a * 2 + 1) * rows, columns]
            bottom = total[(a * 2 + 1) * rows:(a * 2 + 2) * rows, columns]
            at = n_aux * n_mu - 1 - (a * n_mu + pair * 2)
            out[at] = jnp.where(lower, top, pltpu.roll(bottom, 64, 1)).astype(BF16)
            out[at - 1] = jnp.where(lower, pltpu.roll(top, 64, 1), bottom).astype(BF16)


def sum_kernel(parts, out):
    total = parts[0].astype(F32)
    for d in range(1, parts.shape[0]):
        total += parts[d].astype(F32)
    rows = parts.shape[1]
    out[:rows, :] = total[:, :64]
    out[rows:, :] = total[:, 64:]


def fast(n_mu, n_aux, three_center, nu_slots, nu_count, density, metric_tensor, sig_slots, sig_count):
    orb, lam_all = density.shape
    slots, aux_width = three_center.shape[1:3]
    lam = lam_all // n_mu
    turns = [[(z, z ^ s) for z in range(n_mu)] for s in range(n_mu)]
    dens = [density] + [lax.ppermute(density, "mu", turns[s]) for s in DENSITY_ORDER]
    nu_slots, sig_slots = jnp.swapaxes(nu_slots, 1, 2), jnp.swapaxes(sig_slots, 1, 2)
    chunks = three_center.shape[3] // 256
    t_shape = jax.ShapeDtypeStruct((2 * chunks * aux_width, slots * 256), BF16)
    m_shape = jax.ShapeDtypeStruct((lam * aux_width, n_mu * orb), BF16)
    packed = pl.pallas_call(
        tensor_kernel,
        out_shape=t_shape,
        in_specs=[HBM],
        out_specs=VMEM,
        scratch_shapes=[
            pltpu.VMEM((slots * 4, aux_width, chunks * 64), F32),
            pltpu.SemaphoreType.DMA((slots * 4,)),
        ],
        compiler_params=params(50),
        cost_estimate=pl.CostEstimate(flops=10_000_000, bytes_accessed=6_000_000, transcendentals=0),
        name="tensor",
    )(three_center)
    half_shape = jax.ShapeDtypeStruct((orb, lam * aux_width), BF16)
    halves = pl.pallas_call(
        functools.partial(half_kernel, n_mu),
        out_shape=(half_shape,) * n_mu,
        in_specs=[SMEM, SMEM] + [VMEM] * (n_mu + 1),
        out_specs=(VMEM,) * n_mu,
        scratch_shapes=[
            pltpu.VMEM((n_mu, orb, 256), F32),
            pltpu.VMEM((slots * 256, 256), BF16),
            pltpu.VMEM((chunks * 128, 128), F32),
        ],
        compiler_params=params(16),
        cost_estimate=pl.CostEstimate(flops=1_200_000_000, bytes_accessed=4_000_000, transcendentals=0),
        name="half",
    )(nu_slots, nu_count, *dens, packed)
    m_hi, m_lo = pl.pallas_call(
        metric_kernel,
        out_shape=(m_shape, m_shape),
        in_specs=[SMEM, SMEM, ANY, VMEM],
        out_specs=(VMEM, VMEM),
        compiler_params=params(16),
        cost_estimate=pl.CostEstimate(flops=10_000_000, bytes_accessed=2_000_000, transcendentals=0),
        name="metric",
    )(sig_slots, sig_count, halves[0], metric_tensor)
    halves = [halves[0]] + [
        lax.ppermute(halves[s], "mu", turns[HALF_ORDER[s]]) for s in range(1, n_mu)
    ]
    rows = n_mu * orb // n_aux
    parts = pl.pallas_call(
        functools.partial(exchange_kernel, n_mu, n_aux),
        out_shape=jax.ShapeDtypeStruct((n_aux * n_mu, rows // 2, 128), BF16),
        in_specs=[VMEM] * (n_mu + 2),
        out_specs=VMEM,
        scratch_shapes=[pltpu.VMEM((n_mu * orb, n_mu * orb), F32)],
        compiler_params=params(16),
        cost_estimate=pl.CostEstimate(flops=300_000_000, bytes_accessed=2_000_000, transcendentals=0),
        name="exchange",
    )(*halves, m_hi, m_lo)
    down = list(reversed(range(n_aux * n_mu)))
    parts = lax.all_to_all(parts, ("aux", "mu"), 0, 0, axis_index_groups=[down])
    return pl.pallas_call(
        sum_kernel,
        out_shape=jax.ShapeDtypeStruct((rows, orb), F32),
        in_specs=[VMEM],
        out_specs=VMEM,
        compiler_params=params(8),
        name="sum",
    )(parts)


def general(three_center, nu_slots, nu_count, density, metric_tensor, sig_slots, sig_count):
    highest = lax.Precision.HIGHEST
    orb_block = density.shape[0]
    lam_all = density.shape[1]
    aux_width = three_center.shape[2]
    dens_all = lax.all_gather(density, "mu", axis=0, tiled=True)

    def add_slot(k, running):
        nu_pick = nu_slots[0, k, 0]
        dens_rows = lax.dynamic_slice_in_dim(dens_all, nu_pick * orb_block, orb_block, 0)
        slab_piece = lax.dynamic_index_in_dim(three_center[0], k, 0, keepdims=False).reshape(
            aux_width, orb_block, orb_block
        )
        return running + jnp.einsum("pij,jl->lpi", slab_piece, dens_rows, precision=highest)

    halfway = lax.fori_loop(
        0, nu_count[0, 0], add_slot, jnp.zeros((lam_all, aux_width, orb_block), F32)
    )
    relayed = lax.all_to_all(halfway.astype(BF16), "mu", split_axis=0, concat_axis=2, tiled=True)
    widened = relayed.astype(F32)
    lam_rows = relayed.shape[0]
    orbitals = relayed.shape[2]

    def add_target(q, running):
        target = sig_slots[0, q, 0]
        weights = lax.dynamic_index_in_dim(metric_tensor[0], q, 0, keepdims=False).reshape(
            aux_width, lam_rows, orb_block
        )
        contrib = jnp.einsum("rpm,prc->mc", widened, weights, precision=highest)
        current = lax.dynamic_slice_in_dim(running, target * orb_block, orb_block, 1)
        return lax.dynamic_update_slice_in_dim(running, current + contrib, target * orb_block, 1)

    partial_k = lax.fori_loop(
        0, sig_count[0, 0], add_target, jnp.zeros((orbitals, orbitals), F32)
    )
    row_share = lax.psum_scatter(partial_k, "aux", scatter_dimension=0, tiled=True)
    return lax.psum_scatter(row_share, "mu", scatter_dimension=1, tiled=True)


def solution(mesh):
    n_aux, n_mu = mesh.shape["aux"], mesh.shape["mu"]

    def shards(three_center, nu_slots, nu_count, density, metric_tensor, sig_slots, sig_count):
        args = (three_center, nu_slots, nu_count, density, metric_tensor, sig_slots, sig_count)
        orb, lam_all = density.shape
        fits = (
            (n_aux, n_mu, orb, lam_all) == (8, 4, 64, 64)
            and three_center.shape[2:] == (64, orb * orb)
            and metric_tensor.shape[2:] == (64, lam_all // n_mu * orb)
        )
        return fast(n_mu, n_aux, *args) if fits else general(*args)

    placed = (
        P("mu", None, "aux", None),
        P("mu", None, "aux"),
        P("mu", "aux"),
        P("mu", None),
        P("mu", None, "aux", None),
        P("mu", None, "aux"),
        P("mu", "aux"),
    )
    return jax.shard_map(
        shards, mesh=mesh, in_specs=placed, out_specs=P("aux", "mu"), check_vma=False
    )
```

```python
import functools

import jax
import jax.numpy as jnp
from jax import lax
from jax.experimental import pallas as pl
from jax.experimental.pallas import tpu as pltpu
from jax.sharding import PartitionSpec as P

F32 = jnp.float32
BF16 = jnp.bfloat16
VMEM = pl.BlockSpec(memory_space=pltpu.VMEM)
SMEM = pl.BlockSpec(memory_space=pltpu.SMEM)
ANY = pl.BlockSpec(memory_space=pl.ANY)
HBM = pl.BlockSpec(memory_space=pltpu.HBM)


DENSITY_ORDER = (2, 3, 1)
HALF_ORDER = (0, 2, 3, 1)


def by_distance(refs, order):
    return [refs[0]] + [refs[1 + order.index(s)] for s in range(1, len(refs))]


def params(mib):
    return pltpu.CompilerParams(vmem_limit_bytes=mib * 1024 * 1024)


def split(x):
    hi = x.astype(BF16)
    return hi, (x - hi.astype(F32)).astype(BF16)


def iota(shape, dim):
    return lax.broadcasted_iota(jnp.int32, shape, dim)


def tensor_kernel(tensor, packed, buffer, arrived):
    _, slots, aux_width, width = tensor.shape
    parts = buffer.shape[0] // slots
    span = width // parts

    def fetch(k, part):
        return pltpu.make_async_copy(
            tensor.at[0, k, :, pl.ds(part * span, span)],
            buffer.at[k * parts + part],
            arrived.at[k * parts + part],
        )

    order = [(k, part) for k in range(slots) for part in range(parts)]
    for k, part in order:
        fetch(k, part).start()
    for k, part in order:
        fetch(k, part).wait()
        for chunk in range(span // 128):
            hi, lo = split(buffer[k * parts + part, :, chunk * 128:(chunk + 1) * 128])
            at = (part * (span // 128) + chunk) * aux_width
            packed[at:at + aux_width, k * 256:k * 256 + 128] = hi
            packed[at:at + aux_width, k * 256 + 128:(k + 1) * 256] = lo


def metric_kernel(sig_slots, sig_count, after, metric, placed):
    depth = placed.shape[0] // 2
    m_hi, m_lo = placed.at[pl.ds(0, depth)], placed.at[pl.ds(depth, depth)]
    _, sig, aux_width, width = metric.shape
    half = iota((aux_width, 128), 1) >= 64
    pair_of = jnp.where(half, 1, 0)
    targets = [jnp.where(q < sig_count[0, 0], sig_slots[0, 0, q], -1) for q in range(sig)]
    for pair in range(width // 128):
        sums = [[jnp.zeros((aux_width, 128), F32) for _ in range(2)] for _ in range(2)]
        for q in range(sig):
            block = metric[0, q, :, pair * 128:(pair + 1) * 128]
            turned = pltpu.roll(block, 64, 1)
            both = (jnp.where(half, turned, block), jnp.where(half, block, turned))
            for out_half in range(2):
                here = pair_of + 2 * out_half == targets[q]
                for parity in range(2):
                    sums[parity][out_half] += jnp.where(here, both[parity], 0.0)
        for parity in range(2):
            r = 2 * pair + parity
            at = ((r % 8) * 2 + r // 8) * aux_width
            for out_half in range(2):
                hi, lo = split(sums[parity][out_half])
                columns = slice(out_half * 128, (out_half + 1) * 128)
                m_hi[at:at + aux_width, columns] = hi
                m_lo[at:at + aux_width, columns] = lo


def half_kernel(n_mu, nu_slots, nu_count, *refs):
    dens = by_distance(refs[:n_mu], DENSITY_ORDER)
    packed = refs[n_mu]
    outs = refs[n_mu + 1:2 * n_mu + 1]
    d_both, weights, turned = refs[2 * n_mu + 1:]
    z = lax.axis_index("mu")
    orb, lam_all = dens[0].shape
    lam = lam_all // n_mu
    slots = nu_slots.shape[2]
    row, col = iota((lam_all, 128), 0), iota((lam_all, 128), 1)
    group = z
    for slot in range(1, n_mu):
        group = jnp.where((col >> 3) & 3 == slot, z ^ HALF_ORDER[slot], group)
    wanted = group * lam + (col >> 6) * 8 + (col & 7)
    choose = jnp.where(row == wanted, 1.0, 0.0).astype(BF16)
    for s in range(n_mu):
        hi, lo = split(dens[s][...])
        d_both[s, :, :128] = jnp.dot(hi, choose, preferred_element_type=F32)
        d_both[s, :, 128:] = jnp.dot(lo, choose, preferred_element_type=F32)
    orbital = (iota((orb, 256), 1) >> 5) & 1
    for k in range(slots):
        live = jnp.where(k < nu_count[0, 0], 1.0, 0.0)
        both = d_both[z ^ nu_slots[0, 0, k]] * live
        for i in range(2):
            block = jnp.where(orbital == i, both, 0.0).astype(BF16)
            for part in range(2):
                at = k * 256 + part * 128 + i * orb
                weights[at:at + orb, :] = block
    aux_width = outs[0].shape[1] // lam
    lower = iota((aux_width, 128), 1) < 64
    group_rows = packed.shape[0] // 2
    per_group = group_rows // (2 * aux_width)
    span = per_group * 4
    for part in range(packed.shape[0] // group_rows):
        product = jnp.dot(
            packed[part * group_rows:(part + 1) * group_rows, :],
            weights[...],
            preferred_element_type=F32,
        )
        total = product[:, :128] + product[:, 128:]
        for chunk in range(per_group):
            at = chunk * 2 * aux_width
            one, two = total[at:at + aux_width], total[at + aux_width:at + 2 * aux_width]
            top = jnp.where(lower, one, pltpu.roll(two, 64, 1))
            bottom = jnp.where(lower, pltpu.roll(one, 64, 1), two)
            at = (part * per_group + chunk) * 128
            turned[at:at + 128, :] = jnp.concatenate([top, bottom], axis=0).T
        for s in range(n_mu):
            for r in range(8):
                picked = turned[pl.ds(part * per_group * 128 + s * 8 + r, span, stride=32), :]
                outs[s][part * span:(part + 1) * span, r * 128:(r + 1) * 128] = picked.astype(BF16)


def exchange_kernel(n_mu, n_aux, *refs):
    halves = refs[:n_mu]
    placed, out, total = refs[n_mu:]
    z = lax.axis_index("mu")
    left = jnp.concatenate([h[...] for h in halves], axis=0)
    left = jnp.concatenate([left, left], axis=1)
    product = jnp.dot(left, placed[...], preferred_element_type=F32)
    orb = halves[0].shape[0]
    for s in range(n_mu):
        block = z ^ HALF_ORDER[s]
        total[pl.ds(pl.multiple_of(block * orb, orb), orb), :] = product[s * orb:(s + 1) * orb]
    rows = out.shape[1]
    lower = iota((rows, 128), 1) < 64
    for a in range(n_aux):
        for pair in range(n_mu // 2):
            columns = slice(pair * 128, (pair + 1) * 128)
            top = total[a * 2 * rows:(a * 2 + 1) * rows, columns]
            bottom = total[(a * 2 + 1) * rows:(a * 2 + 2) * rows, columns]
            at = n_aux * n_mu - 1 - (a * n_mu + pair * 2)
            out[at] = jnp.where(lower, top, pltpu.roll(bottom, 64, 1)).astype(BF16)
            out[at - 1] = jnp.where(lower, pltpu.roll(top, 64, 1), bottom).astype(BF16)


def sum_kernel(parts, out):
    total = parts[0].astype(F32)
    for d in range(1, parts.shape[0]):
        total += parts[d].astype(F32)
    rows = parts.shape[1]
    out[:rows, :] = total[:, :64]
    out[rows:, :] = total[:, 64:]


def fast(n_mu, n_aux, three_center, nu_slots, nu_count, density, metric_tensor, sig_slots, sig_count):
    orb, lam_all = density.shape
    slots, aux_width = three_center.shape[1:3]
    lam = lam_all // n_mu
    turns = [[(z, z ^ s) for z in range(n_mu)] for s in range(n_mu)]
    dens = [density] + [lax.ppermute(density, "mu", turns[s]) for s in DENSITY_ORDER]
    nu_slots, sig_slots = jnp.swapaxes(nu_slots, 1, 2), jnp.swapaxes(sig_slots, 1, 2)
    chunks = three_center.shape[3] // 256
    t_shape = jax.ShapeDtypeStruct((2 * chunks * aux_width, slots * 256), BF16)
    m_shape = jax.ShapeDtypeStruct((2 * lam * aux_width, n_mu * orb), BF16)
    packed = pl.pallas_call(
        tensor_kernel,
        out_shape=t_shape,
        in_specs=[HBM],
        out_specs=VMEM,
        scratch_shapes=[
            pltpu.VMEM((slots * 4, aux_width, chunks * 64), F32),
            pltpu.SemaphoreType.DMA((slots * 4,)),
        ],
        compiler_params=params(50),
        cost_estimate=pl.CostEstimate(flops=10_000_000, bytes_accessed=6_000_000, transcendentals=0),
        name="tensor",
    )(three_center)
    half_shape = jax.ShapeDtypeStruct((orb, lam * aux_width), BF16)
    halves = pl.pallas_call(
        functools.partial(half_kernel, n_mu),
        out_shape=(half_shape,) * n_mu,
        in_specs=[SMEM, SMEM] + [VMEM] * (n_mu + 1),
        out_specs=(VMEM,) * n_mu,
        scratch_shapes=[
            pltpu.VMEM((n_mu, orb, 256), F32),
            pltpu.VMEM((slots * 256, 256), BF16),
            pltpu.VMEM((chunks * 128, 128), F32),
        ],
        compiler_params=params(16),
        cost_estimate=pl.CostEstimate(flops=1_200_000_000, bytes_accessed=4_000_000, transcendentals=0),
        name="half",
    )(nu_slots, nu_count, *dens, packed)
    placed = pl.pallas_call(
        metric_kernel,
        out_shape=m_shape,
        in_specs=[SMEM, SMEM, ANY, VMEM],
        out_specs=VMEM,
        compiler_params=params(16),
        cost_estimate=pl.CostEstimate(flops=10_000_000, bytes_accessed=2_000_000, transcendentals=0),
        name="metric",
    )(sig_slots, sig_count, halves[0], metric_tensor)
    halves = [halves[0]] + [
        lax.ppermute(halves[s], "mu", turns[HALF_ORDER[s]]) for s in range(1, n_mu)
    ]
    rows = n_mu * orb // n_aux
    parts = pl.pallas_call(
        functools.partial(exchange_kernel, n_mu, n_aux),
        out_shape=jax.ShapeDtypeStruct((n_aux * n_mu, rows // 2, 128), BF16),
        in_specs=[VMEM] * (n_mu + 1),
        out_specs=VMEM,
        scratch_shapes=[pltpu.VMEM((n_mu * orb, n_mu * orb), F32)],
        compiler_params=params(16),
        cost_estimate=pl.CostEstimate(flops=300_000_000, bytes_accessed=2_000_000, transcendentals=0),
        name="exchange",
    )(*halves, placed)
    down = list(reversed(range(n_aux * n_mu)))
    parts = lax.all_to_all(parts, ("aux", "mu"), 0, 0, axis_index_groups=[down])
    return pl.pallas_call(
        sum_kernel,
        out_shape=jax.ShapeDtypeStruct((rows, orb), F32),
        in_specs=[VMEM],
        out_specs=VMEM,
        compiler_params=params(8),
        name="sum",
    )(parts)


def general(three_center, nu_slots, nu_count, density, metric_tensor, sig_slots, sig_count):
    highest = lax.Precision.HIGHEST
    orb_block = density.shape[0]
    lam_all = density.shape[1]
    aux_width = three_center.shape[2]
    dens_all = lax.all_gather(density, "mu", axis=0, tiled=True)

    def add_slot(k, running):
        nu_pick = nu_slots[0, k, 0]
        dens_rows = lax.dynamic_slice_in_dim(dens_all, nu_pick * orb_block, orb_block, 0)
        slab_piece = lax.dynamic_index_in_dim(three_center[0], k, 0, keepdims=False).reshape(
            aux_width, orb_block, orb_block
        )
        return running + jnp.einsum("pij,jl->lpi", slab_piece, dens_rows, precision=highest)

    halfway = lax.fori_loop(
        0, nu_count[0, 0], add_slot, jnp.zeros((lam_all, aux_width, orb_block), F32)
    )
    relayed = lax.all_to_all(halfway.astype(BF16), "mu", split_axis=0, concat_axis=2, tiled=True)
    widened = relayed.astype(F32)
    lam_rows = relayed.shape[0]
    orbitals = relayed.shape[2]

    def add_target(q, running):
        target = sig_slots[0, q, 0]
        weights = lax.dynamic_index_in_dim(metric_tensor[0], q, 0, keepdims=False).reshape(
            aux_width, lam_rows, orb_block
        )
        contrib = jnp.einsum("rpm,prc->mc", widened, weights, precision=highest)
        current = lax.dynamic_slice_in_dim(running, target * orb_block, orb_block, 1)
        return lax.dynamic_update_slice_in_dim(running, current + contrib, target * orb_block, 1)

    partial_k = lax.fori_loop(
        0, sig_count[0, 0], add_target, jnp.zeros((orbitals, orbitals), F32)
    )
    row_share = lax.psum_scatter(partial_k, "aux", scatter_dimension=0, tiled=True)
    return lax.psum_scatter(row_share, "mu", scatter_dimension=1, tiled=True)


def solution(mesh):
    n_aux, n_mu = mesh.shape["aux"], mesh.shape["mu"]

    def shards(three_center, nu_slots, nu_count, density, metric_tensor, sig_slots, sig_count):
        args = (three_center, nu_slots, nu_count, density, metric_tensor, sig_slots, sig_count)
        orb, lam_all = density.shape
        fits = (
            (n_aux, n_mu, orb, lam_all) == (8, 4, 64, 64)
            and three_center.shape[2:] == (64, orb * orb)
            and metric_tensor.shape[2:] == (64, lam_all // n_mu * orb)
        )
        return fast(n_mu, n_aux, *args) if fits else general(*args)

    placed = (
        P("mu", None, "aux", None),
        P("mu", None, "aux"),
        P("mu", "aux"),
        P("mu", None),
        P("mu", None, "aux", None),
        P("mu", None, "aux"),
        P("mu", "aux"),
    )
    return jax.shard_map(
        shards, mesh=mesh, in_specs=placed, out_specs=P("aux", "mu"), check_vma=False
    )
```

```python
import functools

import jax
import jax.numpy as jnp
from jax import lax
from jax.experimental import pallas as pl
from jax.experimental.pallas import tpu as pltpu
from jax.sharding import PartitionSpec as P

F32 = jnp.float32
BF16 = jnp.bfloat16
VMEM = pl.BlockSpec(memory_space=pltpu.VMEM)
SMEM = pl.BlockSpec(memory_space=pltpu.SMEM)
ANY = pl.BlockSpec(memory_space=pl.ANY)
HBM = pl.BlockSpec(memory_space=pltpu.HBM)


DENSITY_ORDER = (2, 3, 1)
HALF_ORDER = (0, 2, 3, 1)


def by_distance(refs, order):
    return [refs[0]] + [refs[1 + order.index(s)] for s in range(1, len(refs))]


def params(mib):
    return pltpu.CompilerParams(vmem_limit_bytes=mib * 1024 * 1024)


def split(x):
    hi = x.astype(BF16)
    return hi, (x - hi.astype(F32)).astype(BF16)


def iota(shape, dim):
    return lax.broadcasted_iota(jnp.int32, shape, dim)


def tensor_kernel(tensor, packed, buffer, arrived):
    _, slots, aux_width, width = tensor.shape
    parts = buffer.shape[0] // slots
    span = width // parts

    def fetch(k, part):
        return pltpu.make_async_copy(
            tensor.at[0, k, :, pl.ds(part * span, span)],
            buffer.at[k * parts + part],
            arrived.at[k * parts + part],
        )

    order = [(k, part) for k in range(slots) for part in range(parts)]
    for k, part in order:
        fetch(k, part).start()
    for k, part in order:
        fetch(k, part).wait()
        for chunk in range(span // 128):
            hi, lo = split(buffer[k * parts + part, :, chunk * 128:(chunk + 1) * 128])
            at = (part * (span // 128) + chunk) * aux_width
            packed[at:at + aux_width, k * 256:k * 256 + 128] = hi
            packed[at:at + aux_width, k * 256 + 128:(k + 1) * 256] = lo


def metric_kernel(sig_slots, sig_count, after, metric, m_hi, m_lo):
    _, sig, aux_width, width = metric.shape
    half = iota((aux_width, 128), 1) >= 64
    pair_of = jnp.where(half, 1, 0)
    targets = [jnp.where(q < sig_count[0, 0], sig_slots[0, 0, q], -1) for q in range(sig)]
    for pair in range(width // 128):
        sums = [[jnp.zeros((aux_width, 128), F32) for _ in range(2)] for _ in range(2)]
        for q in range(sig):
            block = metric[0, q, :, pair * 128:(pair + 1) * 128]
            turned = pltpu.roll(block, 64, 1)
            both = (jnp.where(half, turned, block), jnp.where(half, block, turned))
            for out_half in range(2):
                here = pair_of + 2 * out_half == targets[q]
                for parity in range(2):
                    sums[parity][out_half] += jnp.where(here, both[parity], 0.0)
        for parity in range(2):
            r = 2 * pair + parity
            at = ((r % 8) * 2 + r // 8) * aux_width
            for out_half in range(2):
                hi, lo = split(sums[parity][out_half])
                columns = slice(out_half * 128, (out_half + 1) * 128)
                m_hi[at:at + aux_width, columns] = hi
                m_lo[at:at + aux_width, columns] = lo


def half_kernel(n_mu, nu_slots, nu_count, *refs):
    dens = by_distance(refs[:n_mu], DENSITY_ORDER)
    packed = refs[n_mu]
    outs = refs[n_mu + 1:2 * n_mu + 1]
    d_both, weights, turned = refs[2 * n_mu + 1:]
    z = lax.axis_index("mu")
    orb, lam_all = dens[0].shape
    lam = lam_all // n_mu
    slots = nu_slots.shape[2]
    row, col = iota((lam_all, 128), 0), iota((lam_all, 128), 1)
    group = z
    for slot in range(1, n_mu):
        group = jnp.where((col >> 3) & 3 == slot, z ^ HALF_ORDER[slot], group)
    wanted = group * lam + (col >> 6) * 8 + (col & 7)
    choose = jnp.where(row == wanted, 1.0, 0.0).astype(BF16)
    for s in range(n_mu):
        hi, lo = split(dens[s][...])
        d_both[s, :, :128] = jnp.dot(hi, choose, preferred_element_type=F32)
        d_both[s, :, 128:] = jnp.dot(lo, choose, preferred_element_type=F32)
    orbital = (iota((orb, 256), 1) >> 5) & 1
    for k in range(slots):
        live = jnp.where(k < nu_count[0, 0], 1.0, 0.0)
        both = d_both[z ^ nu_slots[0, 0, k]] * live
        for i in range(2):
            block = jnp.where(orbital == i, both, 0.0).astype(BF16)
            for part in range(2):
                at = k * 256 + part * 128 + i * orb
                weights[at:at + orb, :] = block
    aux_width = outs[0].shape[1] // lam
    lower = iota((aux_width, 128), 1) < 64
    per_group = 512 // (2 * aux_width)
    span = per_group * 4
    for part in range(packed.shape[0] // 512):
        for chunk in range(per_group):
            if chunk % 2 == 0:
                first = part * 512 + chunk * 2 * aux_width
                product = jnp.dot(
                    packed[first:first + 256, :], weights[...], preferred_element_type=F32
                )
                total = product[:, :128] + product[:, 128:]
            at = chunk % 2 * 2 * aux_width
            one, two = total[at:at + aux_width], total[at + aux_width:at + 2 * aux_width]
            top = jnp.where(lower, one, pltpu.roll(two, 64, 1))
            bottom = jnp.where(lower, pltpu.roll(one, 64, 1), two)
            at = (part * per_group + chunk) * 128
            turned[at:at + 128, :] = jnp.concatenate([top, bottom], axis=0).T
        for s in range(n_mu):
            for r in range(8):
                picked = turned[pl.ds(part * per_group * 128 + s * 8 + r, span, stride=32), :]
                outs[s][part * span:(part + 1) * span, r * 128:(r + 1) * 128] = picked.astype(BF16)


def exchange_kernel(n_mu, n_aux, *refs):
    halves = refs[:n_mu]
    m_hi, m_lo, out, total = refs[n_mu:]
    z = lax.axis_index("mu")
    left = jnp.concatenate([h[...] for h in halves], axis=0)
    product = jnp.dot(left, m_hi[...], preferred_element_type=F32)
    product += jnp.dot(left, m_lo[...], preferred_element_type=F32)
    orb = halves[0].shape[0]
    for s in range(n_mu):
        block = z ^ HALF_ORDER[s]
        total[pl.ds(pl.multiple_of(block * orb, orb), orb), :] = product[s * orb:(s + 1) * orb]
    rows = out.shape[1]
    lower = iota((rows, 128), 1) < 64
    for a in range(n_aux):
        for pair in range(n_mu // 2):
            columns = slice(pair * 128, (pair + 1) * 128)
            top = total[a * 2 * rows:(a * 2 + 1) * rows, columns]
            bottom = total[(a * 2 + 1) * rows:(a * 2 + 2) * rows, columns]
            at = n_aux * n_mu - 1 - (a * n_mu + pair * 2)
            out[at] = jnp.where(lower, top, pltpu.roll(bottom, 64, 1)).astype(BF16)
            out[at - 1] = jnp.where(lower, pltpu.roll(top, 64, 1), bottom).astype(BF16)


def sum_kernel(parts, out):
    total = parts[0].astype(F32)
    for d in range(1, parts.shape[0]):
        total += parts[d].astype(F32)
    rows = parts.shape[1]
    out[:rows, :] = total[:, :64]
    out[rows:, :] = total[:, 64:]


def fast(n_mu, n_aux, three_center, nu_slots, nu_count, density, metric_tensor, sig_slots, sig_count):
    orb, lam_all = density.shape
    slots, aux_width = three_center.shape[1:3]
    lam = lam_all // n_mu
    turns = [[(z, z ^ s) for z in range(n_mu)] for s in range(n_mu)]
    dens = [density] + [lax.ppermute(density, "mu", turns[s]) for s in DENSITY_ORDER]
    nu_slots, sig_slots = jnp.swapaxes(nu_slots, 1, 2), jnp.swapaxes(sig_slots, 1, 2)
    chunks = three_center.shape[3] // 256
    t_shape = jax.ShapeDtypeStruct((2 * chunks * aux_width, slots * 256), BF16)
    m_shape = jax.ShapeDtypeStruct((lam * aux_width, n_mu * orb), BF16)
    packed = pl.pallas_call(
        tensor_kernel,
        out_shape=t_shape,
        in_specs=[HBM],
        out_specs=VMEM,
        scratch_shapes=[
            pltpu.VMEM((slots * 4, aux_width, chunks * 64), F32),
            pltpu.SemaphoreType.DMA((slots * 4,)),
        ],
        compiler_params=params(50),
        cost_estimate=pl.CostEstimate(flops=10_000_000, bytes_accessed=6_000_000, transcendentals=0),
        name="tensor",
    )(three_center)
    half_shape = jax.ShapeDtypeStruct((orb, lam * aux_width), BF16)
    halves = pl.pallas_call(
        functools.partial(half_kernel, n_mu),
        out_shape=(half_shape,) * n_mu,
        in_specs=[SMEM, SMEM] + [VMEM] * (n_mu + 1),
        out_specs=(VMEM,) * n_mu,
        scratch_shapes=[
            pltpu.VMEM((n_mu, orb, 256), F32),
            pltpu.VMEM((slots * 256, 256), BF16),
            pltpu.VMEM((chunks * 128, 128), F32),
        ],
        compiler_params=params(16),
        cost_estimate=pl.CostEstimate(flops=1_200_000_000, bytes_accessed=4_000_000, transcendentals=0),
        name="half",
    )(nu_slots, nu_count, *dens, packed)
    m_hi, m_lo = pl.pallas_call(
        metric_kernel,
        out_shape=(m_shape, m_shape),
        in_specs=[SMEM, SMEM, ANY, VMEM],
        out_specs=(VMEM, VMEM),
        compiler_params=params(16),
        cost_estimate=pl.CostEstimate(flops=10_000_000, bytes_accessed=2_000_000, transcendentals=0),
        name="metric",
    )(sig_slots, sig_count, halves[0], metric_tensor)
    halves = [halves[0]] + [
        lax.ppermute(halves[s], "mu", turns[HALF_ORDER[s]]) for s in range(1, n_mu)
    ]
    rows = n_mu * orb // n_aux
    parts = pl.pallas_call(
        functools.partial(exchange_kernel, n_mu, n_aux),
        out_shape=jax.ShapeDtypeStruct((n_aux * n_mu, rows // 2, 128), BF16),
        in_specs=[VMEM] * (n_mu + 2),
        out_specs=VMEM,
        scratch_shapes=[pltpu.VMEM((n_mu * orb, n_mu * orb), F32)],
        compiler_params=params(16),
        cost_estimate=pl.CostEstimate(flops=300_000_000, bytes_accessed=2_000_000, transcendentals=0),
        name="exchange",
    )(*halves, m_hi, m_lo)
    down = list(reversed(range(n_aux * n_mu)))
    parts = lax.all_to_all(parts, ("aux", "mu"), 0, 0, axis_index_groups=[down])
    return pl.pallas_call(
        sum_kernel,
        out_shape=jax.ShapeDtypeStruct((rows, orb), F32),
        in_specs=[VMEM],
        out_specs=VMEM,
        compiler_params=params(8),
        name="sum",
    )(parts)


def general(three_center, nu_slots, nu_count, density, metric_tensor, sig_slots, sig_count):
    highest = lax.Precision.HIGHEST
    orb_block = density.shape[0]
    lam_all = density.shape[1]
    aux_width = three_center.shape[2]
    dens_all = lax.all_gather(density, "mu", axis=0, tiled=True)

    def add_slot(k, running):
        nu_pick = nu_slots[0, k, 0]
        dens_rows = lax.dynamic_slice_in_dim(dens_all, nu_pick * orb_block, orb_block, 0)
        slab_piece = lax.dynamic_index_in_dim(three_center[0], k, 0, keepdims=False).reshape(
            aux_width, orb_block, orb_block
        )
        return running + jnp.einsum("pij,jl->lpi", slab_piece, dens_rows, precision=highest)

    halfway = lax.fori_loop(
        0, nu_count[0, 0], add_slot, jnp.zeros((lam_all, aux_width, orb_block), F32)
    )
    relayed = lax.all_to_all(halfway.astype(BF16), "mu", split_axis=0, concat_axis=2, tiled=True)
    widened = relayed.astype(F32)
    lam_rows = relayed.shape[0]
    orbitals = relayed.shape[2]

    def add_target(q, running):
        target = sig_slots[0, q, 0]
        weights = lax.dynamic_index_in_dim(metric_tensor[0], q, 0, keepdims=False).reshape(
            aux_width, lam_rows, orb_block
        )
        contrib = jnp.einsum("rpm,prc->mc", widened, weights, precision=highest)
        current = lax.dynamic_slice_in_dim(running, target * orb_block, orb_block, 1)
        return lax.dynamic_update_slice_in_dim(running, current + contrib, target * orb_block, 1)

    partial_k = lax.fori_loop(
        0, sig_count[0, 0], add_target, jnp.zeros((orbitals, orbitals), F32)
    )
    row_share = lax.psum_scatter(partial_k, "aux", scatter_dimension=0, tiled=True)
    return lax.psum_scatter(row_share, "mu", scatter_dimension=1, tiled=True)


def solution(mesh):
    n_aux, n_mu = mesh.shape["aux"], mesh.shape["mu"]

    def shards(three_center, nu_slots, nu_count, density, metric_tensor, sig_slots, sig_count):
        args = (three_center, nu_slots, nu_count, density, metric_tensor, sig_slots, sig_count)
        orb, lam_all = density.shape
        fits = (
            (n_aux, n_mu, orb, lam_all) == (8, 4, 64, 64)
            and three_center.shape[2:] == (64, orb * orb)
            and metric_tensor.shape[2:] == (64, lam_all // n_mu * orb)
        )
        return fast(n_mu, n_aux, *args) if fits else general(*args)

    placed = (
        P("mu", None, "aux", None),
        P("mu", None, "aux"),
        P("mu", "aux"),
        P("mu", None),
        P("mu", None, "aux", None),
        P("mu", None, "aux"),
        P("mu", "aux"),
    )
    return jax.shard_map(
        shards, mesh=mesh, in_specs=placed, out_specs=P("aux", "mu"), check_vma=False
    )
```

```python
import functools

import jax
import jax.numpy as jnp
from jax import lax
from jax.experimental import pallas as pl
from jax.experimental.pallas import tpu as pltpu
from jax.sharding import PartitionSpec as P

F32 = jnp.float32
BF16 = jnp.bfloat16
VMEM = pl.BlockSpec(memory_space=pltpu.VMEM)
SMEM = pl.BlockSpec(memory_space=pltpu.SMEM)
ANY = pl.BlockSpec(memory_space=pl.ANY)
HBM = pl.BlockSpec(memory_space=pltpu.HBM)


DENSITY_ORDER = (2, 3, 1)
HALF_ORDER = (0, 2, 3, 1)


def by_distance(refs, order):
    return [refs[0]] + [refs[1 + order.index(s)] for s in range(1, len(refs))]


def params(mib):
    return pltpu.CompilerParams(vmem_limit_bytes=mib * 1024 * 1024)


def split(x):
    hi = x.astype(BF16)
    return hi, (x - hi.astype(F32)).astype(BF16)


def iota(shape, dim):
    return lax.broadcasted_iota(jnp.int32, shape, dim)


def tensor_kernel(tensor, packed, buffer, arrived):
    _, slots, aux_width, width = tensor.shape
    parts = buffer.shape[0] // slots
    span = width // parts

    def fetch(k, part):
        return pltpu.make_async_copy(
            tensor.at[0, k, :, pl.ds(part * span, span)],
            buffer.at[k * parts + part],
            arrived.at[k * parts + part],
        )

    order = [(k, part) for k in range(slots) for part in range(parts)]
    for k, part in order:
        fetch(k, part).start()
    for k, part in order:
        fetch(k, part).wait()
        for chunk in range(span // 128):
            hi, lo = split(buffer[k * parts + part, :, chunk * 128:(chunk + 1) * 128])
            at = (part * (span // 128) + chunk) * aux_width
            packed[at:at + aux_width, k * 256:k * 256 + 128] = hi
            packed[at:at + aux_width, k * 256 + 128:(k + 1) * 256] = lo


def metric_kernel(sig_slots, sig_count, after, metric, m_hi, m_lo):
    _, sig, aux_width, width = metric.shape
    half = iota((aux_width, 128), 1) >= 64
    pair_of = jnp.where(half, 1, 0)
    targets = [jnp.where(q < sig_count[0, 0], sig_slots[0, 0, q], -1) for q in range(sig)]
    for pair in range(width // 128):
        sums = [[jnp.zeros((aux_width, 128), F32) for _ in range(2)] for _ in range(2)]
        for q in range(sig):
            block = metric[0, q, :, pair * 128:(pair + 1) * 128]
            turned = pltpu.roll(block, 64, 1)
            both = (jnp.where(half, turned, block), jnp.where(half, block, turned))
            for out_half in range(2):
                here = pair_of + 2 * out_half == targets[q]
                for parity in range(2):
                    sums[parity][out_half] += jnp.where(here, both[parity], 0.0)
        for parity in range(2):
            r = 2 * pair + parity
            at = ((r % 8) * 2 + r // 8) * aux_width
            for out_half in range(2):
                hi, lo = split(sums[parity][out_half])
                columns = slice(out_half * 128, (out_half + 1) * 128)
                m_hi[at:at + aux_width, columns] = hi
                m_lo[at:at + aux_width, columns] = lo


def half_kernel(n_mu, nu_slots, nu_count, *refs):
    dens = by_distance(refs[:n_mu], DENSITY_ORDER)
    packed = refs[n_mu]
    outs = refs[n_mu + 1:2 * n_mu + 1]
    d_both, weights, turned = refs[2 * n_mu + 1:]
    z = lax.axis_index("mu")
    orb, lam_all = dens[0].shape
    lam = lam_all // n_mu
    slots = nu_slots.shape[2]
    row, col = iota((lam_all, 128), 0), iota((lam_all, 128), 1)
    group = z
    for slot in range(1, n_mu):
        group = jnp.where((col >> 3) & 3 == slot, z ^ HALF_ORDER[slot], group)
    wanted = group * lam + (col >> 6) * 8 + (col & 7)
    choose = jnp.where(row == wanted, 1.0, 0.0).astype(BF16)
    for s in range(n_mu):
        hi, lo = split(dens[s][...])
        d_both[s, :, :128] = jnp.dot(hi, choose, preferred_element_type=F32)
        d_both[s, :, 128:] = jnp.dot(lo, choose, preferred_element_type=F32)
    orbital = (iota((orb, 256), 1) >> 5) & 1
    for k in range(slots):
        live = jnp.where(k < nu_count[0, 0], 1.0, 0.0)
        both = d_both[z ^ nu_slots[0, 0, k]] * live
        for i in range(2):
            block = jnp.where(orbital == i, both, 0.0).astype(BF16)
            for part in range(2):
                at = k * 256 + part * 128 + i * orb
                weights[at:at + orb, :] = block
    aux_width = outs[0].shape[1] // lam
    lower = iota((aux_width, 128), 1) < 64
    per_group = 512 // (2 * aux_width)
    span = per_group * 4
    for part in range(packed.shape[0] // 512):
        product = jnp.dot(
            packed[part * 512:(part + 1) * 512, :], weights[...], preferred_element_type=F32
        )
        total = product[:, :128] + product[:, 128:]
        for chunk in range(per_group):
            at = chunk * 2 * aux_width
            one, two = total[at:at + aux_width], total[at + aux_width:at + 2 * aux_width]
            top = jnp.where(lower, one, pltpu.roll(two, 64, 1))
            bottom = jnp.where(lower, pltpu.roll(one, 64, 1), two)
            at = (part * per_group + chunk) * 128
            turned[at:at + 128, :] = jnp.concatenate([top, bottom], axis=0).T
        for s in range(n_mu):
            for r in range(8):
                picked = turned[pl.ds(part * per_group * 128 + s * 8 + r, span, stride=32), :]
                outs[s][part * span:(part + 1) * span, r * 128:(r + 1) * 128] = picked.astype(BF16)


def exchange_kernel(n_mu, n_aux, *refs):
    halves = refs[:n_mu]
    m_hi, m_lo, out, total = refs[n_mu:]
    z = lax.axis_index("mu")
    left = jnp.concatenate([h[...] for h in halves], axis=0)
    product = jnp.dot(left, m_hi[...], preferred_element_type=F32)
    product += jnp.dot(left, m_lo[...], preferred_element_type=F32)
    orb = halves[0].shape[0]
    for s in range(n_mu):
        block = z ^ HALF_ORDER[s]
        total[pl.ds(pl.multiple_of(block * orb, orb), orb), :] = product[s * orb:(s + 1) * orb]
    rows = out.shape[1]
    lower = iota((rows, 128), 1) < 64
    for a in range(n_aux):
        for pair in range(n_mu // 2):
            columns = slice(pair * 128, (pair + 1) * 128)
            top = total[a * 2 * rows:(a * 2 + 1) * rows, columns]
            bottom = total[(a * 2 + 1) * rows:(a * 2 + 2) * rows, columns]
            at = a * n_mu + pair * 2
            out[at] = jnp.where(lower, top, pltpu.roll(bottom, 64, 1)).astype(BF16)
            out[at + 1] = jnp.where(lower, pltpu.roll(top, 64, 1), bottom).astype(BF16)


def sum_kernel(parts, out):
    total = parts[0].astype(F32)
    for d in range(1, parts.shape[0]):
        total += parts[d].astype(F32)
    rows = parts.shape[1]
    out[:rows, :] = total[:, :64]
    out[rows:, :] = total[:, 64:]


def fast(n_mu, n_aux, three_center, nu_slots, nu_count, density, metric_tensor, sig_slots, sig_count):
    orb, lam_all = density.shape
    slots, aux_width = three_center.shape[1:3]
    lam = lam_all // n_mu
    turns = [[(z, z ^ s) for z in range(n_mu)] for s in range(n_mu)]
    dens = [density] + [lax.ppermute(density, "mu", turns[s]) for s in DENSITY_ORDER]
    nu_slots, sig_slots = jnp.swapaxes(nu_slots, 1, 2), jnp.swapaxes(sig_slots, 1, 2)
    chunks = three_center.shape[3] // 256
    t_shape = jax.ShapeDtypeStruct((2 * chunks * aux_width, slots * 256), BF16)
    m_shape = jax.ShapeDtypeStruct((lam * aux_width, n_mu * orb), BF16)
    packed = pl.pallas_call(
        tensor_kernel,
        out_shape=t_shape,
        in_specs=[HBM],
        out_specs=VMEM,
        scratch_shapes=[
            pltpu.VMEM((slots * 4, aux_width, chunks * 64), F32),
            pltpu.SemaphoreType.DMA((slots * 4,)),
        ],
        compiler_params=params(50),
        cost_estimate=pl.CostEstimate(flops=10_000_000, bytes_accessed=6_000_000, transcendentals=0),
        name="tensor",
    )(three_center)
    half_shape = jax.ShapeDtypeStruct((orb, lam * aux_width), BF16)
    halves = pl.pallas_call(
        functools.partial(half_kernel, n_mu),
        out_shape=(half_shape,) * n_mu,
        in_specs=[SMEM, SMEM] + [VMEM] * (n_mu + 1),
        out_specs=(VMEM,) * n_mu,
        scratch_shapes=[
            pltpu.VMEM((n_mu, orb, 256), F32),
            pltpu.VMEM((slots * 256, 256), BF16),
            pltpu.VMEM((chunks * 128, 128), F32),
        ],
        compiler_params=params(16),
        cost_estimate=pl.CostEstimate(flops=1_200_000_000, bytes_accessed=4_000_000, transcendentals=0),
        name="half",
    )(nu_slots, nu_count, *dens, packed)
    m_hi, m_lo = pl.pallas_call(
        metric_kernel,
        out_shape=(m_shape, m_shape),
        in_specs=[SMEM, SMEM, ANY, VMEM],
        out_specs=(VMEM, VMEM),
        compiler_params=params(16),
        cost_estimate=pl.CostEstimate(flops=10_000_000, bytes_accessed=2_000_000, transcendentals=0),
        name="metric",
    )(sig_slots, sig_count, halves[0], metric_tensor)
    halves = [halves[0]] + [
        lax.ppermute(halves[s], "mu", turns[HALF_ORDER[s]]) for s in range(1, n_mu)
    ]
    rows = n_mu * orb // n_aux
    parts = pl.pallas_call(
        functools.partial(exchange_kernel, n_mu, n_aux),
        out_shape=jax.ShapeDtypeStruct((n_aux * n_mu, rows // 2, 128), BF16),
        in_specs=[VMEM] * (n_mu + 2),
        out_specs=VMEM,
        scratch_shapes=[pltpu.VMEM((n_mu * orb, n_mu * orb), F32)],
        compiler_params=params(16),
        cost_estimate=pl.CostEstimate(flops=300_000_000, bytes_accessed=2_000_000, transcendentals=0),
        name="exchange",
    )(*halves, m_hi, m_lo)
    parts = lax.all_to_all(parts, ("aux", "mu"), 0, 0)
    return pl.pallas_call(
        sum_kernel,
        out_shape=jax.ShapeDtypeStruct((rows, orb), F32),
        in_specs=[VMEM],
        out_specs=VMEM,
        compiler_params=params(8),
        name="sum",
    )(parts)


def general(three_center, nu_slots, nu_count, density, metric_tensor, sig_slots, sig_count):
    highest = lax.Precision.HIGHEST
    orb_block = density.shape[0]
    lam_all = density.shape[1]
    aux_width = three_center.shape[2]
    dens_all = lax.all_gather(density, "mu", axis=0, tiled=True)

    def add_slot(k, running):
        nu_pick = nu_slots[0, k, 0]
        dens_rows = lax.dynamic_slice_in_dim(dens_all, nu_pick * orb_block, orb_block, 0)
        slab_piece = lax.dynamic_index_in_dim(three_center[0], k, 0, keepdims=False).reshape(
            aux_width, orb_block, orb_block
        )
        return running + jnp.einsum("pij,jl->lpi", slab_piece, dens_rows, precision=highest)

    halfway = lax.fori_loop(
        0, nu_count[0, 0], add_slot, jnp.zeros((lam_all, aux_width, orb_block), F32)
    )
    relayed = lax.all_to_all(halfway.astype(BF16), "mu", split_axis=0, concat_axis=2, tiled=True)
    widened = relayed.astype(F32)
    lam_rows = relayed.shape[0]
    orbitals = relayed.shape[2]

    def add_target(q, running):
        target = sig_slots[0, q, 0]
        weights = lax.dynamic_index_in_dim(metric_tensor[0], q, 0, keepdims=False).reshape(
            aux_width, lam_rows, orb_block
        )
        contrib = jnp.einsum("rpm,prc->mc", widened, weights, precision=highest)
        current = lax.dynamic_slice_in_dim(running, target * orb_block, orb_block, 1)
        return lax.dynamic_update_slice_in_dim(running, current + contrib, target * orb_block, 1)

    partial_k = lax.fori_loop(
        0, sig_count[0, 0], add_target, jnp.zeros((orbitals, orbitals), F32)
    )
    row_share = lax.psum_scatter(partial_k, "aux", scatter_dimension=0, tiled=True)
    return lax.psum_scatter(row_share, "mu", scatter_dimension=1, tiled=True)


def solution(mesh):
    n_aux, n_mu = mesh.shape["aux"], mesh.shape["mu"]

    def shards(three_center, nu_slots, nu_count, density, metric_tensor, sig_slots, sig_count):
        args = (three_center, nu_slots, nu_count, density, metric_tensor, sig_slots, sig_count)
        orb, lam_all = density.shape
        fits = (
            (n_aux, n_mu, orb, lam_all) == (8, 4, 64, 64)
            and three_center.shape[2:] == (64, orb * orb)
            and metric_tensor.shape[2:] == (64, lam_all // n_mu * orb)
        )
        return fast(n_mu, n_aux, *args) if fits else general(*args)

    placed = (
        P("mu", None, "aux", None),
        P("mu", None, "aux"),
        P("mu", "aux"),
        P("mu", None),
        P("mu", None, "aux", None),
        P("mu", None, "aux"),
        P("mu", "aux"),
    )
    return jax.shard_map(
        shards, mesh=mesh, in_specs=placed, out_specs=P("aux", "mu"), check_vma=False
    )
```

```python
import functools

import jax
import jax.numpy as jnp
from jax import lax
from jax.experimental import pallas as pl
from jax.experimental.pallas import tpu as pltpu
from jax.sharding import PartitionSpec as P

F32 = jnp.float32
BF16 = jnp.bfloat16
VMEM = pl.BlockSpec(memory_space=pltpu.VMEM)
SMEM = pl.BlockSpec(memory_space=pltpu.SMEM)
ANY = pl.BlockSpec(memory_space=pl.ANY)
HBM = pl.BlockSpec(memory_space=pltpu.HBM)


DENSITY_ORDER = (2, 3, 1)
HALF_ORDER = (0, 2, 3, 1)


def by_distance(refs, order):
    return [refs[0]] + [refs[1 + order.index(s)] for s in range(1, len(refs))]


def params(mib):
    return pltpu.CompilerParams(vmem_limit_bytes=mib * 1024 * 1024)


def split(x):
    hi = x.astype(BF16)
    return hi, (x - hi.astype(F32)).astype(BF16)


def iota(shape, dim):
    return lax.broadcasted_iota(jnp.int32, shape, dim)


def tensor_kernel(tensor, packed, buffer, arrived):
    _, slots, aux_width, width = tensor.shape
    parts = buffer.shape[0] // slots
    span = width // parts

    def fetch(k, part):
        return pltpu.make_async_copy(
            tensor.at[0, k, :, pl.ds(part * span, span)],
            buffer.at[k * parts + part],
            arrived.at[k * parts + part],
        )

    order = [(k, part) for k in range(slots) for part in range(parts)]
    for k, part in order:
        fetch(k, part).start()
    for k, part in order:
        fetch(k, part).wait()
        for chunk in range(span // 128):
            hi, lo = split(buffer[k * parts + part, :, chunk * 128:(chunk + 1) * 128])
            at = (part * (span // 128) + chunk) * aux_width
            packed[at:at + aux_width, k * 256:k * 256 + 128] = hi
            packed[at:at + aux_width, k * 256 + 128:(k + 1) * 256] = lo


def metric_kernel(sig_slots, sig_count, after, metric, m_hi, m_lo):
    _, sig, aux_width, width = metric.shape
    half = iota((aux_width, 128), 1) >= 64
    pair_of = jnp.where(half, 1, 0)
    targets = [jnp.where(q < sig_count[0, 0], sig_slots[0, 0, q], -1) for q in range(sig)]
    for pair in range(width // 128):
        sums = [[jnp.zeros((aux_width, 128), F32) for _ in range(2)] for _ in range(2)]
        for q in range(sig):
            block = metric[0, q, :, pair * 128:(pair + 1) * 128]
            turned = pltpu.roll(block, 64, 1)
            both = (jnp.where(half, turned, block), jnp.where(half, block, turned))
            for out_half in range(2):
                here = pair_of + 2 * out_half == targets[q]
                for parity in range(2):
                    sums[parity][out_half] += jnp.where(here, both[parity], 0.0)
        for parity in range(2):
            r = 2 * pair + parity
            at = ((r % 8) * 2 + r // 8) * aux_width
            for out_half in range(2):
                hi, lo = split(sums[parity][out_half])
                columns = slice(out_half * 128, (out_half + 1) * 128)
                m_hi[at:at + aux_width, columns] = hi
                m_lo[at:at + aux_width, columns] = lo


def half_kernel(n_mu, nu_slots, nu_count, *refs):
    dens = by_distance(refs[:n_mu], DENSITY_ORDER)
    packed = refs[n_mu]
    outs = refs[n_mu + 1:2 * n_mu + 1]
    d_both, weights, turned = refs[2 * n_mu + 1:]
    z = lax.axis_index("mu")
    orb, lam_all = dens[0].shape
    lam = lam_all // n_mu
    slots = nu_slots.shape[2]
    row, col = iota((lam_all, 128), 0), iota((lam_all, 128), 1)
    group = z
    for slot in range(1, n_mu):
        group = jnp.where((col >> 3) & 3 == slot, z ^ HALF_ORDER[slot], group)
    wanted = group * lam + (col >> 6) * 8 + (col & 7)
    choose = jnp.where(row == wanted, 1.0, 0.0).astype(BF16)
    for s in range(n_mu):
        hi, lo = split(dens[s][...])
        d_both[s, :, :128] = jnp.dot(hi, choose, preferred_element_type=F32)
        d_both[s, :, 128:] = jnp.dot(lo, choose, preferred_element_type=F32)
    orbital = (iota((orb, 256), 1) >> 5) & 1
    for k in range(slots):
        live = jnp.where(k < nu_count[0, 0], 1.0, 0.0)
        both = d_both[z ^ nu_slots[0, 0, k]] * live
        for i in range(2):
            block = jnp.where(orbital == i, both, 0.0).astype(BF16)
            for part in range(2):
                at = k * 256 + part * 128 + i * orb
                weights[at:at + orb, :] = block
    aux_width = outs[0].shape[1] // lam
    lower = iota((aux_width, 128), 1) < 64
    per_group = 512 // (2 * aux_width)
    span = per_group * 4
    for part in range(packed.shape[0] // 512):
        product = jnp.dot(
            packed[part * 512:(part + 1) * 512, :], weights[...], preferred_element_type=F32
        )
        total = product[:, :128] + product[:, 128:]
        for chunk in range(per_group):
            at = chunk * 2 * aux_width
            one, two = total[at:at + aux_width], total[at + aux_width:at + 2 * aux_width]
            top = jnp.where(lower, one, pltpu.roll(two, 64, 1))
            bottom = jnp.where(lower, pltpu.roll(one, 64, 1), two)
            at = (part * per_group + chunk) * 128
            turned[at:at + 128, :] = jnp.concatenate([top, bottom], axis=0).T
        for s in range(n_mu):
            for r in range(8):
                picked = turned[pl.ds(part * per_group * 128 + s * 8 + r, span, stride=32), :]
                outs[s][part * span:(part + 1) * span, r * 128:(r + 1) * 128] = picked.astype(BF16)


def exchange_kernel(n_mu, n_aux, *refs):
    halves = refs[:n_mu]
    m_hi, m_lo, out, total = refs[n_mu:]
    z = lax.axis_index("mu")
    left = jnp.concatenate([h[...] for h in halves], axis=0)
    product = jnp.dot(left, m_hi[...], preferred_element_type=F32)
    product += jnp.dot(left, m_lo[...], preferred_element_type=F32)
    orb = halves[0].shape[0]
    for s in range(n_mu):
        block = z ^ HALF_ORDER[s]
        total[pl.ds(pl.multiple_of(block * orb, orb), orb), :] = product[s * orb:(s + 1) * orb]
    rows = out.shape[1]
    lower = iota((rows, 128), 1) < 64
    for a in range(n_aux):
        for pair in range(n_mu // 2):
            columns = slice(pair * 128, (pair + 1) * 128)
            top = total[a * 2 * rows:(a * 2 + 1) * rows, columns]
            bottom = total[(a * 2 + 1) * rows:(a * 2 + 2) * rows, columns]
            at = a * n_mu + n_mu - 1 - pair * 2
            out[at] = jnp.where(lower, top, pltpu.roll(bottom, 64, 1)).astype(BF16)
            out[at - 1] = jnp.where(lower, pltpu.roll(top, 64, 1), bottom).astype(BF16)


def sum_kernel(parts, out):
    total = parts[0].astype(F32)
    for d in range(1, parts.shape[0]):
        total += parts[d].astype(F32)
    rows = parts.shape[1]
    out[:rows, :] = total[:, :64]
    out[rows:, :] = total[:, 64:]


def fast(n_mu, n_aux, three_center, nu_slots, nu_count, density, metric_tensor, sig_slots, sig_count):
    orb, lam_all = density.shape
    slots, aux_width = three_center.shape[1:3]
    lam = lam_all // n_mu
    turns = [[(z, z ^ s) for z in range(n_mu)] for s in range(n_mu)]
    dens = [density] + [lax.ppermute(density, "mu", turns[s]) for s in DENSITY_ORDER]
    nu_slots, sig_slots = jnp.swapaxes(nu_slots, 1, 2), jnp.swapaxes(sig_slots, 1, 2)
    chunks = three_center.shape[3] // 256
    t_shape = jax.ShapeDtypeStruct((2 * chunks * aux_width, slots * 256), BF16)
    m_shape = jax.ShapeDtypeStruct((lam * aux_width, n_mu * orb), BF16)
    packed = pl.pallas_call(
        tensor_kernel,
        out_shape=t_shape,
        in_specs=[HBM],
        out_specs=VMEM,
        scratch_shapes=[
            pltpu.VMEM((slots * 4, aux_width, chunks * 64), F32),
            pltpu.SemaphoreType.DMA((slots * 4,)),
        ],
        compiler_params=params(50),
        cost_estimate=pl.CostEstimate(flops=10_000_000, bytes_accessed=6_000_000, transcendentals=0),
        name="tensor",
    )(three_center)
    half_shape = jax.ShapeDtypeStruct((orb, lam * aux_width), BF16)
    halves = pl.pallas_call(
        functools.partial(half_kernel, n_mu),
        out_shape=(half_shape,) * n_mu,
        in_specs=[SMEM, SMEM] + [VMEM] * (n_mu + 1),
        out_specs=(VMEM,) * n_mu,
        scratch_shapes=[
            pltpu.VMEM((n_mu, orb, 256), F32),
            pltpu.VMEM((slots * 256, 256), BF16),
            pltpu.VMEM((chunks * 128, 128), F32),
        ],
        compiler_params=params(16),
        cost_estimate=pl.CostEstimate(flops=1_200_000_000, bytes_accessed=4_000_000, transcendentals=0),
        name="half",
    )(nu_slots, nu_count, *dens, packed)
    m_hi, m_lo = pl.pallas_call(
        metric_kernel,
        out_shape=(m_shape, m_shape),
        in_specs=[SMEM, SMEM, ANY, VMEM],
        out_specs=(VMEM, VMEM),
        compiler_params=params(16),
        cost_estimate=pl.CostEstimate(flops=10_000_000, bytes_accessed=2_000_000, transcendentals=0),
        name="metric",
    )(sig_slots, sig_count, halves[0], metric_tensor)
    halves = [halves[0]] + [
        lax.ppermute(halves[s], "mu", turns[HALF_ORDER[s]]) for s in range(1, n_mu)
    ]
    rows = n_mu * orb // n_aux
    parts = pl.pallas_call(
        functools.partial(exchange_kernel, n_mu, n_aux),
        out_shape=jax.ShapeDtypeStruct((n_aux * n_mu, rows // 2, 128), BF16),
        in_specs=[VMEM] * (n_mu + 2),
        out_specs=VMEM,
        scratch_shapes=[pltpu.VMEM((n_mu * orb, n_mu * orb), F32)],
        compiler_params=params(16),
        cost_estimate=pl.CostEstimate(flops=300_000_000, bytes_accessed=2_000_000, transcendentals=0),
        name="exchange",
    )(*halves, m_hi, m_lo)
    down = [a * n_mu + z for a in range(n_aux) for z in reversed(range(n_mu))]
    parts = lax.all_to_all(parts, ("aux", "mu"), 0, 0, axis_index_groups=[down])
    return pl.pallas_call(
        sum_kernel,
        out_shape=jax.ShapeDtypeStruct((rows, orb), F32),
        in_specs=[VMEM],
        out_specs=VMEM,
        compiler_params=params(8),
        name="sum",
    )(parts)


def general(three_center, nu_slots, nu_count, density, metric_tensor, sig_slots, sig_count):
    highest = lax.Precision.HIGHEST
    orb_block = density.shape[0]
    lam_all = density.shape[1]
    aux_width = three_center.shape[2]
    dens_all = lax.all_gather(density, "mu", axis=0, tiled=True)

    def add_slot(k, running):
        nu_pick = nu_slots[0, k, 0]
        dens_rows = lax.dynamic_slice_in_dim(dens_all, nu_pick * orb_block, orb_block, 0)
        slab_piece = lax.dynamic_index_in_dim(three_center[0], k, 0, keepdims=False).reshape(
            aux_width, orb_block, orb_block
        )
        return running + jnp.einsum("pij,jl->lpi", slab_piece, dens_rows, precision=highest)

    halfway = lax.fori_loop(
        0, nu_count[0, 0], add_slot, jnp.zeros((lam_all, aux_width, orb_block), F32)
    )
    relayed = lax.all_to_all(halfway.astype(BF16), "mu", split_axis=0, concat_axis=2, tiled=True)
    widened = relayed.astype(F32)
    lam_rows = relayed.shape[0]
    orbitals = relayed.shape[2]

    def add_target(q, running):
        target = sig_slots[0, q, 0]
        weights = lax.dynamic_index_in_dim(metric_tensor[0], q, 0, keepdims=False).reshape(
            aux_width, lam_rows, orb_block
        )
        contrib = jnp.einsum("rpm,prc->mc", widened, weights, precision=highest)
        current = lax.dynamic_slice_in_dim(running, target * orb_block, orb_block, 1)
        return lax.dynamic_update_slice_in_dim(running, current + contrib, target * orb_block, 1)

    partial_k = lax.fori_loop(
        0, sig_count[0, 0], add_target, jnp.zeros((orbitals, orbitals), F32)
    )
    row_share = lax.psum_scatter(partial_k, "aux", scatter_dimension=0, tiled=True)
    return lax.psum_scatter(row_share, "mu", scatter_dimension=1, tiled=True)


def solution(mesh):
    n_aux, n_mu = mesh.shape["aux"], mesh.shape["mu"]

    def shards(three_center, nu_slots, nu_count, density, metric_tensor, sig_slots, sig_count):
        args = (three_center, nu_slots, nu_count, density, metric_tensor, sig_slots, sig_count)
        orb, lam_all = density.shape
        fits = (
            (n_aux, n_mu, orb, lam_all) == (8, 4, 64, 64)
            and three_center.shape[2:] == (64, orb * orb)
            and metric_tensor.shape[2:] == (64, lam_all // n_mu * orb)
        )
        return fast(n_mu, n_aux, *args) if fits else general(*args)

    placed = (
        P("mu", None, "aux", None),
        P("mu", None, "aux"),
        P("mu", "aux"),
        P("mu", None),
        P("mu", None, "aux", None),
        P("mu", None, "aux"),
        P("mu", "aux"),
    )
    return jax.shard_map(
        shards, mesh=mesh, in_specs=placed, out_specs=P("aux", "mu"), check_vma=False
    )
```
